32 devices in a mesh: gx: 2 (over core), gy: 16 (over z, y, x).
Axes of the slice: x: 2, y: 2, z: 4, core: 2. Of those that a mesh axis runs over, the one named last changes fastest.
Arguments:
- density: float32 [64, 16, 2048], P('gx', None, 'gy'), may hold values from 0.5 to 2
- velocity: float32 [3, 64, 16, 2048], P(None, 'gx', None, 'gy'), may hold values from -1.2 to 1.2
- bfield: float32 [3, 64, 16, 2048], P(None, 'gx', None, 'gy'), may hold values from -1.2 to 1.2
- pressure: float32 [64, 16, 2048], P('gx', None, 'gy'), may hold values from 0.5 to 2
- shear_shift: int32 [], replicated, may hold values from 0 to 2047
- remap_weight: int32 [], replicated, may hold values from 0 to 65535
Outputs:
- state: float32 [8, 64, 16, 2048], P(None, 'gx', None, 'gy')
The draws below stay inside these ranges and needn't reach their ends.
All inputs are finite; a program needn't handle non-finite values.
Results may differ from the reference program's by a relative error of at most 0.0003.
Values sent between devices are 32-bit elements; how exact they have to be, the bound alone decides.
No kernel may reach another device: no remote copies, remote signals or barrier semaphores. Data moves between devices by JAX's collectives and lax.ppermute only.
A program may use at most 128 MiB of HBM per device.

```python
import math
import jax
import jax.numpy as jnp
from jax import lax

CX = 32
CY = 128
NZ = 16
NX = 64
NY = 2048


def edge_layout():
    row_index = jnp.arange(NX, dtype=jnp.int32) % CX
    column_index = jnp.arange(NY, dtype=jnp.int32) % CY
    row_edge = jnp.logical_or(row_index < 2, row_index >= CX - 2)
    column_edge = jnp.logical_or(column_index < 2, column_index >= CY - 2)
    planted = jnp.logical_or(row_edge[:, None, None], column_edge[None, None, :])
    planted = jnp.broadcast_to(planted, (NX, NZ, NY))
    parity = (jnp.arange(NX, dtype=jnp.int32)[:, None, None] + jnp.arange(NZ, dtype=jnp.int32)[None, :, None] + jnp.arange(NY, dtype=jnp.int32)[None, None, :]) % 2
    parity_sign = 1.0 - 2.0 * parity.astype(jnp.float32)
    return (planted, parity_sign)


def positive_field(key, planted_low, planted_high):
    planted, parity_sign = edge_layout()
    key_flip, key_fill, key_level = jax.random.split(key, 3)
    flip_sign = jnp.where(jax.random.uniform(key_flip, (NX, NZ, NY)) < 0.15, -1.0, 1.0)
    level = planted_low * jnp.exp(jax.random.uniform(key_level, (NX, NZ, NY)) * math.log(planted_high / planted_low))
    extreme = jnp.where(parity_sign * flip_sign > 0.0, planted_high, level)
    filling = 0.5 * jnp.exp(jax.random.uniform(key_fill, (NX, NZ, NY)) * math.log(4.0))
    return jnp.where(planted, extreme, filling).astype(jnp.float32)


def vector_field(key):
    planted, parity_sign = edge_layout()
    key_flip, key_comp, key_fill = jax.random.split(key, 3)
    flip_sign = jnp.where(jax.random.uniform(key_flip, (3, NX, NZ, NY)) < 0.15, -1.0, 1.0)
    component_sign = jnp.where(jax.random.uniform(key_comp, (3, 1, 1, 1)) < 0.5, -1.0, 1.0)
    extreme = 1.2 * component_sign * flip_sign * parity_sign[None]
    filling = jnp.clip(0.3 * jax.random.normal(key_fill, (3, NX, NZ, NY)), -1.2, 1.2)
    return jnp.where(planted[None], extreme, filling).astype(jnp.float32)


def draw_density(key, part):
    return positive_field(jax.random.fold_in(key, 37), 0.5, 2.0)


def draw_pressure(key, part):
    return positive_field(jax.random.fold_in(key, 41), 1.2, 2.0)


def draw_velocity(key, part):
    return vector_field(jax.random.fold_in(key, 11))


def draw_bfield(key, part):
    return vector_field(jax.random.fold_in(key, 23))


def setup_inputs(seed: int = 0) -> dict:
    splits = jax.random.split(jax.random.key(seed), 7)
    density = draw_density(jax.random.fold_in(splits[6], 71), 0)
    velocity = draw_velocity(jax.random.fold_in(splits[6], 71), 0)
    bfield = draw_bfield(jax.random.fold_in(splits[6], 71), 0)
    pressure = draw_pressure(jax.random.fold_in(splits[6], 71), 0)
    shear_shift = jax.random.randint(splits[4], (), 0, NY).astype(jnp.int32)
    remap_weight = jax.random.randint(splits[5], (), 0, 65536).astype(jnp.int32)
    return {"density": density, "velocity": velocity, "bfield": bfield, "pressure": pressure, "shear_shift": shear_shift, "remap_weight": remap_weight}


GAMMA = 5.0 / 3.0
SHEAR_Q = 1.5
TIME_STEP = 0.03
WEIGHT_SCALE = 1.0 / 65536.0

def minmod(upper, lower):
    return jnp.where(upper * lower > 0.0, jnp.sign(upper) * jnp.minimum(jnp.abs(upper), jnp.abs(lower)), 0.0)

def to_primitive(conserved):
    density = conserved[0]
    velocity = conserved[1:4] / density
    magnetic = conserved[4:7]
    pressure = (GAMMA - 1.0) * (conserved[7] - 0.5 * density * lax.optimization_barrier(jnp.sum(velocity * velocity, axis=0)) - 0.5 * lax.optimization_barrier(jnp.sum(magnetic * magnetic, axis=0)))
    return jnp.concatenate([density[None], velocity, magnetic, pressure[None]], axis=0)

def point_flux(primitive, normal_axis):
    density = primitive[0]
    velocity = primitive[1:4]
    magnetic = primitive[4:7]
    pressure = primitive[7]
    mag_square = lax.optimization_barrier(jnp.sum(magnetic * magnetic, axis=0))
    total_pressure = pressure + 0.5 * mag_square
    energy = pressure / (GAMMA - 1.0) + 0.5 * density * lax.optimization_barrier(jnp.sum(velocity * velocity, axis=0)) + 0.5 * mag_square
    normal_speed = velocity[normal_axis]
    normal_field = magnetic[normal_axis]
    velocity_dot = lax.optimization_barrier(jnp.sum(velocity * magnetic, axis=0))
    momentum_flux = []
    induction_flux = []
    for component in range(3):
        term = density * velocity[component] * normal_speed - normal_field * magnetic[component]
        if component == normal_axis:
            term = term + total_pressure
        momentum_flux.append(term)
        induction_flux.append(normal_speed * magnetic[component] - normal_field * velocity[component])
    energy_flux = (energy + total_pressure) * normal_speed - normal_field * velocity_dot
    flux = jnp.stack([density * normal_speed] + momentum_flux + induction_flux + [energy_flux])
    conserved = jnp.stack([density, density * velocity[0], density * velocity[1], density * velocity[2], magnetic[0], magnetic[1], magnetic[2], energy])
    sound_square = GAMMA * pressure / density
    alfven_square = mag_square / density
    transverse = jnp.zeros_like(density)
    for component in range(3):
        if component != normal_axis:
            transverse = transverse + magnetic[component] * magnetic[component]
    transverse = transverse / density
    spread = sound_square - alfven_square
    fast_speed = jnp.sqrt(0.5 * (sound_square + alfven_square + jnp.sqrt(spread * spread + 4.0 * sound_square * transverse)))
    return (flux, conserved, jnp.abs(normal_speed) + fast_speed)

def slab(array, start, stop, axis):
    return lax.slice_in_dim(array, start, stop, axis=axis)

def flux_difference(primitive, axis, normal_axis):
    length = primitive.shape[axis] - 4
    upper = slab(primitive, 2, length + 4, axis) - slab(primitive, 1, length + 3, axis)
    lower = slab(primitive, 1, length + 3, axis) - slab(primitive, 0, length + 2, axis)
    slopes = minmod(upper, lower)
    left_state = slab(primitive, 1, length + 2, axis) + 0.5 * slab(slopes, 0, length + 1, axis)
    right_state = slab(primitive, 2, length + 3, axis) - 0.5 * slab(slopes, 1, length + 2, axis)
    flux_left, cons_left, speed_left = point_flux(left_state, normal_axis)
    flux_right, cons_right, speed_right = point_flux(right_state, normal_axis)
    speed = jnp.maximum(speed_left, speed_right)
    face = 0.5 * (flux_left + flux_right) - 0.5 * speed * (cons_right - cons_left)
    return slab(face, 1, length + 1, axis) - slab(face, 0, length, axis)

def source_terms(conserved, radial, omega):
    zeros = jnp.zeros_like(conserved[0])
    momentum_x = 2.0 * omega * conserved[2] + 2.0 * SHEAR_Q * omega * omega * conserved[0] * radial
    momentum_y = -2.0 * omega * conserved[1]
    energy = 2.0 * SHEAR_Q * omega * omega * radial * conserved[1]
    return jnp.stack([zeros, momentum_x, momentum_y, zeros, zeros, zeros, zeros, energy])

def boost(conserved, delta):
    momentum_y = conserved[2] + conserved[0] * delta
    energy = conserved[7] + conserved[2] * delta + 0.5 * conserved[0] * delta * delta
    return jnp.stack([conserved[0], conserved[1], momentum_y, conserved[3], conserved[4], conserved[5], conserved[6], energy])

def remap(source, shift, weight):
    return (1.0 - weight) * jnp.roll(source, shift, axis=3) + weight * jnp.roll(source, shift + 1, axis=3)

def pad_periodic(array, axis):
    total = array.shape[axis]
    return jnp.concatenate([slab(array, total - 2, total, axis), array, slab(array, 0, 2, axis)], axis=axis)

def section_rate(conserved, shift, weight, omega, radial):
    other_shift = (NY - 1 - shift).astype(jnp.int32)
    other_weight = 1.0 - weight
    left = boost(remap(conserved[:, NX - 2:], shift, weight), 1.0)
    right = boost(remap(conserved[:, :2], other_shift, other_weight), -1.0)
    radial_pad = jnp.concatenate([left, conserved, right], axis=1)
    change = flux_difference(to_primitive(pad_periodic(conserved, 3)), 3, 1)
    change = change + flux_difference(to_primitive(pad_periodic(conserved, 2)), 2, 2)
    change = change + flux_difference(to_primitive(radial_pad), 1, 0)
    return source_terms(conserved, radial, omega) - change

def reference(density, velocity, bfield, pressure, shear_shift, remap_weight):
    omega = 1.0 / (SHEAR_Q * NX)
    radial = (jnp.arange(NX).astype(jnp.float32) + 0.5 - 0.5 * NX)[:, None, None]
    weight = remap_weight.astype(jnp.float32) * WEIGHT_SCALE
    shift = shear_shift.astype(jnp.int32)
    speed_y = velocity[1] - SHEAR_Q * omega * radial
    moving = jnp.stack([velocity[0], speed_y, velocity[2]])
    energy = pressure / (GAMMA - 1.0) + 0.5 * density * lax.optimization_barrier(jnp.sum(moving * moving, axis=0)) + 0.5 * lax.optimization_barrier(jnp.sum(bfield * bfield, axis=0))
    start_state = jnp.concatenate([density[None], density[None] * moving, bfield, energy[None]], axis=0)
    middle = start_state + TIME_STEP * section_rate(start_state, shift, weight, omega, radial)
    final = 0.5 * start_state + 0.5 * (middle + TIME_STEP * section_rate(middle, shift, weight, omega, radial))
    return final
```

```python
import functools

import jax
import jax.numpy as jnp
from jax import lax
from jax.experimental import pallas as pl
from jax.experimental.pallas import tpu as pltpu
from jax.sharding import PartitionSpec as P

GAMMA = 5.0 / 3.0
SHEAR_Q = 1.5
TIME_STEP = 0.03
WEIGHT_SCALE = 1.0 / 65536.0
TINY = 1e-30
FIELDS = 8


def root(x):
    return x * lax.rsqrt(jnp.maximum(x, TINY))


def side(state, normal):
    rho, pressure = state[0], state[7]
    vel, mag = state[1:4], state[4:7]
    one, two = [c for c in range(3) if c != normal]
    mom = [rho * v for v in vel]
    vn, bn = vel[normal], mag[normal]
    mn = mom[normal]
    mnvn = mn * vn
    kinetic = 0.5 * ((mnvn + mom[one] * vel[one]) + mom[two] * vel[two])
    bn2 = bn * bn
    bt2 = mag[one] * mag[one] + mag[two] * mag[two]
    half_b2 = 0.5 * (bt2 + bn2)
    inner = kinetic + 1.5 * pressure
    energy = inner + half_b2
    ind_one = vn * mag[one] - bn * vel[one]
    ind_two = vn * mag[two] - bn * vel[two]
    flux = [None] * FIELDS
    flux[0] = mn
    flux[1 + normal] = mnvn + (pressure + half_b2) - bn2
    flux[1 + one] = mn * vel[one] - bn * mag[one]
    flux[1 + two] = mn * vel[two] - bn * mag[two]
    flux[4 + one] = ind_one
    flux[4 + two] = ind_two
    flux[7] = vn * (inner + pressure) + (mag[one] * ind_one + mag[two] * ind_two)
    cons = [rho] + mom + list(mag) + [energy]
    half_gp = (0.5 * GAMMA) * pressure
    spread = half_gp - half_b2
    disc = spread * spread + (GAMMA * pressure) * bt2
    fast = (half_gp + half_b2) + root(disc)
    speed = jnp.abs(vn) + fast * lax.rsqrt(jnp.maximum(rho * fast, TINY))
    return flux, cons, speed


def face(left, right, normal):
    fl, ul, sl = side(left, normal)
    fr, ur, sr = side(right, normal)
    speed = jnp.maximum(sl, sr)
    out = []
    for f in range(FIELDS):
        jump = speed * (ur[f] - ul[f])
        out.append(-jump if fl[f] is None else (fl[f] + fr[f]) - jump)
    return out


def limited(up, down):
    return jnp.maximum(jnp.minimum(up, down), jnp.minimum(jnp.maximum(up, down), 0.0))


def shifted(x, by, axis):
    return pltpu.roll(x, by % x.shape[axis], axis)


def to_conserved(w):
    rho = w[0]
    mom = [rho * v for v in w[1:4]]
    kinetic = 0.5 * (mom[0] * w[1] + mom[1] * w[2] + mom[2] * w[3])
    magnetic = 0.5 * (w[4] * w[4] + w[5] * w[5] + w[6] * w[6])
    return [rho] + mom + list(w[4:7]) + [1.5 * w[7] + kinetic + magnetic]


def to_primitive(u):
    inverse = 1.0 / u[0]
    vel = [m * inverse for m in u[1:4]]
    kinetic = 0.5 * (u[1] * vel[0] + u[2] * vel[1] + u[3] * vel[2])
    magnetic = 0.5 * (u[4] * u[4] + u[5] * u[5] + u[6] * u[6])
    return [u[0]] + vel + list(u[4:7]) + [(GAMMA - 1.0) * (u[7] - kinetic - magnetic)]


def lanes_of(shape):
    return lax.broadcasted_iota(jnp.int32, shape, 1)


def load_row(ref, i):
    return [ref[f, i] for f in range(FIELDS)]


def pack_row(ref, f, i, value, lane, width):
    moved = pltpu.roll(value, lax.rem(4 * i + 2, width), 1)
    ref[f] = jnp.where(lane // 4 == i, moved, ref[f])


def send_edges(flags, get_row, shear_ref, swap_refs, rows):
    first = flags[0] == 1
    for k in range(2):
        low, high = get_row(k), get_row(rows - 2 + k)
        if len(swap_refs) == 1:
            for f in range(FIELDS):
                swap_refs[0][f, k] = jnp.where(first, high[f], low[f])
        else:
            for f in range(FIELDS):
                swap_refs[0][f, k] = low[f]
                swap_refs[1][f, k] = high[f]
        outer = to_conserved([jnp.where(first, low[f], high[f]) for f in range(FIELDS)])
        for f in range(FIELDS):
            shear_ref[f, 1 + k] = outer[f]


def prepare_kernel(flags, radial0, rho_ref, vel_ref, mag_ref, pres_ref, w_ref, out_a, out_b, *swap):
    rows, _, width = rho_ref.shape
    lane = lanes_of(rho_ref.shape[1:])
    omega_q = radial0[1]

    def body(i, carry):
        x = radial0[0] + i.astype(jnp.float32)
        w = [rho_ref[i], vel_ref[0, i], vel_ref[1, i] - omega_q * x, vel_ref[2, i]]
        w += [mag_ref[0, i], mag_ref[1, i], mag_ref[2, i], pres_ref[i]]
        for f in range(FIELDS):
            w_ref[f, i] = w[f]
            pack_row(out_b, f, i, w[f], lane, width)
        return carry

    lax.fori_loop(0, rows, body, 0)
    for f in range(FIELDS):
        out_a[f, 0] = out_b[f]
    send_edges(flags, lambda i: load_row(w_ref, i), out_a, swap, rows)


def axis_states(w, axis):
    left, right = [], []
    for f in range(FIELDS):
        up = 0.5 * (shifted(w[f], -1, axis) - w[f])
        slope = limited(up, shifted(up, 1, axis))
        left.append(w[f] + slope)
        right.append(w[f] - slope)
    return left, right


def interior_kernel(second, radial0, w_ref, *refs):
    if second:
        w0_ref, u1_ref, v_ref, t_ref, wl_ref, fx_ref = refs
    else:
        v_ref, t_ref, wl_ref, fx_ref = refs
    rows, _, width = w_ref.shape[1:]
    step = 0.5 * TIME_STEP if second else TIME_STEP
    coef = 0.5 * step
    lane = lanes_of(w_ref.shape[2:])
    inner = jnp.logical_and(lane >= 1, lane < width - 2)
    omega_q = radial0[1]
    omega = omega_q / SHEAR_Q

    def body(i, carry):
        w = load_row(w_ref, i)
        left, right = axis_states(w, 0)
        fz = face(left, [shifted(r, -1, 0) for r in right], 2)
        total = [f - shifted(f, 1, 0) for f in fz]
        left, right = axis_states(w, 1)
        for f in range(FIELDS):
            pack_row(t_ref, f, i, jnp.where(lane < width // 2, right[f], left[f]), lane, width)
        fy = face(left, [shifted(r, -1, 1) for r in right], 1)
        fy = [jnp.where(inner, f, 0.0) for f in fy]
        total = [total[f] + (fy[f] - shifted(fy[f], 1, 1)) for f in range(FIELDS)]
        x = radial0[0] + i.astype(jnp.float32)
        cons = to_conserved(w)
        if second:
            base = [0.5 * (a + u1_ref[f, i]) for f, a in enumerate(to_conserved(load_row(w0_ref, i)))]
        else:
            base = cons
        tidal = 2.0 * omega * omega_q * x
        value = [base[f] - coef * total[f] for f in range(FIELDS)]
        value[1] = value[1] + step * (2.0 * omega * cons[2] + tidal * cons[0])
        value[2] = value[2] - step * (2.0 * omega * cons[1])
        value[7] = value[7] + step * (tidal * cons[1])
        for f in range(FIELDS):
            v_ref[f, i] = value[f]
        return carry

    lax.fori_loop(0, rows, body, 0)

    def states(i):
        left, right = [], []
        for f in range(FIELDS):
            here = w_ref[f, i]
            slope = limited(0.5 * (w_ref[f, i + 1] - here), 0.5 * (here - w_ref[f, i - 1]))
            left.append(here + slope)
            right.append(here - slope)
        return left, right

    left, _ = states(1)
    for f in range(FIELDS):
        wl_ref[f] = left[f]
        fx_ref[f] = jnp.zeros_like(left[f])

    def body_x(i, carry):
        left, right = states(i + 1)
        fx = face([wl_ref[f] for f in range(FIELDS)], right, 0)
        for f in range(FIELDS):
            v_ref[f, i] = v_ref[f, i] - coef * (fx[f] - fx_ref[f])
            wl_ref[f] = left[f]
            fx_ref[f] = fx[f]
        return carry

    lax.fori_loop(1, rows - 2, body_x, 0)
    for f in range(FIELDS):
        v_ref[f, rows - 2] = v_ref[f, rows - 2] + coef * fx_ref[f]


def window_kernel(flags, weights, own_ref, far_ref, out_ref):
    last = flags[1] == 1
    width = own_ref.shape[-1]
    start = flags[2]
    lane = lanes_of(own_ref.shape[2:])

    def taken(near, far, at):
        back = lax.rem(2 * width - at, width)
        return jnp.where(lane < width - at, pltpu.roll(near, back, 1), pltpu.roll(far, back, 1))

    for k in range(2):
        ghost = []
        for f in range(FIELDS):
            own, far = own_ref[f, 1 + k], far_ref[f, 1 + k]
            near = jnp.where(last, far, own)
            rest = jnp.where(last, own, far)
            ghost.append(weights[0] * taken(near, rest, start + 1) + weights[1] * taken(near, rest, start))
        delta = weights[2]
        boosted = list(ghost)
        boosted[2] = ghost[2] + ghost[0] * delta
        boosted[7] = ghost[7] + ghost[2] * delta + 0.5 * ghost[0] * delta * delta
        prim = to_primitive(boosted)
        for f in range(FIELDS):
            out_ref[f, k] = prim[f]


def edge_kernel(second, flags, v_ref, w_ref, o_ref, da_ref, db_ref, t_ref, xl_ref, xr_ref, g_ref, *refs):
    rows, high, width = w_ref.shape[1:]
    step = 0.5 * TIME_STEP if second else TIME_STEP
    coef = 0.5 * step
    if second:
        out_ref, d_ref = refs
    else:
        w1_ref, out_ref, out_a, out_b = refs[:4]
        swap, d_ref = refs[4:-1], refs[-1]
    first, last = flags[0] == 1, flags[1] == 1
    lane = lanes_of((high, width))
    place = lane % 4

    own = [o_ref[f] for f in range(FIELDS)]
    low_side = [jnp.where(first, db_ref[f], da_ref[f, 0]) for f in range(FIELDS)]
    high_side = [jnp.where(first, da_ref[f, 0], db_ref[f]) for f in range(FIELDS)]
    inner = [t_ref[f] for f in range(FIELDS)]
    a = [jnp.where(place < 2, low_side[f], own[f]) for f in range(FIELDS)]
    b = [jnp.where(place < 2, own[f], high_side[f]) for f in range(FIELDS)]
    left, right = axis_states(a, 1)
    right = [shifted(jnp.where(place == 3, inner[f], right[f]), -1, 1) for f in range(FIELDS)]
    fa = face(left, right, 1)
    left, right = axis_states(b, 1)
    left = [jnp.where(place == 0, inner[f], left[f]) for f in range(FIELDS)]
    fb = face(left, [shifted(r, -1, 1) for r in right], 1)
    for f in range(FIELDS):
        upper = jnp.where(place == 3, 0.0, jnp.where(place < 2, fb[f], fa[f]))
        lower = shifted(jnp.where(place == 0, fb[f], fa[f]), 1, 1)
        lower = jnp.where(place == 0, 0.0, lower)
        d_ref[f] = coef * (upper - lower)

    def x_states(cells):
        left, right = [], []
        for f in range(FIELDS):
            before, here, after = (c[f] for c in cells)
            slope = limited(0.5 * (after - here), 0.5 * (here - before))
            left.append(here + slope)
            right.append(here - slope)
        return left, right

    ghost_low = [[jnp.where(first, g_ref[f, k], xl_ref[f, k]) for f in range(FIELDS)] for k in range(2)]
    cells = ghost_low + [load_row(w_ref, i) for i in range(3)]
    sides = [x_states(cells[k : k + 3]) for k in range(3)]
    outer = face(sides[0][0], sides[1][1], 0)
    inner_face = face(sides[1][0], sides[2][1], 0)
    for f in range(FIELDS):
        v_ref[f, 0] = v_ref[f, 0] - coef * (inner_face[f] - outer[f])
        v_ref[f, 1] = v_ref[f, 1] + coef * inner_face[f]
    ghost_high = [[jnp.where(last, g_ref[f, k], xr_ref[f, k]) for f in range(FIELDS)] for k in range(2)]
    cells = [load_row(w_ref, rows - 3 + i) for i in range(3)] + ghost_high
    sides = [x_states(cells[k : k + 3]) for k in range(3)]
    inner_face = face(sides[0][0], sides[1][1], 0)
    outer = face(sides[1][0], sides[2][1], 0)
    for f in range(FIELDS):
        v_ref[f, rows - 2] = v_ref[f, rows - 2] - coef * inner_face[f]
        v_ref[f, rows - 1] = v_ref[f, rows - 1] - coef * (outer[f] - inner_face[f])

    edge = jnp.logical_or(lane < 2, lane >= width - 2)

    def body(i, carry):
        back = lax.rem(2 * width - 2 - 4 * i, width)
        value = []
        for f in range(FIELDS):
            move = jnp.where(edge, pltpu.roll(d_ref[f], back, 1), 0.0)
            value.append(v_ref[f, i] - move)
            out_ref[f, i] = value[f]
        if not second:
            prim = to_primitive(value)
            for f in range(FIELDS):
                w1_ref[f, i] = prim[f]
                pack_row(out_b, f, i, prim[f], lane, width)
        return carry

    lax.fori_loop(0, rows, body, 0)
    if not second:
        for f in range(FIELDS):
            out_a[f, 0] = out_b[f]
        send_edges(flags, lambda i: load_row(w1_ref, i), out_a, swap, rows)


def call(kernel, name, scalars, arrays, shapes, scratch=(), aliases=None):
    smem = pl.BlockSpec(memory_space=pltpu.SMEM)
    vmem = pl.BlockSpec(memory_space=pltpu.VMEM)
    return pl.pallas_call(
        kernel,
        name=name,
        out_shape=[jax.ShapeDtypeStruct(s, jnp.float32) for s in shapes],
        in_specs=[smem] * len(scalars) + [vmem] * len(arrays),
        out_specs=[vmem] * len(shapes),
        scratch_shapes=[pltpu.VMEM(s, jnp.float32) for s in scratch],
        input_output_aliases=aliases or {},
        compiler_params=pltpu.CompilerParams(vmem_limit_bytes=48 * 1024 * 1024),
    )(*scalars, *arrays)


def exchange(out_a, out_b, swap):
    count_x, count_y = lax.axis_size("gx"), lax.axis_size("gy")
    ahead, behind = [], []
    for gx in range(count_x):
        turn = -1 if gx == 0 else 1
        for gy in range(count_y):
            here = gx * count_y + gy
            ahead.append((here, gx * count_y + (gy + turn) % count_y))
            behind.append((here, gx * count_y + (gy - turn) % count_y))
    got_a = lax.ppermute(out_a, ("gx", "gy"), ahead)
    got_b = lax.ppermute(out_b, ("gx", "gy"), behind)
    if len(swap) == 1:
        low = high = lax.ppermute(swap[0], "gx", [(0, 1), (1, 0)])
    else:
        low = lax.ppermute(swap[1], "gx", [(i, i + 1) for i in range(count_x - 1)])
        high = lax.ppermute(swap[0], "gx", [(i + 1, i) for i in range(count_x - 1)])
    return got_a, got_b, low, high


def shear_exchange(ghost, block):
    count_x, count_y = lax.axis_size("gx"), lax.axis_size("gy")
    last = (count_x - 1) * count_y

    def branch(by):
        pairs = []
        for gy in range(count_y):
            pairs.append((last + gy, (gy + by) % count_y))
            pairs.append((gy, last + (gy - by) % count_y))
        return lambda x: lax.ppermute(x, ("gx", "gy"), pairs)

    return lax.switch(block, [branch(by) for by in range(count_y)], ghost)


def on_device(density, velocity, bfield, pressure, shear_shift, remap_weight):
    rows, high, width = density.shape
    count_x = lax.axis_size("gx")
    total_x = rows * count_x
    omega = 1.0 / (SHEAR_Q * total_x)
    row = lax.axis_index("gx")
    is_first, is_last = row == 0, row == count_x - 1
    radial0 = (row * rows).astype(jnp.float32) + 0.5 - 0.5 * total_x
    radial0 = jnp.stack([radial0, jnp.float32(SHEAR_Q * omega)])
    weight = remap_weight.astype(jnp.float32) * WEIGHT_SCALE
    block, rest = shear_shift // width, shear_shift % width
    start = jnp.where(is_last, width - 1 - rest, rest)
    flags = jnp.stack([is_first.astype(jnp.int32), is_last.astype(jnp.int32), start.astype(jnp.int32)])
    other = 1.0 - weight
    weights = jnp.stack(
        [
            jnp.where(is_last, 1.0 - weight, 1.0 - other),
            jnp.where(is_last, weight, other),
            jnp.where(is_last, 1.0, -1.0),
        ]
    )
    full = (FIELDS, rows, high, width)
    slab = (FIELDS, 2, high, width)
    tile = (FIELDS, high, width)
    sends = [(FIELDS, 3, high, width), tile] + [slab] * (1 if count_x == 2 else 2)

    w0, out_a, out_b, *swap = call(
        prepare_kernel, "prepare", [flags, radial0], [density, velocity, bfield, pressure], [full] + sends
    )
    got_a, got_b, low, high_x = exchange(out_a, out_b, swap)
    v, t = call(
        functools.partial(interior_kernel, False), "inner_1", [radial0], [w0], [full, tile], [tile, tile]
    )
    (ghost,) = call(window_kernel, "window", [flags, weights], [out_a, got_a], [slab])
    got_g = shear_exchange(ghost, block)
    w1, u1, out_a, out_b2, *swap = call(
        functools.partial(edge_kernel, False),
        "edge_1",
        [flags],
        [v, w0, out_b, got_a, got_b, t, low, high_x, got_g],
        [full, full] + sends,
        [tile],
    )
    got_a, got_b, low, high_x = exchange(out_a, out_b2, swap)
    v, t = call(
        functools.partial(interior_kernel, True), "inner_2", [radial0], [w1, w0, u1], [full, tile], [tile, tile]
    )
    (ghost,) = call(window_kernel, "window", [flags, weights], [out_a, got_a], [slab])
    got_g = shear_exchange(ghost, block)
    (out,) = call(
        functools.partial(edge_kernel, True),
        "edge_2",
        [flags],
        [v, w1, out_b2, got_a, got_b, t, low, high_x, got_g],
        [full],
        [tile],
    )
    return out


def solution(mesh):
    placed = (
        P("gx", None, "gy"),
        P(None, "gx", None, "gy"),
        P(None, "gx", None, "gy"),
        P("gx", None, "gy"),
        P(),
        P(),
    )
    return jax.shard_map(
        on_device, mesh=mesh, in_specs=placed, out_specs=P(None, "gx", None, "gy"), check_vma=False
    )
```

```python
import functools

import jax
import jax.numpy as jnp
from jax import lax
from jax.experimental import pallas as pl
from jax.experimental.pallas import tpu as pltpu
from jax.sharding import PartitionSpec as P

GAMMA = 5.0 / 3.0
SHEAR_Q = 1.5
TIME_STEP = 0.03
WEIGHT_SCALE = 1.0 / 65536.0
TINY = 1e-30
FIELDS = 8


def root(x):
    return x * lax.rsqrt(jnp.maximum(x, TINY))


def side(state, normal):
    rho, pressure = state[0], state[7]
    vel, mag = state[1:4], state[4:7]
    one, two = [c for c in range(3) if c != normal]
    mom = [rho * v for v in vel]
    vn, bn = vel[normal], mag[normal]
    mn = mom[normal]
    mnvn = mn * vn
    kinetic = 0.5 * ((mnvn + mom[one] * vel[one]) + mom[two] * vel[two])
    bn2 = bn * bn
    bt2 = mag[one] * mag[one] + mag[two] * mag[two]
    half_b2 = 0.5 * (bt2 + bn2)
    inner = kinetic + 1.5 * pressure
    energy = inner + half_b2
    ind_one = vn * mag[one] - bn * vel[one]
    ind_two = vn * mag[two] - bn * vel[two]
    flux = [None] * FIELDS
    flux[0] = mn
    flux[1 + normal] = mnvn + (pressure + half_b2) - bn2
    flux[1 + one] = mn * vel[one] - bn * mag[one]
    flux[1 + two] = mn * vel[two] - bn * mag[two]
    flux[4 + one] = ind_one
    flux[4 + two] = ind_two
    flux[7] = vn * (inner + pressure) + (mag[one] * ind_one + mag[two] * ind_two)
    cons = [rho] + mom + list(mag) + [energy]
    half_gp = (0.5 * GAMMA) * pressure
    spread = half_gp - half_b2
    disc = spread * spread + (GAMMA * pressure) * bt2
    fast = (half_gp + half_b2) + root(disc)
    speed = jnp.abs(vn) + fast * lax.rsqrt(jnp.maximum(rho * fast, TINY))
    return flux, cons, speed


def face(left, right, normal):
    fl, ul, sl = side(left, normal)
    fr, ur, sr = side(right, normal)
    speed = jnp.maximum(sl, sr)
    out = []
    for f in range(FIELDS):
        jump = speed * (ur[f] - ul[f])
        out.append(-jump if fl[f] is None else (fl[f] + fr[f]) - jump)
    return out


def limited(up, down):
    return jnp.maximum(jnp.minimum(up, down), jnp.minimum(jnp.maximum(up, down), 0.0))


def shifted(x, by, axis):
    return pltpu.roll(x, by % x.shape[axis], axis)


def to_conserved(w):
    rho = w[0]
    mom = [rho * v for v in w[1:4]]
    kinetic = 0.5 * (mom[0] * w[1] + mom[1] * w[2] + mom[2] * w[3])
    magnetic = 0.5 * (w[4] * w[4] + w[5] * w[5] + w[6] * w[6])
    return [rho] + mom + list(w[4:7]) + [1.5 * w[7] + kinetic + magnetic]


def to_primitive(u):
    inverse = 1.0 / u[0]
    vel = [m * inverse for m in u[1:4]]
    kinetic = 0.5 * (u[1] * vel[0] + u[2] * vel[1] + u[3] * vel[2])
    magnetic = 0.5 * (u[4] * u[4] + u[5] * u[5] + u[6] * u[6])
    return [u[0]] + vel + list(u[4:7]) + [(GAMMA - 1.0) * (u[7] - kinetic - magnetic)]


def lanes_of(shape):
    return lax.broadcasted_iota(jnp.int32, shape, 1)


def load_row(ref, i):
    return [ref[f, i] for f in range(FIELDS)]


def pack_edges(ref, out_ref):
    rows, high, width = ref.shape[1:]
    lane = lanes_of((high, width))
    for f in range(FIELDS):
        packed = shifted(ref[f, 0], 2, 1)
        for i in range(1, rows):
            packed = jnp.where(lane >= 4 * i, shifted(ref[f, i], 4 * i + 2, 1), packed)
        out_ref[f] = packed


def send_edges(flags, w_ref, pack_ref, shear_ref, swap_refs):
    rows = w_ref.shape[1]
    pack_edges(w_ref, pack_ref)
    first = flags[0] == 1
    for k in range(2):
        low, high = load_row(w_ref, k), load_row(w_ref, rows - 2 + k)
        if len(swap_refs) == 1:
            for f in range(FIELDS):
                swap_refs[0][f, k] = jnp.where(first, high[f], low[f])
        else:
            for f in range(FIELDS):
                swap_refs[0][f, k] = low[f]
                swap_refs[1][f, k] = high[f]
        outer = to_conserved([jnp.where(first, low[f], high[f]) for f in range(FIELDS)])
        for f in range(FIELDS):
            shear_ref[f, k] = outer[f]


def prepare_kernel(flags, radial0, rho_hbm, vel_hbm, mag_hbm, pres_hbm, w_ref, pack_ref, shear_ref, *rest):
    swap, sems = rest[:-1], rest[-1]
    rows = w_ref.shape[1]
    parts = sems.shape[1]
    size = rows // parts
    copies = []
    for part in range(parts):
        at = pl.ds(part * size, size)
        copies.append(
            [
                pltpu.make_async_copy(rho_hbm.at[at], w_ref.at[0, at], sems.at[0, part]),
                pltpu.make_async_copy(vel_hbm.at[:, at], w_ref.at[pl.ds(1, 3), at], sems.at[1, part]),
                pltpu.make_async_copy(mag_hbm.at[:, at], w_ref.at[pl.ds(4, 3), at], sems.at[2, part]),
                pltpu.make_async_copy(pres_hbm.at[at], w_ref.at[7, at], sems.at[3, part]),
            ]
        )
        for copy in copies[-1]:
            copy.start()
    for part in range(parts):
        for copy in copies[part]:
            copy.wait()
        for i in range(part * size, (part + 1) * size):
            w_ref[2, i] = w_ref[2, i] - radial0[1] * (radial0[0] + float(i))
    send_edges(flags, w_ref, pack_ref, shear_ref, swap)


def axis_states(w, half):
    left, right = [], []
    for f in range(FIELDS):
        up = shifted(half[f], -1, 1) - half[f]
        slope = limited(up, shifted(up, 1, 1))
        left.append(w[f] + slope)
        right.append(w[f] - slope)
    return left, right


def wrapped(ref, f, value, before, after):
    high = value.shape[0]
    ref[f, 8 : 8 + high] = value
    if before:
        ref[f, 0:8] = value[high - 8 : high]
    if after:
        ref[f, 8 + high : 16 + high] = value[0:8]


def interior_kernel(second, radial0, w_ref, *refs):
    if second:
        w0_ref, u1_ref = refs[:2]
        refs = refs[2:]
    v_ref, t_ref, h_ref, hz_ref, rz_ref, fz_ref, wl_ref, dx_ref, fx_ref = refs
    rows, high, width = w_ref.shape[1:]
    step = 0.5 * TIME_STEP if second else TIME_STEP
    coef = 0.5 * step
    lane = lanes_of(w_ref.shape[2:])
    inner = jnp.logical_and(lane >= 1, lane < width - 2)
    omega_q = radial0[1]
    omega = omega_q / SHEAR_Q
    next_row, same_row, last_row = slice(9, 9 + high), slice(8, 8 + high), slice(7, 7 + high)

    def body(i, carry):
        w = load_row(w_ref, i)
        half = [0.5 * x for x in w]
        left = []
        for f in range(FIELDS):
            h_ref[f, i] = half[f]
            wrapped(hz_ref, f, half[f], True, True)
            slope = limited(hz_ref[f, next_row] - half[f], half[f] - hz_ref[f, last_row])
            left.append(w[f] + slope)
            wrapped(rz_ref, f, w[f] - slope, False, True)
        fz = face(left, [rz_ref[f, next_row] for f in range(FIELDS)], 2)
        total = []
        for f in range(FIELDS):
            wrapped(fz_ref, f, fz[f], True, False)
            total.append(fz[f] - fz_ref[f, last_row])
        left, right = axis_states(w, half)
        back = lax.rem(4 * i + 2, width)
        for f in range(FIELDS):
            ends = pltpu.roll(jnp.where(lane < width // 2, right[f], left[f]), back, 1)
            t_ref[f] = jnp.where(lane >= 4 * i, ends, t_ref[f])
        fy = face(left, [shifted(r, -1, 1) for r in right], 1)
        fy = [jnp.where(inner, f, 0.0) for f in fy]
        total = [total[f] + (fy[f] - shifted(fy[f], 1, 1)) for f in range(FIELDS)]
        x = radial0[0] + i.astype(jnp.float32)
        cons = to_conserved(w)
        if second:
            base = [0.5 * (a + u1_ref[f, i]) for f, a in enumerate(to_conserved(load_row(w0_ref, i)))]
        else:
            base = cons
        tidal = 2.0 * omega * omega_q * x
        value = [base[f] - coef * total[f] for f in range(FIELDS)]
        value[1] = value[1] + ((step * 2.0) * omega * cons[2] + (step * tidal) * cons[0])
        value[2] = value[2] - ((step * 2.0) * omega) * cons[1]
        value[7] = value[7] + (step * tidal) * cons[1]
        for f in range(FIELDS):
            v_ref[f, i] = value[f]
        return carry

    lax.fori_loop(0, rows, body, 0)

    def states(i):
        left, right = [], []
        for f in range(FIELDS):
            up = h_ref[f, i + 1] - h_ref[f, i]
            slope = limited(up, dx_ref[f])
            dx_ref[f] = up
            here = w_ref[f, i]
            left.append(here + slope)
            right.append(here - slope)
        return left, right

    for f in range(FIELDS):
        dx_ref[f] = h_ref[f, 1] - h_ref[f, 0]
    left, _ = states(1)
    for f in range(FIELDS):
        wl_ref[f] = left[f]
        fx_ref[f] = jnp.zeros_like(left[f])

    def body_x(i, carry):
        left, right = states(i + 1)
        fx = face([wl_ref[f] for f in range(FIELDS)], right, 0)
        for f in range(FIELDS):
            v_ref[f, i] = v_ref[f, i] - coef * (fx[f] - fx_ref[f])
            wl_ref[f] = left[f]
            fx_ref[f] = fx[f]
        return carry

    lax.fori_loop(1, rows - 2, body_x, 0)
    for f in range(FIELDS):
        v_ref[f, rows - 2] = v_ref[f, rows - 2] + coef * fx_ref[f]


def sheared_rows(flags, weights, near_ref, next_ref):
    first = flags[0] == 1
    high, width = near_ref.shape[2:]
    start = flags[2]
    lane = lanes_of((high, width))

    def taken(one, two, at):
        back = lax.rem(2 * width - at, width)
        return jnp.where(lane < width - at, pltpu.roll(one, back, 1), pltpu.roll(two, back, 1))

    rows = []
    for k in range(2):
        ghost = []
        for f in range(FIELDS):
            near, following = near_ref[f, k], next_ref[f, k]
            one = jnp.where(first, following, near)
            two = jnp.where(first, near, following)
            ghost.append(weights[0] * taken(one, two, start + 1) + weights[1] * taken(one, two, start))
        delta = weights[2]
        boosted = list(ghost)
        boosted[2] = ghost[2] + ghost[0] * delta
        boosted[7] = ghost[7] + ghost[2] * delta + 0.5 * ghost[0] * delta * delta
        rows.append(to_primitive(boosted))
    return rows


def edge_kernel(
    second, flags, weights, v_ref, w_ref, own_ref, low_ref, high_ref, t_ref, xl_ref, xr_ref, near_ref, next_ref, *refs
):
    rows, high, width = w_ref.shape[1:]
    step = 0.5 * TIME_STEP if second else TIME_STEP
    coef = 0.5 * step
    if second:
        out_ref, d_ref = refs
    else:
        w1_ref, out_ref, pack_ref, shear_ref = refs[:4]
        swap, d_ref = refs[4:-1], refs[-1]
    first, last = flags[0] == 1, flags[1] == 1
    lane = lanes_of((high, width))
    place = lane % 4

    own = [own_ref[f] for f in range(FIELDS)]
    inner = [t_ref[f] for f in range(FIELDS)]
    a = [jnp.where(place < 2, low_ref[f], own[f]) for f in range(FIELDS)]
    b = [jnp.where(place < 2, own[f], high_ref[f]) for f in range(FIELDS)]
    left, right = axis_states(a, [0.5 * x for x in a])
    right = [shifted(jnp.where(place == 3, inner[f], right[f]), -1, 1) for f in range(FIELDS)]
    fa = face(left, right, 1)
    left, right = axis_states(b, [0.5 * x for x in b])
    left = [jnp.where(place == 0, inner[f], left[f]) for f in range(FIELDS)]
    fb = face(left, [shifted(r, -1, 1) for r in right], 1)
    for f in range(FIELDS):
        upper = jnp.where(place == 3, 0.0, jnp.where(place < 2, fb[f], fa[f]))
        lower = shifted(jnp.where(place == 0, fb[f], fa[f]), 1, 1)
        lower = jnp.where(place == 0, 0.0, lower)
        d_ref[f] = coef * (upper - lower)

    def x_states(cells):
        left, right = [], []
        for f in range(FIELDS):
            before, here, after = (c[f] for c in cells)
            slope = limited(0.5 * (after - here), 0.5 * (here - before))
            left.append(here + slope)
            right.append(here - slope)
        return left, right

    ghost = sheared_rows(flags, weights, near_ref, next_ref)
    ghost_low = [[jnp.where(first, ghost[k][f], xl_ref[f, k]) for f in range(FIELDS)] for k in range(2)]
    cells = ghost_low + [load_row(w_ref, i) for i in range(3)]
    sides = [x_states(cells[k : k + 3]) for k in range(3)]
    outer = face(sides[0][0], sides[1][1], 0)
    inner_face = face(sides[1][0], sides[2][1], 0)
    for f in range(FIELDS):
        v_ref[f, 0] = v_ref[f, 0] - coef * (inner_face[f] - outer[f])
        v_ref[f, 1] = v_ref[f, 1] + coef * inner_face[f]
    ghost_high = [[jnp.where(last, ghost[k][f], xr_ref[f, k]) for f in range(FIELDS)] for k in range(2)]
    cells = [load_row(w_ref, rows - 3 + i) for i in range(3)] + ghost_high
    sides = [x_states(cells[k : k + 3]) for k in range(3)]
    inner_face = face(sides[0][0], sides[1][1], 0)
    outer = face(sides[1][0], sides[2][1], 0)
    for f in range(FIELDS):
        v_ref[f, rows - 2] = v_ref[f, rows - 2] - coef * inner_face[f]
        v_ref[f, rows - 1] = v_ref[f, rows - 1] - coef * (outer[f] - inner_face[f])

    edge = jnp.logical_or(lane < 2, lane >= width - 2)
    for f in range(FIELDS):
        packed = d_ref[f]
        for i in range(rows):
            out_ref[f, i] = v_ref[f, i] - jnp.where(edge, shifted(packed, -2 - 4 * i, 1), 0.0)
    if not second:

        def body(i, carry):
            prim = to_primitive(load_row(out_ref, i))
            for f in range(FIELDS):
                w1_ref[f, i] = prim[f]
            return carry

        lax.fori_loop(0, rows, body, 0, unroll=4)
        send_edges(flags, w1_ref, pack_ref, shear_ref, swap)


def call(kernel, name, scalars, arrays, shapes, scratch=(), in_hbm=False):
    smem = pl.BlockSpec(memory_space=pltpu.SMEM)
    vmem = pl.BlockSpec(memory_space=pltpu.VMEM)
    return pl.pallas_call(
        kernel,
        name=name,
        out_shape=[jax.ShapeDtypeStruct(s, jnp.float32) for s in shapes],
        in_specs=[smem] * len(scalars) + [pl.BlockSpec(memory_space=pl.ANY) if in_hbm else vmem] * len(arrays),
        out_specs=[vmem] * len(shapes),
        scratch_shapes=[pltpu.VMEM(s, jnp.float32) if isinstance(s, tuple) else s for s in scratch],
        compiler_params=pltpu.CompilerParams(vmem_limit_bytes=16 * 1024 * 1024),
    )(*scalars, *arrays)


def exchange(block, pack, shear, swap):
    count_x, count_y = lax.axis_size("gx"), lax.axis_size("gy")
    last = (count_x - 1) * count_y

    def crossing(by):
        pairs = []
        for gy in range(count_y):
            pairs.append((last + gy, (gy + by) % count_y))
            pairs.append((gy, last + (gy - by) % count_y))
        return lax.ppermute(shear, ("gx", "gy"), pairs)

    near, following = crossing(block), crossing(block + 1)
    low = lax.ppermute(pack, "gy", [(i, (i + 1) % count_y) for i in range(count_y)])
    high = lax.ppermute(pack, "gy", [((i + 1) % count_y, i) for i in range(count_y)])
    if len(swap) == 1:
        x_low = x_high = lax.ppermute(swap[0], "gx", [(0, 1), (1, 0)])
    else:
        x_low = lax.ppermute(swap[1], "gx", [(i, i + 1) for i in range(count_x - 1)])
        x_high = lax.ppermute(swap[0], "gx", [(i + 1, i) for i in range(count_x - 1)])
    return low, high, x_low, x_high, near, following


def sections(block, flags, weights, radial0, w0, pack, shear, *swap):
    full = w0.shape
    high, width = full[2:]
    tile = (FIELDS, high, width)
    padded = (FIELDS, high + 16, width)
    scratch = [full, padded, padded, padded, tile, tile, tile]
    sends = [pack.shape, shear.shape] + [s.shape for s in swap]

    low, high_y, *others = exchange(block, pack, shear, swap)
    v, t = call(functools.partial(interior_kernel, False), "inner_1", [radial0], [w0], [full, tile], scratch)
    w1, u1, pack1, shear1, *swap1 = call(
        functools.partial(edge_kernel, False),
        "edge_1",
        [flags, weights],
        [v, w0, pack, low, high_y, t, *others],
        [full, full] + sends,
        [tile],
    )
    low, high_y, *others = exchange(block, pack1, shear1, swap1)
    v, t = call(functools.partial(interior_kernel, True), "inner_2", [radial0], [w1, w0, u1], [full, tile], scratch)
    (out,) = call(
        functools.partial(edge_kernel, True),
        "edge_2",
        [flags, weights],
        [v, w1, pack1, low, high_y, t, *others],
        [full],
        [tile],
    )
    return out


def on_device(density, velocity, bfield, pressure, shear_shift, remap_weight):
    rows, high, width = density.shape
    count_x, count_y = lax.axis_size("gx"), lax.axis_size("gy")
    total_x = rows * count_x
    omega = 1.0 / (SHEAR_Q * total_x)
    row = lax.axis_index("gx")
    is_first, is_last = row == 0, row == count_x - 1
    radial0 = (row * rows).astype(jnp.float32) + 0.5 - 0.5 * total_x
    radial0 = jnp.stack([radial0, jnp.float32(SHEAR_Q * omega)])
    weight = remap_weight.astype(jnp.float32) * WEIGHT_SCALE
    block, rest = shear_shift // width, shear_shift % width
    start = jnp.where(is_first, width - 1 - rest, rest)
    flags = jnp.stack([is_first.astype(jnp.int32), is_last.astype(jnp.int32), start.astype(jnp.int32)])
    other = 1.0 - weight
    weights = jnp.stack(
        [
            jnp.where(is_first, 1.0 - weight, 1.0 - other),
            jnp.where(is_first, weight, other),
            jnp.where(is_first, 1.0, -1.0),
        ]
    )
    full = (FIELDS, rows, high, width)
    slab = (FIELDS, 2, high, width)
    sends = [(FIELDS, high, width), slab] + [slab] * (1 if count_x == 2 else 2)
    start_state = call(
        prepare_kernel,
        "prepare",
        [flags, radial0],
        [density, velocity, bfield, pressure],
        [full] + sends,
        [pltpu.SemaphoreType.DMA((4, 2))],
        in_hbm=True,
    )
    branches = [functools.partial(sections, by) for by in range(count_y)]
    return lax.switch(block, branches, flags, weights, radial0, *start_state)


def solution(mesh):
    placed = (
        P("gx", None, "gy"),
        P(None, "gx", None, "gy"),
        P(None, "gx", None, "gy"),
        P("gx", None, "gy"),
        P(),
        P(),
    )
    return jax.shard_map(
        on_device, mesh=mesh, in_specs=placed, out_specs=P(None, "gx", None, "gy"), check_vma=False
    )
```

```python
import functools

import jax
import jax.numpy as jnp
from jax import lax
from jax.experimental import pallas as pl
from jax.experimental.pallas import tpu as pltpu
from jax.sharding import PartitionSpec as P

GAMMA = 5.0 / 3.0
SHEAR_Q = 1.5
TIME_STEP = 0.03
WEIGHT_SCALE = 1.0 / 65536.0
TINY = 1e-30
FIELDS = 8


def root(x):
    return x * lax.rsqrt(jnp.maximum(x, TINY))


def side(state, normal):
    rho, pressure = state[0], state[7]
    vel, mag = state[1:4], state[4:7]
    one, two = [c for c in range(3) if c != normal]
    mom = [rho * v for v in vel]
    vn, bn = vel[normal], mag[normal]
    mn = mom[normal]
    mnvn = mn * vn
    kinetic = 0.5 * ((mnvn + mom[one] * vel[one]) + mom[two] * vel[two])
    bn2 = bn * bn
    bt2 = mag[one] * mag[one] + mag[two] * mag[two]
    half_b2 = 0.5 * (bt2 + bn2)
    inner = kinetic + 1.5 * pressure
    energy = inner + half_b2
    ind_one = vn * mag[one] - bn * vel[one]
    ind_two = vn * mag[two] - bn * vel[two]
    flux = [None] * FIELDS
    flux[0] = mn
    flux[1 + normal] = mnvn + (pressure + half_b2) - bn2
    flux[1 + one] = mn * vel[one] - bn * mag[one]
    flux[1 + two] = mn * vel[two] - bn * mag[two]
    flux[4 + one] = ind_one
    flux[4 + two] = ind_two
    flux[7] = vn * (inner + pressure) + (mag[one] * ind_one + mag[two] * ind_two)
    cons = [rho] + mom + list(mag) + [energy]
    half_gp = (0.5 * GAMMA) * pressure
    spread = half_gp - half_b2
    disc = spread * spread + (GAMMA * pressure) * bt2
    fast = (half_gp + half_b2) + root(disc)
    speed = jnp.abs(vn) + fast * lax.rsqrt(jnp.maximum(rho * fast, TINY))
    return flux, cons, speed


def face(left, right, normal):
    fl, ul, sl = side(left, normal)
    fr, ur, sr = side(right, normal)
    speed = jnp.maximum(sl, sr)
    out = []
    for f in range(FIELDS):
        jump = speed * (ur[f] - ul[f])
        out.append(-jump if fl[f] is None else (fl[f] + fr[f]) - jump)
    return out


def limited(up, down):
    return jnp.maximum(jnp.minimum(up, down), jnp.minimum(jnp.maximum(up, down), 0.0))


def shifted(x, by, axis):
    return pltpu.roll(x, by % x.shape[axis], axis)


def to_conserved(w):
    rho = w[0]
    mom = [rho * v for v in w[1:4]]
    kinetic = 0.5 * (mom[0] * w[1] + mom[1] * w[2] + mom[2] * w[3])
    magnetic = 0.5 * (w[4] * w[4] + w[5] * w[5] + w[6] * w[6])
    return [rho] + mom + list(w[4:7]) + [1.5 * w[7] + kinetic + magnetic]


def to_primitive(u):
    inverse = 1.0 / u[0]
    vel = [m * inverse for m in u[1:4]]
    kinetic = 0.5 * (u[1] * vel[0] + u[2] * vel[1] + u[3] * vel[2])
    magnetic = 0.5 * (u[4] * u[4] + u[5] * u[5] + u[6] * u[6])
    return [u[0]] + vel + list(u[4:7]) + [(GAMMA - 1.0) * (u[7] - kinetic - magnetic)]


def lanes_of(shape):
    return lax.broadcasted_iota(jnp.int32, shape, 1)


def load_row(ref, i):
    return [ref[f, i] for f in range(FIELDS)]


def pack_edges(ref, out_ref):
    rows, high, width = ref.shape[1:]
    lane = lanes_of((high, width))
    per_tile = width // 8
    for f in range(FIELDS):
        for i in range(rows):
            at = 8 * (i % per_tile)
            moved = shifted(ref[f, i], at + 4, 1)
            packed = moved if at == 0 else jnp.where(lane >= at, moved, packed)
            if at == 8 * (per_tile - 1) or i == rows - 1:
                out_ref[f, i // per_tile] = packed


def halves(pack_ref, last_ref, first_ref):
    lane = lanes_of(pack_ref.shape[2:])
    low = lane % 8 < 4
    for f in range(FIELDS):
        one, two = pack_ref[f, 0], pack_ref[f, 1]
        last_ref[f] = jnp.where(low, one, shifted(two, 4, 1))
        first_ref[f] = jnp.where(low, shifted(one, -4, 1), two)


def send_edges(flags, w_ref, pack_ref, last_ref, first_ref, shear_ref, swap_refs):
    rows = w_ref.shape[1]
    pack_edges(w_ref, pack_ref)
    halves(pack_ref, last_ref, first_ref)
    first = flags[0] == 1
    for k in range(2):
        low, high = load_row(w_ref, k), load_row(w_ref, rows - 2 + k)
        if len(swap_refs) == 1:
            for f in range(FIELDS):
                swap_refs[0][f, k] = jnp.where(first, high[f], low[f])
        else:
            for f in range(FIELDS):
                swap_refs[0][f, k] = low[f]
                swap_refs[1][f, k] = high[f]
        outer = to_conserved([jnp.where(first, low[f], high[f]) for f in range(FIELDS)])
        for f in range(FIELDS):
            shear_ref[f, k] = outer[f]


def prepare_kernel(flags, radial0, rho_hbm, vel_hbm, mag_hbm, pres_hbm, w_ref, *rest):
    *sends, sems = rest
    rows = w_ref.shape[1]
    parts = sems.shape[1]
    size = rows // parts
    copies = []
    for part in range(parts):
        at = pl.ds(part * size, size)
        copies.append(
            [
                pltpu.make_async_copy(rho_hbm.at[at], w_ref.at[0, at], sems.at[0, part]),
                pltpu.make_async_copy(vel_hbm.at[:, at], w_ref.at[pl.ds(1, 3), at], sems.at[1, part]),
                pltpu.make_async_copy(mag_hbm.at[:, at], w_ref.at[pl.ds(4, 3), at], sems.at[2, part]),
                pltpu.make_async_copy(pres_hbm.at[at], w_ref.at[7, at], sems.at[3, part]),
            ]
        )
        for copy in copies[-1]:
            copy.start()
    for part in range(parts):
        for copy in copies[part]:
            copy.wait()
        for i in range(part * size, (part + 1) * size):
            w_ref[2, i] = w_ref[2, i] - radial0[1] * (radial0[0] + float(i))
    send_edges(flags, w_ref, *sends[:4], sends[4:])


def axis_states(w, half):
    left, right = [], []
    for f in range(FIELDS):
        up = shifted(half[f], -1, 1) - half[f]
        slope = limited(up, shifted(up, 1, 1))
        left.append(w[f] + slope)
        right.append(w[f] - slope)
    return left, right


def wrapped(ref, f, value, before, after):
    high = value.shape[0]
    ref[f, 8 : 8 + high] = value
    if before:
        ref[f, 0:8] = value[high - 8 : high]
    if after:
        ref[f, 8 + high : 16 + high] = value[0:8]


def interior_kernel(second, radial0, w_ref, *refs):
    if second:
        w0_ref, u1_ref = refs[:2]
        refs = refs[2:]
    v_ref, hz_ref, rz_ref, fz_ref, wl_ref, dx_ref, fx_ref = refs
    rows, high, width = w_ref.shape[1:]
    step = 0.5 * TIME_STEP if second else TIME_STEP
    coef = 0.5 * step
    lane = lanes_of(w_ref.shape[2:])
    inner = jnp.logical_and(lane >= 1, lane < width - 2)
    omega_q = radial0[1]
    omega = omega_q / SHEAR_Q
    next_row, last_row = slice(9, 9 + high), slice(7, 7 + high)

    for f in range(FIELDS):
        blank = jnp.zeros((high, width), jnp.float32)
        dx_ref[f], fx_ref[f], wl_ref[f] = blank, blank, w_ref[f, 0]

    def body(i, carry):
        w = load_row(w_ref, i)
        half = [0.5 * x for x in w]

        left = []
        for f in range(FIELDS):
            wrapped(hz_ref, f, half[f], True, True)
            slope = limited(hz_ref[f, next_row] - half[f], half[f] - hz_ref[f, last_row])
            left.append(w[f] + slope)
            wrapped(rz_ref, f, w[f] - slope, False, True)
        fz = face(left, [rz_ref[f, next_row] for f in range(FIELDS)], 2)
        total = []
        for f in range(FIELDS):
            wrapped(fz_ref, f, fz[f], True, False)
            total.append(fz[f] - fz_ref[f, last_row])

        left, right = axis_states(w, half)
        fy = face(left, [shifted(r, -1, 1) for r in right], 1)
        fy = [jnp.where(inner, f, 0.0) for f in fy]
        total = [total[f] + (fy[f] - shifted(fy[f], 1, 1)) for f in range(FIELDS)]

        after, before = jnp.minimum(i + 1, rows - 1), jnp.maximum(i - 1, 0)
        right, wl = [], [wl_ref[f] for f in range(FIELDS)]
        for f in range(FIELDS):
            up = 0.5 * w_ref[f, after] - half[f]
            slope = limited(up, dx_ref[f])
            dx_ref[f] = up
            wl_ref[f] = w[f] + slope
            right.append(w[f] - slope)
        fx = face(wl, right, 0)
        valid = jnp.logical_and(i >= 2, i <= rows - 2)
        for f in range(FIELDS):
            here = jnp.where(valid, fx[f], 0.0)
            v_ref[f, before] = v_ref[f, before] - coef * (here - fx_ref[f])
            fx_ref[f] = here

        x = radial0[0] + i.astype(jnp.float32)
        cons = to_conserved(w)
        if second:
            base = [0.5 * (a + u1_ref[f, i]) for f, a in enumerate(to_conserved(load_row(w0_ref, i)))]
        else:
            base = cons
        tidal = 2.0 * omega * omega_q * x
        value = [base[f] - coef * total[f] for f in range(FIELDS)]
        value[1] = value[1] + ((step * 2.0) * omega * cons[2] + (step * tidal) * cons[0])
        value[2] = value[2] - ((step * 2.0) * omega) * cons[1]
        value[7] = value[7] + (step * tidal) * cons[1]
        for f in range(FIELDS):
            v_ref[f, i] = value[f]
        return carry

    lax.fori_loop(0, rows, body, 0)


def sheared_rows(flags, weights, near_ref, next_ref):
    first = flags[0] == 1
    high, width = near_ref.shape[2:]
    start = flags[2]
    lane = lanes_of((high, width))

    def taken(one, two, at):
        back = lax.rem(2 * width - at, width)
        return jnp.where(lane < width - at, pltpu.roll(one, back, 1), pltpu.roll(two, back, 1))

    rows = []
    for k in range(2):
        ghost = []
        for f in range(FIELDS):
            near, following = near_ref[f, k], next_ref[f, k]
            one = jnp.where(first, following, near)
            two = jnp.where(first, near, following)
            ghost.append(weights[0] * taken(one, two, start + 1) + weights[1] * taken(one, two, start))
        delta = weights[2]
        boosted = list(ghost)
        boosted[2] = ghost[2] + ghost[0] * delta
        boosted[7] = ghost[7] + ghost[2] * delta + 0.5 * ghost[0] * delta * delta
        rows.append(to_primitive(boosted))
    return rows


def edge_kernel(
    second, flags, weights, v_ref, w_ref, own_ref, low_ref, high_ref, xl_ref, xr_ref, near_ref, next_ref, *refs
):
    rows, high, width = w_ref.shape[1:]
    step = 0.5 * TIME_STEP if second else TIME_STEP
    coef = 0.5 * step
    if second:
        out_ref, d_ref = refs
    else:
        w1_ref, out_ref, *sends, d_ref = refs
    first, last = flags[0] == 1, flags[1] == 1
    lane = lanes_of((high, width))
    place = lane % 8
    low = place < 4

    for part in range(2):
        own = [own_ref[f, part] for f in range(FIELDS)]
        a = [low_ref[f] if part == 0 else shifted(low_ref[f], -4, 1) for f in range(FIELDS)]
        b = [shifted(high_ref[f], 4, 1) if part == 0 else high_ref[f] for f in range(FIELDS)]
        a = [jnp.where(low, a[f], own[f]) for f in range(FIELDS)]
        b = [jnp.where(low, own[f], b[f]) for f in range(FIELDS)]
        left, right = axis_states(a, [0.5 * x for x in a])
        fa = face(left, [shifted(r, -1, 1) for r in right], 1)
        left, right = axis_states(b, [0.5 * x for x in b])
        fb = face(left, [shifted(r, -1, 1) for r in right], 1)
        upper_at = jnp.logical_and(place >= 2, place <= 4)
        lower_at = jnp.logical_and(place >= 3, place <= 5)
        for f in range(FIELDS):
            upper = jnp.where(upper_at, jnp.where(low, fb[f], fa[f]), 0.0)
            lower = shifted(jnp.where(place == 2, fb[f], fa[f]), 1, 1)
            d_ref[f, part] = coef * (upper - jnp.where(lower_at, lower, 0.0))

    def x_states(cells):
        left, right = [], []
        for f in range(FIELDS):
            before, here, after = (c[f] for c in cells)
            slope = limited(0.5 * (after - here), 0.5 * (here - before))
            left.append(here + slope)
            right.append(here - slope)
        return left, right

    ghost = sheared_rows(flags, weights, near_ref, next_ref)
    ghost_low = [[jnp.where(first, ghost[k][f], xl_ref[f, k]) for f in range(FIELDS)] for k in range(2)]
    cells = ghost_low + [load_row(w_ref, i) for i in range(3)]
    sides = [x_states(cells[k : k + 3]) for k in range(3)]
    outer = face(sides[0][0], sides[1][1], 0)
    inner_face = face(sides[1][0], sides[2][1], 0)
    for f in range(FIELDS):
        v_ref[f, 0] = v_ref[f, 0] - coef * (inner_face[f] - outer[f])
        v_ref[f, 1] = v_ref[f, 1] + coef * inner_face[f]
    ghost_high = [[jnp.where(last, ghost[k][f], xr_ref[f, k]) for f in range(FIELDS)] for k in range(2)]
    cells = [load_row(w_ref, rows - 3 + i) for i in range(3)] + ghost_high
    sides = [x_states(cells[k : k + 3]) for k in range(3)]
    inner_face = face(sides[0][0], sides[1][1], 0)
    outer = face(sides[1][0], sides[2][1], 0)
    for f in range(FIELDS):
        v_ref[f, rows - 2] = v_ref[f, rows - 2] - coef * inner_face[f]
        v_ref[f, rows - 1] = v_ref[f, rows - 1] - coef * (outer[f] - inner_face[f])

    edge = jnp.logical_or(lane < 2, lane >= width - 2)
    per_tile = width // 8
    for f in range(FIELDS):
        for i in range(rows):
            move = shifted(d_ref[f, i // per_tile], -4 - 8 * (i % per_tile), 1)
            out_ref[f, i] = v_ref[f, i] - jnp.where(edge, move, 0.0)
    if not second:

        def body(i, carry):
            prim = to_primitive(load_row(out_ref, i))
            for f in range(FIELDS):
                w1_ref[f, i] = prim[f]
            return carry

        lax.fori_loop(0, rows, body, 0, unroll=4)
        send_edges(flags, w1_ref, *sends[:4], sends[4:])


def call(kernel, name, scalars, arrays, shapes, scratch=(), in_hbm=False):
    smem = pl.BlockSpec(memory_space=pltpu.SMEM)
    vmem = pl.BlockSpec(memory_space=pltpu.VMEM)
    return pl.pallas_call(
        kernel,
        name=name,
        out_shape=[jax.ShapeDtypeStruct(s, jnp.float32) for s in shapes],
        in_specs=[smem] * len(scalars) + [pl.BlockSpec(memory_space=pltpu.HBM) if in_hbm else vmem] * len(arrays),
        out_specs=[vmem] * len(shapes),
        scratch_shapes=[pltpu.VMEM(s, jnp.float32) if isinstance(s, tuple) else s for s in scratch],
        compiler_params=pltpu.CompilerParams(vmem_limit_bytes=16 * 1024 * 1024),
    )(*scalars, *arrays)


def exchange(last, first, swap):
    count_x, count_y = lax.axis_size("gx"), lax.axis_size("gy")
    low = lax.ppermute(last, "gy", [(i, (i + 1) % count_y) for i in range(count_y)])
    high = lax.ppermute(first, "gy", [((i + 1) % count_y, i) for i in range(count_y)])
    if len(swap) == 1:
        x_low = x_high = lax.ppermute(swap[0], "gx", [(0, 1), (1, 0)])
    else:
        x_low = lax.ppermute(swap[1], "gx", [(i, i + 1) for i in range(count_x - 1)])
        x_high = lax.ppermute(swap[0], "gx", [(i + 1, i) for i in range(count_x - 1)])
    return low, high, x_low, x_high


def crossing(by, shear):
    count_x, count_y = lax.axis_size("gx"), lax.axis_size("gy")
    last = (count_x - 1) * count_y
    pairs = []
    for gy in range(count_y):
        pairs.append((last + gy, (gy + by) % count_y))
        pairs.append((gy, last + (gy - by) % count_y))
    return lax.ppermute(shear, ("gx", "gy"), pairs)


def inner_part(second, block, radial0, shear, *states):
    full = states[0].shape
    high, width = full[2:]
    tile = (FIELDS, high, width)
    padded = (FIELDS, high + 16, width)
    scratch = [padded, padded, padded, tile, tile, tile]

    def branch(by):
        def run(radial0, shear, *states):
            near, following = crossing(by, shear), crossing(by + 1, shear)
            kernel = functools.partial(interior_kernel, second)
            (v,) = call(kernel, "inner_2" if second else "inner_1", [radial0], list(states), [full], scratch)
            return v, near, following

        return run

    branches = [branch(by) for by in range(lax.axis_size("gy"))]
    return lax.switch(block, branches, radial0, shear, *states)


def sections(block, flags, weights, radial0, w0, pack, last, first, shear, *swap):
    full = w0.shape
    moves = [pack.shape]
    sends = [x.shape for x in (pack, last, first, shear, *swap)]
    got = exchange(last, first, swap)
    v, *sheared = inner_part(False, block, radial0, shear, w0)
    w1, u1, pack1, last1, first1, shear1, *swap1 = call(
        functools.partial(edge_kernel, False),
        "edge_1",
        [flags, weights],
        [v, w0, pack, *got, *sheared],
        [full, full] + sends,
        moves,
    )
    got = exchange(last1, first1, swap1)
    v, *sheared = inner_part(True, block, radial0, shear1, w1, w0, u1)
    (out,) = call(
        functools.partial(edge_kernel, True),
        "edge_2",
        [flags, weights],
        [v, w1, pack1, *got, *sheared],
        [full],
        moves,
    )
    return out


def on_device(density, velocity, bfield, pressure, shear_shift, remap_weight):
    rows, high, width = density.shape
    count_x, count_y = lax.axis_size("gx"), lax.axis_size("gy")
    total_x = rows * count_x
    omega = 1.0 / (SHEAR_Q * total_x)
    row = lax.axis_index("gx")
    is_first, is_last = row == 0, row == count_x - 1
    radial0 = (row * rows).astype(jnp.float32) + 0.5 - 0.5 * total_x
    radial0 = jnp.stack([radial0, jnp.float32(SHEAR_Q * omega)])
    weight = remap_weight.astype(jnp.float32) * WEIGHT_SCALE
    block, rest = shear_shift // width, shear_shift % width
    start = jnp.where(is_first, width - 1 - rest, rest)
    flags = jnp.stack([is_first.astype(jnp.int32), is_last.astype(jnp.int32), start.astype(jnp.int32)])
    other = 1.0 - weight
    weights = jnp.stack(
        [
            jnp.where(is_first, 1.0 - weight, 1.0 - other),
            jnp.where(is_first, weight, other),
            jnp.where(is_first, 1.0, -1.0),
        ]
    )
    full = (FIELDS, rows, high, width)
    slab = (FIELDS, 2, high, width)
    packed = (FIELDS, 8 * rows // width, high, width)
    tile = (FIELDS, high, width)
    sends = [packed, tile, tile, slab] + [slab] * (1 if count_x == 2 else 2)
    start_state = call(
        prepare_kernel,
        "prepare",
        [flags, radial0],
        [density, velocity, bfield, pressure],
        [full] + sends,
        [pltpu.SemaphoreType.DMA((4, 2))],
        in_hbm=True,
    )
    return sections(block, flags, weights, radial0, *start_state)


def solution(mesh):
    placed = (
        P("gx", None, "gy"),
        P(None, "gx", None, "gy"),
        P(None, "gx", None, "gy"),
        P("gx", None, "gy"),
        P(),
        P(),
    )
    return jax.shard_map(
        on_device, mesh=mesh, in_specs=placed, out_specs=P(None, "gx", None, "gy"), check_vma=False
    )
```

```python
import functools

import jax
import jax.numpy as jnp
from jax import lax
from jax.experimental import pallas as pl
from jax.experimental.pallas import tpu as pltpu
from jax.sharding import PartitionSpec as P

GAMMA = 5.0 / 3.0
SHEAR_Q = 1.5
TIME_STEP = 0.03
WEIGHT_SCALE = 1.0 / 65536.0
TINY = 1e-30
FIELDS = 8
PAD = 8


def root(x):
    return x * lax.rsqrt(jnp.maximum(x, TINY))


def side(state, normal):
    rho, pressure = state[0], state[7]
    vel, mag = state[1:4], state[4:7]
    one, two = [c for c in range(3) if c != normal]
    mom = [rho * v for v in vel]
    vn, bn = vel[normal], mag[normal]
    mn = mom[normal]
    mnvn = mn * vn
    kinetic = 0.5 * ((mnvn + mom[one] * vel[one]) + mom[two] * vel[two])
    bn2 = bn * bn
    bt2 = mag[one] * mag[one] + mag[two] * mag[two]
    half_b2 = 0.5 * (bt2 + bn2)
    inner = kinetic + 1.5 * pressure
    energy = inner + half_b2
    ind_one = vn * mag[one] - bn * vel[one]
    ind_two = vn * mag[two] - bn * vel[two]
    flux = [None] * FIELDS
    flux[0] = mn
    flux[1 + normal] = mnvn + (pressure + half_b2) - bn2
    flux[1 + one] = mn * vel[one] - bn * mag[one]
    flux[1 + two] = mn * vel[two] - bn * mag[two]
    flux[4 + one] = ind_one
    flux[4 + two] = ind_two
    flux[7] = vn * (inner + pressure) + (mag[one] * ind_one + mag[two] * ind_two)
    cons = [rho] + mom + list(mag) + [energy]
    half_gp = (0.5 * GAMMA) * pressure
    spread = half_gp - half_b2
    disc = spread * spread + (GAMMA * pressure) * bt2
    fast = (half_gp + half_b2) + root(disc)
    speed = jnp.abs(vn) + fast * lax.rsqrt(jnp.maximum(rho * fast, TINY))
    return flux, cons, speed


def face(left, right, normal):
    fl, ul, sl = side(left, normal)
    fr, ur, sr = side(right, normal)
    speed = jnp.maximum(sl, sr)
    out = []
    for f in range(FIELDS):
        jump = speed * (ur[f] - ul[f])
        out.append(-jump if fl[f] is None else (fl[f] + fr[f]) - jump)
    return out


def limited(up, down):
    return jnp.maximum(jnp.minimum(up, down), jnp.minimum(jnp.maximum(up, down), 0.0))


def to_conserved(w):
    rho = w[0]
    mom = [rho * v for v in w[1:4]]
    kinetic = 0.5 * (mom[0] * w[1] + mom[1] * w[2] + mom[2] * w[3])
    magnetic = 0.5 * (w[4] * w[4] + w[5] * w[5] + w[6] * w[6])
    return [rho] + mom + list(w[4:7]) + [1.5 * w[7] + kinetic + magnetic]


def to_primitive(u):
    inverse = 1.0 / u[0]
    vel = [m * inverse for m in u[1:4]]
    kinetic = 0.5 * (u[1] * vel[0] + u[2] * vel[1] + u[3] * vel[2])
    magnetic = 0.5 * (u[4] * u[4] + u[5] * u[5] + u[6] * u[6])
    return [u[0]] + vel + list(u[4:7]) + [(GAMMA - 1.0) * (u[7] - kinetic - magnetic)]


def lanes_of(shape):
    return lax.broadcasted_iota(jnp.int32, shape, 1)


def load_row(ref, i):
    return [ref[f, i] for f in range(FIELDS)]


def turn(w_ref, f, g, wt_ref):
    high, width = w_ref.shape[2:]
    size = width // high
    tile = w_ref[f, g * size : (g + 1) * size].reshape(width, width)
    wt_ref[f, g, PAD : PAD + width] = tile.T


def send_columns(wt_ref, last_ref, first_ref):
    groups, rows = wt_ref.shape[1:3]
    for f in range(FIELDS):
        for k in range(2):
            for g in range(groups):
                to = slice(k * groups + g, k * groups + g + 1)
                first_ref[f, to] = wt_ref[f, g, PAD + k : PAD + k + 1]
                last_ref[f, to] = wt_ref[f, g, rows - PAD - 2 + k : rows - PAD - 1 + k]


def send_rows(flags, w_ref, shear_ref, *swap_refs):
    rows = w_ref.shape[1]
    first = flags[0] == 1
    for k in range(2):
        low, high = load_row(w_ref, k), load_row(w_ref, rows - 2 + k)
        if len(swap_refs) == 1:
            for f in range(FIELDS):
                swap_refs[0][f, k] = jnp.where(first, high[f], low[f])
        else:
            for f in range(FIELDS):
                swap_refs[0][f, k] = low[f]
                swap_refs[1][f, k] = high[f]
        outer = to_conserved([jnp.where(first, low[f], high[f]) for f in range(FIELDS)])
        for f in range(FIELDS):
            shear_ref[f, k] = outer[f]


def prepare_kernel(flags, radial0, rho_hbm, vel_hbm, mag_hbm, pres_hbm, w_ref, wt_ref, last_ref, first_ref, *rest):
    *sends, sems = rest
    rows = w_ref.shape[1]
    parts = sems.shape[1]
    size = rows // parts
    copies = []
    for part in range(parts):
        at = pl.ds(part * size, size)
        copies.append(
            [
                pltpu.make_async_copy(rho_hbm.at[at], w_ref.at[0, at], sems.at[0, part]),
                pltpu.make_async_copy(vel_hbm.at[:, at], w_ref.at[pl.ds(1, 3), at], sems.at[1, part]),
                pltpu.make_async_copy(mag_hbm.at[:, at], w_ref.at[pl.ds(4, 3), at], sems.at[2, part]),
                pltpu.make_async_copy(pres_hbm.at[at], w_ref.at[7, at], sems.at[3, part]),
            ]
        )
        for copy in copies[-1]:
            copy.start()
    for part in range(parts):
        for copy in copies[part]:
            copy.wait()
        for i in range(part * size, (part + 1) * size):
            w_ref[2, i] = w_ref[2, i] - radial0[1] * (radial0[0] + float(i))
        for f in range(FIELDS):
            turn(w_ref, f, part, wt_ref)
    send_columns(wt_ref, last_ref, first_ref)
    send_rows(flags, w_ref, *sends)


def three_states(cells):
    left, right = [], []
    for f in range(FIELDS):
        before, here, after = (c[f] for c in cells)
        slope = limited(0.5 * (after - here), 0.5 * (here - before))
        left.append(here + slope)
        right.append(here - slope)
    return left, right


def wrapped(ref, f, value, before, after):
    high = value.shape[0]
    ref[f, 8 : 8 + high] = value
    if before:
        ref[f, 0:8] = value[high - 8 : high]
    if after:
        ref[f, 8 + high : 16 + high] = value[0:8]


def behind(ref, f, value):
    high = value.shape[0]
    ref[f, 8 : 8 + high] = value
    result = ref[f, 7 : 7 + high]
    ref[f, 0:8] = value[high - 8 : high]
    return result


def interior_kernel(second, radial0, w_ref, wt_ref, *refs):
    if second:
        w0_ref, u1_ref = refs[:2]
        refs = refs[2:]
    v_ref, dy_ref, hz_ref, rz_ref, fz_ref, wl_ref, dx_ref, fx_ref = refs
    rows, high, width = w_ref.shape[1:]
    groups = wt_ref.shape[1]
    step = 0.5 * TIME_STEP if second else TIME_STEP
    coef = 0.5 * step
    omega_q = radial0[1]
    omega = omega_q / SHEAR_Q
    next_row, last_row = slice(9, 9 + high), slice(7, 7 + high)

    for f in range(FIELDS):
        blank = jnp.zeros((high, width), jnp.float32)
        dx_ref[f], fx_ref[f], wl_ref[f] = blank, blank, w_ref[f, 0]

    def body(i, carry):
        w = load_row(w_ref, i)
        half = [0.5 * x for x in w]

        left = []
        for f in range(FIELDS):
            wrapped(hz_ref, f, half[f], True, True)
            slope = limited(hz_ref[f, next_row] - half[f], half[f] - hz_ref[f, last_row])
            left.append(w[f] + slope)
            wrapped(rz_ref, f, w[f] - slope, False, True)
        fz = face(left, [rz_ref[f, next_row] for f in range(FIELDS)], 2)
        total = []
        for f in range(FIELDS):
            wrapped(fz_ref, f, fz[f], True, False)
            total.append(fz[f] - fz_ref[f, last_row])

        after, before = jnp.minimum(i + 1, rows - 1), jnp.maximum(i - 1, 0)
        right, wl = [], [wl_ref[f] for f in range(FIELDS)]
        for f in range(FIELDS):
            up = 0.5 * w_ref[f, after] - half[f]
            slope = limited(up, dx_ref[f])
            dx_ref[f] = up
            wl_ref[f] = w[f] + slope
            right.append(w[f] - slope)
        fx = face(wl, right, 0)
        valid = jnp.logical_and(i >= 2, i <= rows - 2)
        for f in range(FIELDS):
            here = jnp.where(valid, fx[f], 0.0)
            v_ref[f, before] = v_ref[f, before] - coef * (here - fx_ref[f])
            fx_ref[f] = here

        x = radial0[0] + i.astype(jnp.float32)
        cons = to_conserved(w)
        if second:
            base = [0.5 * (a + u1_ref[f, i]) for f, a in enumerate(to_conserved(load_row(w0_ref, i)))]
        else:
            base = cons
        tidal = 2.0 * omega * omega_q * x
        value = [base[f] - coef * total[f] for f in range(FIELDS)]
        value[1] = value[1] + ((step * 2.0) * omega * cons[2] + (step * tidal) * cons[0])
        value[2] = value[2] - ((step * 2.0) * omega) * cons[1]
        value[7] = value[7] + (step * tidal) * cons[1]
        for f in range(FIELDS):
            v_ref[f, i] = value[f]
        return carry

    lax.fori_loop(0, rows, body, 0)

    size = 16
    strips = width // size
    row = lax.broadcasted_iota(jnp.int32, (size, width), 0)

    def body_y(n, carry):
        g, start = lax.div(n, strips), size * lax.rem(n, strips)
        at = pl.multiple_of(start + PAD, 8)
        left, right = [], []
        for f in range(FIELDS):
            w = wt_ref[f, g, pl.ds(at, size)]
            up = 0.5 * (wt_ref[f, g, pl.ds(at + 1, size)] - w)
            slope = limited(up, behind(hz_ref, f, up))
            left.append(behind(rz_ref, f, w + slope))
            right.append(w - slope)
        fy = face(left, right, 1)
        cell = row + start
        valid = jnp.logical_and(cell >= 2, cell <= width - 2)
        for f in range(FIELDS):
            here = jnp.where(valid, fy[f], 0.0)
            dy_ref[f, g, pl.ds(at - 1, size)] = coef * (here - behind(fz_ref, f, here))
        return carry

    lax.fori_loop(0, groups * strips, body_y, 0)
    for f in range(FIELDS):
        for g in range(groups):
            dy_ref[f, g, PAD + width - 1 : PAD + width] = jnp.zeros((1, width), jnp.float32)


def sheared_rows(flags, weights, near_ref, next_ref):
    first = flags[0] == 1
    high, width = near_ref.shape[2:]
    start = flags[2]
    lane = lanes_of((high, width))

    def taken(one, two, at):
        back = lax.rem(2 * width - at, width)
        return jnp.where(lane < width - at, pltpu.roll(one, back, 1), pltpu.roll(two, back, 1))

    rows = []
    for k in range(2):
        ghost = []
        for f in range(FIELDS):
            near, following = near_ref[f, k], next_ref[f, k]
            one = jnp.where(first, following, near)
            two = jnp.where(first, near, following)
            ghost.append(weights[0] * taken(one, two, start + 1) + weights[1] * taken(one, two, start))
        delta = weights[2]
        boosted = list(ghost)
        boosted[2] = ghost[2] + ghost[0] * delta
        boosted[7] = ghost[7] + ghost[2] * delta + 0.5 * ghost[0] * delta * delta
        rows.append(to_primitive(boosted))
    return rows


def edge_kernel(second, flags, weights, v_ref, dy_ref, w_ref, wt_ref, low_ref, high_ref, xl_ref, xr_ref, near_ref, next_ref, *refs):
    rows, high, width = w_ref.shape[1:]
    groups = wt_ref.shape[1]
    step = 0.5 * TIME_STEP if second else TIME_STEP
    coef = 0.5 * step
    if second:
        out_ref, e_ref, a_ref, c_ref = refs
    else:
        w1_ref, wt1_ref, out_ref, last_ref, first_ref, *sends, e_ref, a_ref, c_ref = refs
    first, last = flags[0] == 1, flags[1] == 1

    for f in range(FIELDS):
        for k in range(5):
            cell = k - 2
            if cell < 0:
                e_ref[f, k, 0:groups] = low_ref[f, k * groups : (k + 1) * groups]
            else:
                for g in range(groups):
                    e_ref[f, k, g : g + 1] = wt_ref[f, g, PAD + cell : PAD + cell + 1]
            cell = width - 3 + k
            if cell >= width:
                at = (cell - width) * groups
                e_ref[f, k, groups : 2 * groups] = high_ref[f, at : at + groups]
            else:
                for g in range(groups):
                    e_ref[f, k, groups + g : groups + g + 1] = wt_ref[f, g, PAD + cell : PAD + cell + 1]
    cells = [[e_ref[f, k] for f in range(FIELDS)] for k in range(5)]
    sides = [three_states(cells[k : k + 3]) for k in range(3)]
    one = face(sides[0][0], sides[1][1], 1)
    two = face(sides[1][0], sides[2][1], 1)
    low_end = lax.broadcasted_iota(jnp.int32, one[0].shape, 0) < groups
    for f in range(FIELDS):
        a_ref[f, 0] = coef * (two[f] - one[f])
        a_ref[f, 1] = coef * jnp.where(low_end, -two[f], one[f])
        for g in range(groups):
            c_ref[f, g] = jnp.zeros((2 * PAD, width), jnp.float32)
            c_ref[f, g, 0:1] = a_ref[f, 0, g : g + 1]
            c_ref[f, g, 1:2] = a_ref[f, 1, g : g + 1]
            c_ref[f, g, 2 * PAD - 2 : 2 * PAD - 1] = a_ref[f, 1, groups + g : groups + g + 1]
            c_ref[f, g, 2 * PAD - 1 : 2 * PAD] = a_ref[f, 0, groups + g : groups + g + 1]

    size = rows // groups
    for g in range(groups):
        at = slice(g * size, (g + 1) * size)
        for f in range(FIELDS):
            head = dy_ref[f, g, PAD : 2 * PAD] + c_ref[f, g, 0:PAD]
            tail = dy_ref[f, g, width : PAD + width] + c_ref[f, g, PAD : 2 * PAD]
            strip = jnp.concatenate([head, dy_ref[f, g, 2 * PAD : width], tail], axis=0)
            out_ref[f, at] = v_ref[f, at] - strip.T.reshape(size, high, width)

    ghost = sheared_rows(flags, weights, near_ref, next_ref)
    ghost_low = [[jnp.where(first, ghost[k][f], xl_ref[f, k]) for f in range(FIELDS)] for k in range(2)]
    cells = ghost_low + [load_row(w_ref, i) for i in range(3)]
    sides = [three_states(cells[k : k + 3]) for k in range(3)]
    outer = face(sides[0][0], sides[1][1], 0)
    inner = face(sides[1][0], sides[2][1], 0)
    for f in range(FIELDS):
        out_ref[f, 0] = out_ref[f, 0] - coef * (inner[f] - outer[f])
        out_ref[f, 1] = out_ref[f, 1] + coef * inner[f]
    ghost_high = [[jnp.where(last, ghost[k][f], xr_ref[f, k]) for f in range(FIELDS)] for k in range(2)]
    cells = [load_row(w_ref, rows - 3 + i) for i in range(3)] + ghost_high
    sides = [three_states(cells[k : k + 3]) for k in range(3)]
    inner = face(sides[0][0], sides[1][1], 0)
    outer = face(sides[1][0], sides[2][1], 0)
    for f in range(FIELDS):
        out_ref[f, rows - 2] = out_ref[f, rows - 2] - coef * inner[f]
        out_ref[f, rows - 1] = out_ref[f, rows - 1] - coef * (outer[f] - inner[f])
    if second:
        return

    def body(i, carry):
        prim = to_primitive(load_row(out_ref, i))
        for f in range(FIELDS):
            w1_ref[f, i] = prim[f]
        return carry

    lax.fori_loop(0, rows, body, 0, unroll=4)
    for g in range(groups):
        for f in range(FIELDS):
            turn(w1_ref, f, g, wt1_ref)
    send_columns(wt1_ref, last_ref, first_ref)
    send_rows(flags, w1_ref, *sends)


def call(kernel, name, scalars, arrays, shapes, scratch=(), in_hbm=False):
    smem = pl.BlockSpec(memory_space=pltpu.SMEM)
    vmem = pl.BlockSpec(memory_space=pltpu.VMEM)
    return pl.pallas_call(
        kernel,
        name=name,
        out_shape=[jax.ShapeDtypeStruct(s, jnp.float32) for s in shapes],
        in_specs=[smem] * len(scalars) + [pl.BlockSpec(memory_space=pltpu.HBM) if in_hbm else vmem] * len(arrays),
        out_specs=[vmem] * len(shapes),
        scratch_shapes=[pltpu.VMEM(s, jnp.float32) if isinstance(s, tuple) else s for s in scratch],
        compiler_params=pltpu.CompilerParams(vmem_limit_bytes=20 * 1024 * 1024),
    )(*scalars, *arrays)


def exchange(last, first, swap):
    count_x, count_y = lax.axis_size("gx"), lax.axis_size("gy")
    low = lax.ppermute(last, "gy", [(i, (i + 1) % count_y) for i in range(count_y)])
    high = lax.ppermute(first, "gy", [((i + 1) % count_y, i) for i in range(count_y)])
    if len(swap) == 1:
        x_low = x_high = lax.ppermute(swap[0], "gx", [(0, 1), (1, 0)])
    else:
        x_low = lax.ppermute(swap[1], "gx", [(i, i + 1) for i in range(count_x - 1)])
        x_high = lax.ppermute(swap[0], "gx", [(i + 1, i) for i in range(count_x - 1)])
    return low, high, x_low, x_high


def crossing(by, shear):
    count_x, count_y = lax.axis_size("gx"), lax.axis_size("gy")
    last = (count_x - 1) * count_y
    pairs = []
    for gy in range(count_y):
        pairs.append((last + gy, (gy + by) % count_y))
        pairs.append((gy, last + (gy - by) % count_y))
    return lax.ppermute(shear, ("gx", "gy"), pairs)


def inner_scratch(full):
    high, width = full[2:]
    tile = (FIELDS, high, width)
    padded = (FIELDS, high + 2 * PAD, width)
    return [padded, padded, padded, tile, tile, tile]


def inner_part(second, block, radial0, shear, *states):
    full, turned = states[0].shape, states[1].shape

    def branch(by):
        def run(radial0, shear, *states):
            near, following = crossing(by, shear), crossing(by + 1, shear)
            kernel = functools.partial(interior_kernel, second)
            name = "inner_2" if second else "inner_1"
            v, dy = call(kernel, name, [radial0], list(states), [full, turned], inner_scratch(full))
            return v, dy, near, following

        return run

    branches = [branch(by) for by in range(lax.axis_size("gy"))]
    return lax.switch(block, branches, radial0, shear, *states)


def sections(block, flags, weights, radial0, w0, wt0, last, first, shear, *swap):
    full, turned = w0.shape, wt0.shape
    groups, width = turned[1], full[3]
    scratch = [(FIELDS, 5, 2 * groups, width), (FIELDS, 2, 2 * groups, width), (FIELDS, groups, 2 * PAD, width)]
    sends = [x.shape for x in (last, first, shear, *swap)]
    got = exchange(last, first, swap)
    v, dy, *sheared = inner_part(False, block, radial0, shear, w0, wt0)
    w1, wt1, u1, last, first, shear, *swap = call(
        functools.partial(edge_kernel, False),
        "edge_1",
        [flags, weights],
        [v, dy, w0, wt0, *got, *sheared],
        [full, turned, full] + sends,
        scratch,
    )
    got = exchange(last, first, swap)
    v, dy, *sheared = inner_part(True, block, radial0, shear, w1, wt1, w0, u1)
    (out,) = call(
        functools.partial(edge_kernel, True),
        "edge_2",
        [flags, weights],
        [v, dy, w1, wt1, *got, *sheared],
        [full],
        scratch,
    )
    return out


def on_device(density, velocity, bfield, pressure, shear_shift, remap_weight):
    rows, high, width = density.shape
    count_x, count_y = lax.axis_size("gx"), lax.axis_size("gy")
    total_x = rows * count_x
    omega = 1.0 / (SHEAR_Q * total_x)
    row = lax.axis_index("gx")
    is_first, is_last = row == 0, row == count_x - 1
    radial0 = (row * rows).astype(jnp.float32) + 0.5 - 0.5 * total_x
    radial0 = jnp.stack([radial0, jnp.float32(SHEAR_Q * omega)])
    weight = remap_weight.astype(jnp.float32) * WEIGHT_SCALE
    block, rest = shear_shift // width, shear_shift % width
    start = jnp.where(is_first, width - 1 - rest, rest)
    flags = jnp.stack([is_first.astype(jnp.int32), is_last.astype(jnp.int32), start.astype(jnp.int32)])
    other = 1.0 - weight
    weights = jnp.stack(
        [
            jnp.where(is_first, 1.0 - weight, 1.0 - other),
            jnp.where(is_first, weight, other),
            jnp.where(is_first, 1.0, -1.0),
        ]
    )
    full = (FIELDS, rows, high, width)
    slab = (FIELDS, 2, high, width)
    groups = rows * high // width
    turned = (FIELDS, groups, width + 2 * PAD, width)
    ends = (FIELDS, 2 * groups, width)
    sends = [ends, ends, slab] + [slab] * (1 if count_x == 2 else 2)
    start_state = call(
        prepare_kernel,
        "prepare",
        [flags, radial0],
        [density, velocity, bfield, pressure],
        [full, turned] + sends,
        [pltpu.SemaphoreType.DMA((4, groups))],
        in_hbm=True,
    )
    return sections(block, flags, weights, radial0, *start_state)


def solution(mesh):
    placed = (
        P("gx", None, "gy"),
        P(None, "gx", None, "gy"),
        P(None, "gx", None, "gy"),
        P("gx", None, "gy"),
        P(),
        P(),
    )
    return jax.shard_map(
        on_device, mesh=mesh, in_specs=placed, out_specs=P(None, "gx", None, "gy"), check_vma=False
    )
```

```python
import functools

import jax
import jax.numpy as jnp
from jax import lax
from jax.experimental import pallas as pl
from jax.experimental.pallas import tpu as pltpu
from jax.sharding import PartitionSpec as P

GAMMA = 5.0 / 3.0
SHEAR_Q = 1.5
TIME_STEP = 0.03
WEIGHT_SCALE = 1.0 / 65536.0
TINY = 1e-30
FIELDS = 8
PAD = 8


def root(x):
    return x * lax.rsqrt(jnp.maximum(x, TINY))


def side(state, normal):
    rho, pressure = state[0], state[7]
    vel, mag = state[1:4], state[4:7]
    one, two = [c for c in range(3) if c != normal]
    mom = [rho * v for v in vel]
    vn, bn = vel[normal], mag[normal]
    mn = mom[normal]
    mnvn = mn * vn
    kinetic = 0.5 * ((mnvn + mom[one] * vel[one]) + mom[two] * vel[two])
    bn2 = bn * bn
    bt2 = mag[one] * mag[one] + mag[two] * mag[two]
    half_b2 = 0.5 * (bt2 + bn2)
    inner = kinetic + 1.5 * pressure
    energy = inner + half_b2
    ind_one = vn * mag[one] - bn * vel[one]
    ind_two = vn * mag[two] - bn * vel[two]
    flux = [None] * FIELDS
    flux[0] = mn
    flux[1 + normal] = mnvn + (pressure + half_b2) - bn2
    flux[1 + one] = mn * vel[one] - bn * mag[one]
    flux[1 + two] = mn * vel[two] - bn * mag[two]
    flux[4 + one] = ind_one
    flux[4 + two] = ind_two
    flux[7] = vn * (inner + pressure) + (mag[one] * ind_one + mag[two] * ind_two)
    cons = [rho] + mom + list(mag) + [energy]
    half_gp = (0.5 * GAMMA) * pressure
    spread = half_gp - half_b2
    disc = spread * spread + (GAMMA * pressure) * bt2
    fast = (half_gp + half_b2) + root(disc)
    speed = jnp.abs(vn) + fast * lax.rsqrt(jnp.maximum(rho * fast, TINY))
    return flux, cons, speed


def face(left, right, normal):
    fl, ul, sl = side(left, normal)
    fr, ur, sr = side(right, normal)
    speed = jnp.maximum(sl, sr)
    out = []
    for f in range(FIELDS):
        jump = speed * (ur[f] - ul[f])
        out.append(-jump if fl[f] is None else (fl[f] + fr[f]) - jump)
    return out


def limited(up, down):
    return jnp.maximum(jnp.minimum(up, down), jnp.minimum(jnp.maximum(up, down), 0.0))


def to_conserved(w):
    rho = w[0]
    mom = [rho * v for v in w[1:4]]
    kinetic = 0.5 * (mom[0] * w[1] + mom[1] * w[2] + mom[2] * w[3])
    magnetic = 0.5 * (w[4] * w[4] + w[5] * w[5] + w[6] * w[6])
    return [rho] + mom + list(w[4:7]) + [1.5 * w[7] + kinetic + magnetic]


def to_primitive(u):
    inverse = 1.0 / u[0]
    vel = [m * inverse for m in u[1:4]]
    kinetic = 0.5 * (u[1] * vel[0] + u[2] * vel[1] + u[3] * vel[2])
    magnetic = 0.5 * (u[4] * u[4] + u[5] * u[5] + u[6] * u[6])
    return [u[0]] + vel + list(u[4:7]) + [(GAMMA - 1.0) * (u[7] - kinetic - magnetic)]


def lanes_of(shape):
    return lax.broadcasted_iota(jnp.int32, shape, 1)


def load_row(ref, i):
    return [ref[f, i] for f in range(FIELDS)]


def turn(w_ref, f, g, wt_ref):
    high, width = w_ref.shape[2:]
    size = width // high
    tile = w_ref[f, pl.ds(g * size, size)].reshape(width, width)
    wt_ref[f, g, PAD : PAD + width] = tile.T


def send_columns(wt_ref, cols_ref, last_ref, first_ref):
    groups, rows = wt_ref.shape[1:3]
    cells = [PAD, PAD + 1, PAD + 2, rows - PAD - 3, rows - PAD - 2, rows - PAD - 1]

    def body(f, carry):
        for k, cell in enumerate(cells):
            for g in range(groups):
                cols_ref[f, k * groups + g : k * groups + g + 1] = wt_ref[f, g, cell : cell + 1]
        first_ref[f] = cols_ref[f, 0 : 2 * groups]
        last_ref[f] = cols_ref[f, 4 * groups : 6 * groups]
        return carry

    lax.fori_loop(0, FIELDS, body, 0)


def send_rows(flags, w_ref, rows_ref, shear_ref, *swap_refs):
    rows = w_ref.shape[1]
    first = flags[0] == 1

    def copy(f, carry):
        rows_ref[f, 0:3] = w_ref[f, 0:3]
        rows_ref[f, 3:6] = w_ref[f, rows - 3 : rows]
        return carry

    lax.fori_loop(0, FIELDS, copy, 0)

    def body(k, carry):
        low, high = load_row(w_ref, k), load_row(w_ref, rows - 2 + k)
        if len(swap_refs) == 1:
            for f in range(FIELDS):
                swap_refs[0][f, k] = jnp.where(first, high[f], low[f])
        else:
            for f in range(FIELDS):
                swap_refs[0][f, k] = low[f]
                swap_refs[1][f, k] = high[f]
        outer = to_conserved([jnp.where(first, low[f], high[f]) for f in range(FIELDS)])
        for f in range(FIELDS):
            shear_ref[f, k] = outer[f]
        return carry

    lax.fori_loop(0, 2, body, 0)


def prepare_kernel(flags, radial0, rho_hbm, vel_hbm, mag_hbm, pres_hbm, w_ref, wt_ref, cols_ref, last_ref, first_ref, *rest):
    *sends, sems = rest
    rows = w_ref.shape[1]
    parts = sems.shape[1]
    size = rows // parts
    copies = []
    for part in range(parts):
        at = pl.ds(part * size, size)
        copies.append(
            [
                pltpu.make_async_copy(rho_hbm.at[at], w_ref.at[0, at], sems.at[0, part]),
                pltpu.make_async_copy(vel_hbm.at[:, at], w_ref.at[pl.ds(1, 3), at], sems.at[1, part]),
                pltpu.make_async_copy(mag_hbm.at[:, at], w_ref.at[pl.ds(4, 3), at], sems.at[2, part]),
                pltpu.make_async_copy(pres_hbm.at[at], w_ref.at[7, at], sems.at[3, part]),
            ]
        )
        for copy in copies[-1]:
            copy.start()
    for part in range(parts):
        for copy in copies[part]:
            copy.wait()
        for i in range(part * size, (part + 1) * size):
            w_ref[2, i] = w_ref[2, i] - radial0[1] * (radial0[0] + float(i))

        def turn_fields(n, carry, part=part):
            for f in range(4):
                turn(w_ref, 4 * n + f, part, wt_ref)
            return carry

        lax.fori_loop(0, FIELDS // 4, turn_fields, 0)
    send_columns(wt_ref, cols_ref, last_ref, first_ref)
    send_rows(flags, w_ref, *sends)


def three_states(cells):
    left, right = [], []
    for f in range(FIELDS):
        before, here, after = (c[f] for c in cells)
        slope = limited(0.5 * (after - here), 0.5 * (here - before))
        left.append(here + slope)
        right.append(here - slope)
    return left, right


def wrapped(ref, f, value, before, after):
    high = value.shape[0]
    ref[f, 8 : 8 + high] = value
    if before:
        ref[f, 0:8] = value[high - 8 : high]
    if after:
        ref[f, 8 + high : 16 + high] = value[0:8]


def behind(ref, f, value):
    high = value.shape[0]
    ref[f, 8 : 8 + high] = value
    result = ref[f, 7 : 7 + high]
    ref[f, 0:8] = value[high - 8 : high]
    return result


def interior_kernel(second, radial0, w_ref, wt_ref, *refs):
    if second:
        w0_ref, u1_ref = refs[:2]
        refs = refs[2:]
    v_ref, dy_ref, hz_ref, rz_ref, fz_ref, wl_ref, dx_ref, fx_ref = refs
    rows, high, width = w_ref.shape[1:]
    groups = wt_ref.shape[1]
    step = 0.5 * TIME_STEP if second else TIME_STEP
    coef = 0.5 * step
    omega_q = radial0[1]
    omega = omega_q / SHEAR_Q
    next_row, last_row = slice(9, 9 + high), slice(7, 7 + high)

    for f in range(FIELDS):
        blank = jnp.zeros((high, width), jnp.float32)
        dx_ref[f], fx_ref[f], wl_ref[f] = blank, blank, w_ref[f, 0]

    def body(i, carry):
        w = load_row(w_ref, i)
        half = [0.5 * x for x in w]

        left = []
        for f in range(FIELDS):
            wrapped(hz_ref, f, half[f], True, True)
            slope = limited(hz_ref[f, next_row] - half[f], half[f] - hz_ref[f, last_row])
            left.append(w[f] + slope)
            wrapped(rz_ref, f, w[f] - slope, False, True)
        fz = face(left, [rz_ref[f, next_row] for f in range(FIELDS)], 2)
        total = []
        for f in range(FIELDS):
            wrapped(fz_ref, f, fz[f], True, False)
            total.append(fz[f] - fz_ref[f, last_row])

        after, before = jnp.minimum(i + 1, rows - 1), jnp.maximum(i - 1, 0)
        right, wl = [], [wl_ref[f] for f in range(FIELDS)]
        for f in range(FIELDS):
            up = 0.5 * w_ref[f, after] - half[f]
            slope = limited(up, dx_ref[f])
            dx_ref[f] = up
            wl_ref[f] = w[f] + slope
            right.append(w[f] - slope)
        fx = face(wl, right, 0)
        valid = jnp.logical_and(i >= 2, i <= rows - 2)
        for f in range(FIELDS):
            here = jnp.where(valid, fx[f], 0.0)
            v_ref[f, before] = v_ref[f, before] - coef * (here - fx_ref[f])
            fx_ref[f] = here

        x = radial0[0] + i.astype(jnp.float32)
        cons = to_conserved(w)
        if second:
            base = [0.5 * (a + u1_ref[f, i]) for f, a in enumerate(to_conserved(load_row(w0_ref, i)))]
        else:
            base = cons
        tidal = 2.0 * omega * omega_q * x
        value = [base[f] - coef * total[f] for f in range(FIELDS)]
        value[1] = value[1] + ((step * 2.0) * omega * cons[2] + (step * tidal) * cons[0])
        value[2] = value[2] - ((step * 2.0) * omega) * cons[1]
        value[7] = value[7] + (step * tidal) * cons[1]
        for f in range(FIELDS):
            v_ref[f, i] = value[f]
        return carry

    lax.fori_loop(0, rows, body, 0)

    size = 16
    strips = width // size
    row = lax.broadcasted_iota(jnp.int32, (size, width), 0)

    def body_y(n, carry):
        g, start = lax.div(n, strips), size * lax.rem(n, strips)
        at = pl.multiple_of(start + PAD, 8)
        left, right = [], []
        for f in range(FIELDS):
            w = wt_ref[f, g, pl.ds(at, size)]
            up = 0.5 * (wt_ref[f, g, pl.ds(at + 1, size)] - w)
            slope = limited(up, behind(hz_ref, f, up))
            left.append(behind(rz_ref, f, w + slope))
            right.append(w - slope)
        fy = face(left, right, 1)
        cell = row + start
        valid = jnp.logical_and(cell >= 2, cell <= width - 2)
        for f in range(FIELDS):
            here = jnp.where(valid, fy[f], 0.0)
            dy_ref[f, g, pl.ds(at - 1, size)] = coef * (here - behind(fz_ref, f, here))
        return carry

    lax.fori_loop(0, groups * strips, body_y, 0)
    for f in range(FIELDS):
        for g in range(groups):
            dy_ref[f, g, PAD + width - 1 : PAD + width] = jnp.zeros((1, width), jnp.float32)


def sheared_rows(flags, weights, near_ref, next_ref, ghost_ref):
    first = flags[0] == 1
    high, width = near_ref.shape[2:]
    start = flags[2]
    back = lax.rem(width - start, width)
    lane = lanes_of((high, width))

    def body(k, carry):
        ghost = []
        for f in range(FIELDS):
            near, following = near_ref[f, k], next_ref[f, k]
            one = jnp.where(first, following, near)
            two = jnp.where(first, near, following)
            one_up, two_up = pltpu.roll(one, width - 1, 1), pltpu.roll(two, width - 1, 1)
            one = weights[0] * jnp.where(lane < width - 1, one_up, two_up) + weights[1] * one
            two = weights[0] * two_up + weights[1] * two
            ghost.append(jnp.where(lane < width - start, pltpu.roll(one, back, 1), pltpu.roll(two, back, 1)))
        delta = weights[2]
        boosted = list(ghost)
        boosted[2] = ghost[2] + ghost[0] * delta
        boosted[7] = ghost[7] + ghost[2] * delta + 0.5 * ghost[0] * delta * delta
        prim = to_primitive(boosted)
        for f in range(FIELDS):
            ghost_ref[f, k] = prim[f]
        return carry

    lax.fori_loop(0, 2, body, 0)


def edge_kernel(second, beside, flags, weights, v_ref, dy_ref, rows_ref, cols_ref, low_ref, high_ref, near_ref, next_ref, *refs):
    beside, refs = refs[:beside], refs[beside:]
    xl_ref, xr_ref = beside[0], beside[-1]
    rows, high, width = v_ref.shape[1:]
    groups = dy_ref.shape[1]
    size = rows // groups
    step = 0.5 * TIME_STEP if second else TIME_STEP
    coef = 0.5 * step
    if second:
        out_hbm, e_ref, a_ref, c_ref, x_ref, ghost_ref, out_ref, sems = refs
    else:
        w1_ref, wt1_ref, out_ref, cols1_ref, last_ref, first_ref, *sends, e_ref, a_ref, c_ref, x_ref, ghost_ref = refs
    first, last = flags[0] == 1, flags[1] == 1

    def gather(f, carry):
        for k in range(5):
            at = slice(k % 2 * groups, k % 2 * groups + groups) if k < 2 else slice((k - 2) * groups, (k - 1) * groups)
            e_ref[f, k, 0:groups] = low_ref[f, at] if k < 2 else cols_ref[f, at]
            at = slice((k + 3) * groups, (k + 4) * groups) if k < 3 else slice((k - 3) * groups, (k - 2) * groups)
            e_ref[f, k, groups : 2 * groups] = cols_ref[f, at] if k < 3 else high_ref[f, at]
        return carry

    lax.fori_loop(0, FIELDS, gather, 0)
    cells = [[e_ref[f, k] for f in range(FIELDS)] for k in range(5)]
    sides = [three_states(cells[k : k + 3]) for k in range(3)]
    one = face(sides[0][0], sides[1][1], 1)
    two = face(sides[1][0], sides[2][1], 1)
    low_end = lax.broadcasted_iota(jnp.int32, one[0].shape, 0) < groups
    for f in range(FIELDS):
        a_ref[f, 0] = coef * (two[f] - one[f])
        a_ref[f, 1] = coef * jnp.where(low_end, -two[f], one[f])

    def scatter(f, carry):
        for g in range(groups):
            c_ref[f, g] = jnp.zeros((2 * PAD, width), jnp.float32)
            c_ref[f, g, 0:1] = a_ref[f, 0, g : g + 1]
            c_ref[f, g, 1:2] = a_ref[f, 1, g : g + 1]
            c_ref[f, g, 2 * PAD - 2 : 2 * PAD - 1] = a_ref[f, 1, groups + g : groups + g + 1]
            c_ref[f, g, 2 * PAD - 1 : 2 * PAD] = a_ref[f, 0, groups + g : groups + g + 1]
        return carry

    lax.fori_loop(0, FIELDS, scatter, 0)

    sheared_rows(flags, weights, near_ref, next_ref, ghost_ref)
    def place(f, carry):
        x_ref[0, f, 0:2] = jnp.where(first, ghost_ref[f], xl_ref[f])
        x_ref[1, f, 3:5] = jnp.where(last, ghost_ref[f], xr_ref[f])
        x_ref[0, f, 2:5] = rows_ref[f, 0:3]
        x_ref[1, f, 0:3] = rows_ref[f, 3:6]
        return carry

    lax.fori_loop(0, FIELDS, place, 0)

    def radial(n, carry):
        end = lax.div(n, 2)
        at = pl.ds(pl.multiple_of(lax.rem(n, 2) * (high // 2), 8), high // 2)
        cells = [[x_ref[end, f, k, at] for f in range(FIELDS)] for k in range(5)]
        sides = [three_states(cells[k : k + 3]) for k in range(3)]
        one = face(sides[0][0], sides[1][1], 0)
        two = face(sides[1][0], sides[2][1], 0)
        for f in range(FIELDS):
            x_ref[end, f, 0, at] = coef * (two[f] - one[f])
            x_ref[end, f, 1, at] = coef * jnp.where(end == 0, -two[f], one[f])
        return carry

    lax.fori_loop(0, 4, radial, 0)
    batch = FIELDS // 2

    def finish(n, carry):
        g = lax.div(n, 2)
        at = pl.ds(g * size, size)
        fields = [lax.rem(n, 2) * batch + f for f in range(batch)]
        for f in fields:
            head = dy_ref[f, g, PAD : 2 * PAD] + c_ref[f, g, 0:PAD]
            tail = dy_ref[f, g, width : PAD + width] + c_ref[f, g, PAD : 2 * PAD]
            strip = jnp.concatenate([head, dy_ref[f, g, 2 * PAD : width], tail], axis=0)
            out_ref[f, at] = v_ref[f, at] - strip.T.reshape(size, high, width)

        @pl.when(g == 0)
        def _():
            for f in fields:
                out_ref[f, 0] = out_ref[f, 0] - x_ref[0, f, 0]
                out_ref[f, 1] = out_ref[f, 1] - x_ref[0, f, 1]

        @pl.when(g == groups - 1)
        def _():
            for f in fields:
                out_ref[f, rows - 1] = out_ref[f, rows - 1] - x_ref[1, f, 0]
                out_ref[f, rows - 2] = out_ref[f, rows - 2] - x_ref[1, f, 1]

        if second:
            part = pl.ds(fields[0], batch)
            pltpu.make_async_copy(out_ref.at[part, at], out_hbm.at[part, at], sems.at[n]).start()
        return carry

    lax.fori_loop(0, 2 * groups, finish, 0)
    if second:
        for n in range(2 * groups):
            at, part = pl.ds(n // 2 * size, size), pl.ds(n % 2 * batch, batch)
            pltpu.make_async_copy(out_ref.at[part, at], out_hbm.at[part, at], sems.at[n]).wait()
        return

    def primitives(i, carry):
        prim = to_primitive(load_row(out_ref, i))
        for f in range(FIELDS):
            w1_ref[f, i] = prim[f]
        return carry

    lax.fori_loop(0, rows, primitives, 0, unroll=4)

    def turn_group(n, carry):
        for f in range(batch):
            turn(w1_ref, lax.rem(n, 2) * batch + f, lax.div(n, 2), wt1_ref)
        return carry

    lax.fori_loop(0, 2 * groups, turn_group, 0)
    send_columns(wt1_ref, cols1_ref, last_ref, first_ref)
    send_rows(flags, w1_ref, *sends)


def call(kernel, name, scalars, arrays, shapes, scratch=(), in_hbm=False, out_hbm=False):
    smem = pl.BlockSpec(memory_space=pltpu.SMEM)
    vmem = pl.BlockSpec(memory_space=pltpu.VMEM)
    hbm = pl.BlockSpec(memory_space=pltpu.HBM)
    if in_hbm:
        arrays = [pltpu.with_memory_space_constraint(x, pltpu.HBM) for x in arrays]
    return pl.pallas_call(
        kernel,
        name=name,
        out_shape=[jax.ShapeDtypeStruct(s, jnp.float32) for s in shapes],
        in_specs=[smem] * len(scalars) + [hbm if in_hbm else vmem] * len(arrays),
        out_specs=[hbm if out_hbm else vmem] * len(shapes),
        scratch_shapes=[pltpu.VMEM(s, jnp.float32) if isinstance(s, tuple) else s for s in scratch],
        compiler_params=pltpu.CompilerParams(vmem_limit_bytes=20 * 1024 * 1024),
    )(*scalars, *arrays)


def exchange(last, first, swap):
    count_x, count_y = lax.axis_size("gx"), lax.axis_size("gy")
    low = lax.ppermute(last, "gy", [(i, (i + 1) % count_y) for i in range(count_y)])
    high = lax.ppermute(first, "gy", [((i + 1) % count_y, i) for i in range(count_y)])
    if len(swap) == 1:
        return low, high, lax.ppermute(swap[0], "gx", [(0, 1), (1, 0)])
    x_low = lax.ppermute(swap[1], "gx", [(i, i + 1) for i in range(count_x - 1)])
    x_high = lax.ppermute(swap[0], "gx", [(i + 1, i) for i in range(count_x - 1)])
    return low, high, x_low, x_high


def crossing(by, shear):
    count_x, count_y = lax.axis_size("gx"), lax.axis_size("gy")
    last = (count_x - 1) * count_y
    pairs = []
    for gy in range(count_y):
        pairs.append((last + gy, (gy + by) % count_y))
        pairs.append((gy, last + (gy - by) % count_y))
    return lax.ppermute(shear, ("gx", "gy"), pairs)


def inner_scratch(full):
    high, width = full[2:]
    tile = (FIELDS, high, width)
    padded = (FIELDS, high + 2 * PAD, width)
    return [padded, padded, padded, tile, tile, tile]


def edge_scratch(full, groups):
    high, width = full[2:]
    return [
        (FIELDS, 5, 2 * groups, width),
        (FIELDS, 2, 2 * groups, width),
        (FIELDS, groups, 2 * PAD, width),
        (2, FIELDS, 5, high, width),
        (FIELDS, 2, high, width),
    ]


def sections(block, flags, weights, radial0, w0, wt0, cols, last, first, rows, shear, *swap):
    full, turned = w0.shape, wt0.shape
    groups = turned[1]
    sends = [x.shape for x in (cols, last, first, rows, shear, *swap)]
    scratch = edge_scratch(full, groups)

    def branch(by):
        def run(flags, weights, radial0, w0, wt0, cols, last, first, rows, shear, *swap):
            low, high, *beside = exchange(last, first, swap)
            sheared = crossing(by, shear), crossing(by + 1, shear)
            kernel = functools.partial(interior_kernel, False)
            v, dy = call(kernel, "inner_1", [radial0], [w0, wt0], [full, turned], inner_scratch(full))
            w1, wt1, u1, cols, last, first, rows, shear, *swap = call(
                functools.partial(edge_kernel, False, len(beside)),
                "edge_1",
                [flags, weights],
                [v, dy, rows, cols, low, high, *sheared, *beside],
                [full, turned, full] + sends,
                scratch,
            )
            low, high, *beside = exchange(last, first, swap)
            sheared = crossing(by, shear), crossing(by + 1, shear)
            kernel = functools.partial(interior_kernel, True)
            v, dy = call(kernel, "inner_2", [radial0], [w1, wt1, w0, u1], [full, turned], inner_scratch(full))
            return v, dy, rows, cols, low, high, *sheared, *beside

        return run

    branches = [branch(by) for by in range(lax.axis_size("gy"))]
    arrays = lax.switch(
        block, branches, flags, weights, radial0, w0, wt0, cols, last, first, rows, shear, *swap
    )
    (out,) = call(
        functools.partial(edge_kernel, True, 1 if lax.axis_size("gx") == 2 else 2),
        "edge_2",
        [flags, weights],
        arrays,
        [full],
        scratch + [full, pltpu.SemaphoreType.DMA((2 * groups,))],
        out_hbm=True,
    )
    return out


def on_device(density, velocity, bfield, pressure, shear_shift, remap_weight):
    rows, high, width = density.shape
    count_x, count_y = lax.axis_size("gx"), lax.axis_size("gy")
    total_x = rows * count_x
    omega = 1.0 / (SHEAR_Q * total_x)
    row = lax.axis_index("gx")
    is_first, is_last = row == 0, row == count_x - 1
    radial0 = (row * rows).astype(jnp.float32) + 0.5 - 0.5 * total_x
    radial0 = jnp.stack([radial0, jnp.float32(SHEAR_Q * omega)])
    weight = remap_weight.astype(jnp.float32) * WEIGHT_SCALE
    block, rest = shear_shift // width, shear_shift % width
    start = jnp.where(is_first, width - 1 - rest, rest)
    flags = jnp.stack([is_first.astype(jnp.int32), is_last.astype(jnp.int32), start.astype(jnp.int32)])
    other = 1.0 - weight
    weights = jnp.stack(
        [
            jnp.where(is_first, 1.0 - weight, 1.0 - other),
            jnp.where(is_first, weight, other),
            jnp.where(is_first, 1.0, -1.0),
        ]
    )
    full = (FIELDS, rows, high, width)
    slab = (FIELDS, 2, high, width)
    groups = rows * high // width
    turned = (FIELDS, groups, width + 2 * PAD, width)
    ends = (FIELDS, 2 * groups, width)
    sends = [(FIELDS, 6 * groups, width), ends, ends, (FIELDS, 6, high, width)]
    sends += [slab] * (2 if count_x == 2 else 3)
    start_state = call(
        prepare_kernel,
        "prepare",
        [flags, radial0],
        [density, velocity, bfield, pressure],
        [full, turned] + sends,
        [pltpu.SemaphoreType.DMA((4, groups))],
        in_hbm=True,
    )
    return sections(block, flags, weights, radial0, *start_state)


def solution(mesh):
    placed = (
        P("gx", None, "gy"),
        P(None, "gx", None, "gy"),
        P(None, "gx", None, "gy"),
        P("gx", None, "gy"),
        P(),
        P(),
    )
    return jax.shard_map(
        on_device, mesh=mesh, in_specs=placed, out_specs=P(None, "gx", None, "gy"), check_vma=False
    )
```

```python
import functools

import jax
import jax.numpy as jnp
from jax import lax
from jax.experimental import pallas as pl
from jax.experimental.pallas import tpu as pltpu
from jax.sharding import PartitionSpec as P

GAMMA = 5.0 / 3.0
SHEAR_Q = 1.5
TIME_STEP = 0.03
WEIGHT_SCALE = 1.0 / 65536.0
TINY = 1e-30
FIELDS = 8
PAD = 8


def root(x):
    return x * lax.rsqrt(jnp.maximum(x, TINY))


def side(state, normal):
    rho, pressure = state[0], state[7]
    vel, mag = state[1:4], state[4:7]
    one, two = [c for c in range(3) if c != normal]
    mom = [rho * v for v in vel]
    vn, bn = vel[normal], mag[normal]
    mn = mom[normal]
    mnvn = mn * vn
    kinetic = 0.5 * ((mnvn + mom[one] * vel[one]) + mom[two] * vel[two])
    bn2 = bn * bn
    bt2 = mag[one] * mag[one] + mag[two] * mag[two]
    half_b2 = 0.5 * (bt2 + bn2)
    inner = kinetic + 1.5 * pressure
    energy = inner + half_b2
    ind_one = vn * mag[one] - bn * vel[one]
    ind_two = vn * mag[two] - bn * vel[two]
    flux = [None] * FIELDS
    flux[0] = mn
    flux[1 + normal] = mnvn + (pressure + half_b2) - bn2
    flux[1 + one] = mn * vel[one] - bn * mag[one]
    flux[1 + two] = mn * vel[two] - bn * mag[two]
    flux[4 + one] = ind_one
    flux[4 + two] = ind_two
    flux[7] = vn * (inner + pressure) + (mag[one] * ind_one + mag[two] * ind_two)
    cons = [rho] + mom + list(mag) + [energy]
    half_gp = (0.5 * GAMMA) * pressure
    spread = half_gp - half_b2
    disc = spread * spread + (GAMMA * pressure) * bt2
    fast = (half_gp + half_b2) + root(disc)
    speed = jnp.abs(vn) + fast * lax.rsqrt(jnp.maximum(rho * fast, TINY))
    return flux, cons, speed


def face(left, right, normal):
    fl, ul, sl = side(left, normal)
    fr, ur, sr = side(right, normal)
    speed = jnp.maximum(sl, sr)
    out = []
    for f in range(FIELDS):
        if fl[f] is None:
            out.append(speed * (ul[f] - ur[f]))
        else:
            out.append((fl[f] + fr[f]) - speed * (ur[f] - ul[f]))
    return out


def limited(up, down):
    return jnp.maximum(jnp.minimum(up, down), jnp.minimum(jnp.maximum(up, down), 0.0))


def to_conserved(w):
    rho = w[0]
    mom = [rho * v for v in w[1:4]]
    kinetic = 0.5 * (mom[0] * w[1] + mom[1] * w[2] + mom[2] * w[3])
    magnetic = 0.5 * (w[4] * w[4] + w[5] * w[5] + w[6] * w[6])
    return [rho] + mom + list(w[4:7]) + [1.5 * w[7] + kinetic + magnetic]


def to_primitive(u):
    inverse = 1.0 / u[0]
    vel = [m * inverse for m in u[1:4]]
    kinetic = 0.5 * (u[1] * vel[0] + u[2] * vel[1] + u[3] * vel[2])
    magnetic = 0.5 * (u[4] * u[4] + u[5] * u[5] + u[6] * u[6])
    return [u[0]] + vel + list(u[4:7]) + [(GAMMA - 1.0) * (u[7] - kinetic - magnetic)]


def lanes_of(shape):
    return lax.broadcasted_iota(jnp.int32, shape, 1)


def load_row(ref, i):
    return [ref[f, i] for f in range(FIELDS)]


def turn(w_ref, f, g, wt_ref):
    high, width = w_ref.shape[2:]
    size = width // high
    tile = w_ref[f, pl.ds(g * size, size)].reshape(width, width)
    wt_ref[f, g, PAD : PAD + width] = tile.T


def pad_ends(wt_ref, f, g):
    rows = wt_ref.shape[2]
    wt_ref[f, g, 0:PAD] = wt_ref[f, g, PAD : 2 * PAD]
    wt_ref[f, g, rows - PAD : rows] = wt_ref[f, g, rows - 2 * PAD : rows - PAD]


def send_columns(flags, groups, wt_ref, cols_ref, even_ref, odd_ref):
    rows = wt_ref.shape[2]
    even = flags[3] == 1
    cells = [PAD, PAD + 1, PAD + 2, rows - PAD - 3, rows - PAD - 2, rows - PAD - 1]

    def body(f, carry):
        for g in range(groups):
            for k, cell in enumerate(cells):
                cols_ref[f, k * groups + g : k * groups + g + 1] = wt_ref[f, g, cell : cell + 1]
            pad_ends(wt_ref, f, g)
        first, last = cols_ref[f, 0 : 2 * groups], cols_ref[f, 4 * groups : 6 * groups]
        even_ref[f] = jnp.where(even, last, first)
        odd_ref[f] = jnp.where(even, first, last)
        return carry

    lax.fori_loop(0, FIELDS, body, 0)


def send_rows(flags, rows_ref, shear_ref, *swap_refs):
    first = flags[0] == 1

    def body(k, carry):
        low, high = load_row(rows_ref, k), load_row(rows_ref, 4 + k)
        if len(swap_refs) == 1:
            for f in range(FIELDS):
                swap_refs[0][f, k] = jnp.where(first, high[f], low[f])
        else:
            for f in range(FIELDS):
                swap_refs[0][f, k] = low[f]
                swap_refs[1][f, k] = high[f]
        outer = to_conserved([jnp.where(first, low[f], high[f]) for f in range(FIELDS)])
        for f in range(FIELDS):
            shear_ref[f, k] = outer[f]
        return carry

    lax.fori_loop(0, 2, body, 0)


def prepare_kernel(flags, radial0, rho_hbm, vel_hbm, mag_hbm, pres_hbm, w_ref, wt_ref, cols_ref, even_ref, odd_ref, rows_ref, *rest):
    *sends, sems = rest
    rows = w_ref.shape[1]
    parts = sems.shape[1]
    size = rows // parts
    copies = []
    for part in range(parts):
        at = pl.ds(part * size, size)
        copies.append(
            [
                pltpu.make_async_copy(rho_hbm.at[at], w_ref.at[0, at], sems.at[0, part]),
                pltpu.make_async_copy(vel_hbm.at[:, at], w_ref.at[pl.ds(1, 3), at], sems.at[1, part]),
                pltpu.make_async_copy(mag_hbm.at[:, at], w_ref.at[pl.ds(4, 3), at], sems.at[2, part]),
                pltpu.make_async_copy(pres_hbm.at[at], w_ref.at[7, at], sems.at[3, part]),
            ]
        )
        for copy in copies[-1]:
            copy.start()
    for part in range(parts):
        for copy in copies[part]:
            copy.wait()
        for i in range(part * size, (part + 1) * size):
            w_ref[2, i] = w_ref[2, i] - radial0[1] * (radial0[0] + float(i))

        def turn_fields(n, carry, part=part):
            for f in range(4):
                turn(w_ref, 4 * n + f, part, wt_ref)
            return carry

        lax.fori_loop(0, FIELDS // 4, turn_fields, 0)
    send_columns(flags, parts, wt_ref, cols_ref, even_ref, odd_ref)

    def copy(f, carry):
        rows_ref[f, 0:3] = w_ref[f, 0:3]
        rows_ref[f, 3:6] = w_ref[f, rows - 3 : rows]
        return carry

    lax.fori_loop(0, FIELDS, copy, 0)
    send_rows(flags, rows_ref, *sends)


def three_states(cells):
    left, right = [], []
    for f in range(FIELDS):
        before, here, after = (c[f] for c in cells)
        slope = limited(0.5 * (after - here), 0.5 * (here - before))
        left.append(here + slope)
        right.append(here - slope)
    return left, right


def wrapped(ref, f, value, before, after):
    high = value.shape[0]
    ref[f, 8 : 8 + high] = value
    if before:
        ref[f, 0:8] = value[high - 8 : high]
    if after:
        ref[f, 8 + high : 16 + high] = value[0:8]


def behind(ref, f, value):
    high = value.shape[0]
    ref[f, 8 : 8 + high] = value
    result = ref[f, 7 : 7 + high]
    ref[f, 0:8] = value[high - 8 : high]
    return result


def interior_kernel(second, radial0, *refs):
    if second:
        wt_ref, w0_ref, v_ref, dy_ref, w_ref, *refs = refs
    else:
        w_ref, wt_ref, vt_ref, v_ref, *refs = refs
        dy_ref = vt_ref
    hz_ref, rz_ref, fz_ref, wl_ref, dx_ref, fx_ref = refs
    rows, high, width = w_ref.shape[1:]
    per_group = width // high
    groups = rows // per_group
    step = 0.5 * TIME_STEP if second else TIME_STEP
    coef = 0.5 * step
    omega_q = radial0[1]
    omega = omega_q / SHEAR_Q
    next_row, last_row = slice(9, 9 + high), slice(7, 7 + high)
    early = per_group + 1

    def turn_result(m):
        g, f = lax.div(m, FIELDS), lax.rem(m, FIELDS)
        tile = v_ref[f, pl.ds(jnp.minimum(g, groups - 1) * per_group, per_group)].reshape(width, width)
        vt_ref[f, jnp.minimum(g, groups), PAD : PAD + width] = tile.T

    def turn_state(m):
        g, f = lax.div(m, FIELDS), lax.rem(m, FIELDS)
        tile = wt_ref[f, g, PAD : PAD + width].T
        w_ref[f, pl.ds(g * per_group, per_group)] = tile.reshape(per_group, high, width)

    def body(i, carry):
        if not second:
            turn_result(jnp.maximum(i - early, 0))
        w = load_row(w_ref, i)
        half = [0.5 * x for x in w]

        left = []
        for f in range(FIELDS):
            wrapped(hz_ref, f, half[f], True, True)
            slope = limited(hz_ref[f, next_row] - half[f], half[f] - hz_ref[f, last_row])
            left.append(w[f] + slope)
            wrapped(rz_ref, f, w[f] - slope, False, True)
        fz = face(left, [rz_ref[f, next_row] for f in range(FIELDS)], 2)
        total = []
        for f in range(FIELDS):
            wrapped(fz_ref, f, fz[f], True, False)
            total.append(fz[f] - fz_ref[f, last_row])

        after, before = jnp.minimum(i + 1, rows - 1), jnp.maximum(i - 1, 0)
        right, wl = [], [wl_ref[f] for f in range(FIELDS)]
        for f in range(FIELDS):
            up = 0.5 * w_ref[f, after] - half[f]
            slope = limited(up, dx_ref[f])
            dx_ref[f] = up
            wl_ref[f] = w[f] + slope
            right.append(w[f] - slope)
        fx = face(wl, right, 0)
        scale = jnp.where(jnp.logical_and(i >= 2, i <= rows - 2), coef, 0.0)
        for f in range(FIELDS):
            here = scale * fx[f]
            v_ref[f, before] = v_ref[f, before] - (here - fx_ref[f])
            fx_ref[f] = here

        x = radial0[0] + i.astype(jnp.float32)
        cons = to_conserved(w)
        if second:
            base = [0.5 * (a + b) for a, b in zip(to_conserved(load_row(w0_ref, i)), cons)]
        else:
            base = cons
        tidal = 2.0 * omega * omega_q * x
        value = [base[f] - coef * total[f] for f in range(FIELDS)]
        value[1] = value[1] + ((step * 2.0) * omega * cons[2] + (step * tidal) * cons[0])
        value[2] = value[2] - ((step * 2.0) * omega) * cons[1]
        value[7] = value[7] + (step * tidal) * cons[1]
        for f in range(FIELDS):
            v_ref[f, i] = value[f]
        return carry

    size = groups * width // rows
    strips = width // size
    row = lax.broadcasted_iota(jnp.int32, (size, width), 0)

    def body_y(n, carry):
        if second:
            turn_state(n)
        else:
            turn_result(rows - early + n)
        g, start = lax.div(n, strips), size * lax.rem(n, strips)
        at = pl.multiple_of(start + PAD, 8)
        left, right = [], []
        for f in range(FIELDS):
            w = wt_ref[f, g, pl.ds(at, size)]
            up = 0.5 * (wt_ref[f, g, pl.ds(at + 1, size)] - w)
            slope = limited(up, behind(hz_ref, f, up))
            left.append(behind(rz_ref, f, w + slope))
            right.append(w - slope)
        fy = face(left, right, 1)
        cell = row + start
        scale = jnp.where(jnp.logical_and(cell >= 2, cell <= width - 2), coef, 0.0)
        for f in range(FIELDS):
            here = scale * fy[f]
            change = here - behind(fz_ref, f, here)
            if second:
                dy_ref[f, g, pl.ds(at - 1, size)] = change
            else:
                vt_ref[f, g, pl.ds(at - 1, size)] = vt_ref[f, g, pl.ds(at - 1, size)] - change
        return carry

    def azimuthal():
        for f in range(FIELDS):
            hz_ref[f, 0:8] = jnp.zeros((8, width), jnp.float32)
            rz_ref[f, 0:8] = wt_ref[f, 0, PAD : 2 * PAD]
            fz_ref[f, 0:8] = jnp.zeros((8, width), jnp.float32)
        lax.fori_loop(0, rows, body_y, 0)

    def others():
        for f in range(FIELDS):
            blank = jnp.zeros((high, width), jnp.float32)
            dx_ref[f], fx_ref[f], wl_ref[f] = blank, blank, w_ref[f, 0]
        lax.fori_loop(0, rows, body, 0)

    if second:
        azimuthal()
        others()
        for f in range(FIELDS):
            for g in range(groups):
                dy_ref[f, g, PAD + width - 1 : PAD + width] = jnp.zeros((1, width), jnp.float32)
    else:
        others()
        azimuthal()


def sheared_rows(flags, weights, near_ref, next_ref, ghost_ref):
    first = flags[0] == 1
    high, width = near_ref.shape[2:]
    start = flags[2]
    back = lax.rem(width - start, width)
    lane = lanes_of((high, width))

    def body(k, carry):
        ghost = []
        for f in range(FIELDS):
            near, following = near_ref[f, k], next_ref[f, k]
            one = jnp.where(first, following, near)
            two = jnp.where(first, near, following)
            one_up, two_up = pltpu.roll(one, width - 1, 1), pltpu.roll(two, width - 1, 1)
            one = weights[0] * jnp.where(lane < width - 1, one_up, two_up) + weights[1] * one
            two = weights[0] * two_up + weights[1] * two
            ghost.append(jnp.where(lane < width - start, pltpu.roll(one, back, 1), pltpu.roll(two, back, 1)))
        delta = weights[2]
        boosted = list(ghost)
        boosted[2] = ghost[2] + ghost[0] * delta
        boosted[7] = ghost[7] + ghost[2] * delta + 0.5 * ghost[0] * delta * delta
        prim = to_primitive(boosted)
        for f in range(FIELDS):
            ghost_ref[f, k] = prim[f]
        return carry

    lax.fori_loop(0, 2, body, 0)


def edge_kernel(second, beside, flags, weights, *refs):
    if second:
        v_ref, dy_ref, *refs = refs
    else:
        vt_ref, *refs = refs
    rows_ref, cols_ref, even_ref, odd_ref, near_ref, next_ref, *refs = refs
    xl_ref, xr_ref = refs[0], refs[beside - 1]
    if second:
        out_hbm, e_ref, a_ref, c_ref, x_ref, ghost_ref, out_ref, sems = refs[beside:]
    else:
        w1_ref, cols1_ref, even1_ref, odd1_ref, rows1_ref, *sends, e_ref, a_ref, c_ref, x_ref, ghost_ref = refs[beside:]
    high, width = rows_ref.shape[2:]
    groups = cols_ref.shape[1] // 6
    size = width // high
    rows = groups * size
    step = 0.5 * TIME_STEP if second else TIME_STEP
    coef = 0.5 * step
    first, last, even = flags[0] == 1, flags[1] == 1, flags[3] == 1

    def gather(f, carry):
        for k in range(2):
            at = slice(k * groups, (k + 1) * groups)
            e_ref[f, k, 0:groups] = jnp.where(even, odd_ref[f, at], even_ref[f, at])
            e_ref[f, 3 + k, groups : 2 * groups] = jnp.where(even, even_ref[f, at], odd_ref[f, at])
        for k in range(3):
            e_ref[f, 2 + k, 0:groups] = cols_ref[f, k * groups : (k + 1) * groups]
            e_ref[f, k, groups : 2 * groups] = cols_ref[f, (3 + k) * groups : (4 + k) * groups]
        return carry

    lax.fori_loop(0, FIELDS, gather, 0)
    cells = [[e_ref[f, k] for f in range(FIELDS)] for k in range(5)]
    sides = [three_states(cells[k : k + 3]) for k in range(3)]
    one = face(sides[0][0], sides[1][1], 1)
    two = face(sides[1][0], sides[2][1], 1)
    low_end = lax.broadcasted_iota(jnp.int32, one[0].shape, 0) < groups
    for f in range(FIELDS):
        a_ref[f, 0] = coef * (two[f] - one[f])
        a_ref[f, 1] = coef * jnp.where(low_end, -two[f], one[f])

    if second:

        def scatter(f, carry):
            for g in range(groups):
                c_ref[f, g] = jnp.zeros((2 * PAD, width), jnp.float32)
                c_ref[f, g, 0:1] = a_ref[f, 0, g : g + 1]
                c_ref[f, g, 1:2] = a_ref[f, 1, g : g + 1]
                c_ref[f, g, 2 * PAD - 2 : 2 * PAD - 1] = a_ref[f, 1, groups + g : groups + g + 1]
                c_ref[f, g, 2 * PAD - 1 : 2 * PAD] = a_ref[f, 0, groups + g : groups + g + 1]
            return carry

        lax.fori_loop(0, FIELDS, scatter, 0)

    sheared_rows(flags, weights, near_ref, next_ref, ghost_ref)
    def place(f, carry):
        x_ref[0, f, 0:2] = jnp.where(first, ghost_ref[f], xl_ref[f])
        x_ref[1, f, 3:5] = jnp.where(last, ghost_ref[f], xr_ref[f])
        x_ref[0, f, 2:5] = rows_ref[f, 0:3]
        x_ref[1, f, 0:3] = rows_ref[f, 3:6]
        return carry

    lax.fori_loop(0, FIELDS, place, 0)

    def radial(n, carry):
        end = lax.div(n, 2)
        at = pl.ds(pl.multiple_of(lax.rem(n, 2) * (high // 2), 8), high // 2)
        cells = [[x_ref[end, f, k, at] for f in range(FIELDS)] for k in range(5)]
        sides = [three_states(cells[k : k + 3]) for k in range(3)]
        one = face(sides[0][0], sides[1][1], 0)
        two = face(sides[1][0], sides[2][1], 0)
        for f in range(FIELDS):
            x_ref[end, f, 0, at] = coef * (two[f] - one[f])
            x_ref[end, f, 1, at] = coef * jnp.where(end == 0, -two[f], one[f])
        return carry

    lax.fori_loop(0, 4, radial, 0)
    batch = FIELDS // 2

    if not second:
        lane = lanes_of((width, width))

        def correct(n, carry):
            for k in range(batch):
                f = n * batch + k
                strip = [x_ref[0, f, 0], x_ref[0, f, 1], jnp.zeros((width - 4 * high, width), jnp.float32)]
                strip = jnp.concatenate(strip + [x_ref[1, f, 1], x_ref[1, f, 0]], axis=0).T
                at = slice(PAD, PAD + width)
                w1_ref[f, 0, at] = vt_ref[f, 0, at] - jnp.where(lane < width // 2, strip, 0.0)
                w1_ref[f, groups - 1, at] = vt_ref[f, groups - 1, at] - jnp.where(lane < width // 2, 0.0, strip)
            return carry

        lax.fori_loop(0, FIELDS // batch, correct, 0)

        def correct_rows(f, carry):
            for g in range(groups):
                places = [(0, 0, g), (1, 1, g), (width - 2, 1, groups + g), (width - 1, 0, groups + g)]
                for to, kind, at in places:
                    to = slice(PAD + to, PAD + to + 1)
                    w1_ref[f, g, to] = w1_ref[f, g, to] - a_ref[f, kind, at : at + 1]
            return carry

        lax.fori_loop(0, FIELDS, correct_rows, 0)
        strips = width // 16

        def primitives(n, carry):
            g, at = lax.div(n, strips), pl.ds(pl.multiple_of(PAD + 16 * lax.rem(n, strips), 8), 16)
            prim = to_primitive([w1_ref[f, g, at] for f in range(FIELDS)])
            for f in range(FIELDS):
                w1_ref[f, g, at] = prim[f]
            return carry

        lax.fori_loop(0, groups * strips, primitives, 0, unroll=4)

        def turn_rows(n, carry):
            for k in range(batch):
                f = n * batch + k
                at = slice(PAD, PAD + width)
                strip = jnp.where(lane < width // 2, w1_ref[f, 0, at], w1_ref[f, groups - 1, at]).T
                rows1_ref[f, 0:3] = strip[0 : 3 * high].reshape(3, high, width)
                rows1_ref[f, 3:6] = strip[width - 3 * high : width].reshape(3, high, width)
            return carry

        lax.fori_loop(0, FIELDS // batch, turn_rows, 0)
        send_columns(flags, groups, w1_ref, cols1_ref, even1_ref, odd1_ref)
        send_rows(flags, rows1_ref, *sends)
        return

    def finish(n, carry):
        g = lax.div(n, 2)
        at = pl.ds(g * size, size)
        fields = [lax.rem(n, 2) * batch + f for f in range(batch)]
        for f in fields:
            head = dy_ref[f, g, PAD : 2 * PAD] + c_ref[f, g, 0:PAD]
            tail = dy_ref[f, g, width : PAD + width] + c_ref[f, g, PAD : 2 * PAD]
            strip = jnp.concatenate([head, dy_ref[f, g, 2 * PAD : width], tail], axis=0)
            out_ref[f, at] = v_ref[f, at] - strip.T.reshape(size, high, width)

        @pl.when(g == 0)
        def _():
            for f in fields:
                out_ref[f, 0] = out_ref[f, 0] - x_ref[0, f, 0]
                out_ref[f, 1] = out_ref[f, 1] - x_ref[0, f, 1]

        @pl.when(g == groups - 1)
        def _():
            for f in fields:
                out_ref[f, rows - 1] = out_ref[f, rows - 1] - x_ref[1, f, 0]
                out_ref[f, rows - 2] = out_ref[f, rows - 2] - x_ref[1, f, 1]

        part = pl.ds(fields[0], batch)
        pltpu.make_async_copy(out_ref.at[part, at], out_hbm.at[part, at], sems.at[n]).start()
        return carry

    lax.fori_loop(0, 2 * groups, finish, 0)
    for n in range(2 * groups):
        at, part = pl.ds(n // 2 * size, size), pl.ds(n % 2 * batch, batch)
        pltpu.make_async_copy(out_ref.at[part, at], out_hbm.at[part, at], sems.at[n]).wait()


def call(kernel, name, scalars, arrays, shapes, scratch=(), in_hbm=False, out_hbm=False, aliases=None):
    smem = pl.BlockSpec(memory_space=pltpu.SMEM)
    vmem = pl.BlockSpec(memory_space=pltpu.VMEM)
    hbm = pl.BlockSpec(memory_space=pltpu.HBM)
    if in_hbm:
        arrays = [pltpu.with_memory_space_constraint(x, pltpu.HBM) for x in arrays]
    return pl.pallas_call(
        kernel,
        name=name,
        out_shape=[jax.ShapeDtypeStruct(s, jnp.float32) for s in shapes],
        in_specs=[smem] * len(scalars) + [hbm if in_hbm else vmem] * len(arrays),
        out_specs=[hbm if out_hbm else vmem] * len(shapes),
        scratch_shapes=[pltpu.VMEM(s, jnp.float32) if isinstance(s, tuple) else s for s in scratch],
        input_output_aliases=aliases or {},
        compiler_params=pltpu.CompilerParams(vmem_limit_bytes=20 * 1024 * 1024),
    )(*scalars, *arrays)


def exchange(even, odd, swap):
    count_x, count_y = lax.axis_size("gx"), lax.axis_size("gy")

    def pairs(start):
        ends = [(i, (i + 1) % count_y) for i in range(start, count_y, 2)]
        return ends + [(j, i) for i, j in ends]

    even, odd = lax.ppermute(even, "gy", pairs(0)), lax.ppermute(odd, "gy", pairs(1))
    if len(swap) == 1:
        return even, odd, lax.ppermute(swap[0], "gx", [(0, 1), (1, 0)])
    x_low = lax.ppermute(swap[1], "gx", [(i, i + 1) for i in range(count_x - 1)])
    x_high = lax.ppermute(swap[0], "gx", [(i + 1, i) for i in range(count_x - 1)])
    return even, odd, x_low, x_high


def crossing(by, shear):
    count_x, count_y = lax.axis_size("gx"), lax.axis_size("gy")
    last = (count_x - 1) * count_y
    pairs = []
    for gy in range(count_y):
        pairs.append((last + gy, (gy + by) % count_y))
        pairs.append((gy, last + (gy - by) % count_y))
    return lax.ppermute(shear, ("gx", "gy"), pairs)


def inner_scratch(full):
    high, width = full[2:]
    tile = (FIELDS, high, width)
    padded = (FIELDS, high + 2 * PAD, width)
    return [padded, padded, padded, tile, tile, tile]


def edge_scratch(full, groups):
    high, width = full[2:]
    return [
        (FIELDS, 5, 2 * groups, width),
        (FIELDS, 2, 2 * groups, width),
        (FIELDS, groups, 2 * PAD, width),
        (2, FIELDS, 5, high, width),
        (FIELDS, 2, high, width),
    ]


def sections(block, flags, weights, radial0, w0, wt0, cols, even, odd, rows, shear, *swap):
    full, turned = w0.shape, wt0.shape
    groups = cols.shape[1] // 6
    sends = [x.shape for x in (cols, even, odd, rows, shear, *swap)]
    scratch = edge_scratch(full, groups)

    def branch(by):
        def run(flags, weights, radial0, w0, wt0, cols, even, odd, rows, shear, *swap):
            even, odd, *beside = exchange(even, odd, swap)
            sheared = crossing(by, shear), crossing(by + 1, shear)
            kernel = functools.partial(interior_kernel, False)
            (vt,) = call(kernel, "inner_1", [radial0], [w0, wt0], [turned], [full] + inner_scratch(full))
            wt1, cols, even, odd, rows, shear, *swap = call(
                functools.partial(edge_kernel, False, len(beside)),
                "edge_1",
                [flags, weights],
                [vt, rows, cols, even, odd, *sheared, *beside],
                [turned] + sends,
                scratch,
                aliases={2: 0},
            )
            even, odd, *beside = exchange(even, odd, swap)
            sheared = crossing(by, shear), crossing(by + 1, shear)
            kernel = functools.partial(interior_kernel, True)
            v, dy = call(kernel, "inner_2", [radial0], [wt1, w0], [full, turned], [full] + inner_scratch(full))
            return v, dy, rows, cols, even, odd, *sheared, *beside

        return run

    branches = [branch(by) for by in range(lax.axis_size("gy"))]
    arrays = lax.switch(
        block, branches, flags, weights, radial0, w0, wt0, cols, even, odd, rows, shear, *swap
    )
    (out,) = call(
        functools.partial(edge_kernel, True, 1 if lax.axis_size("gx") == 2 else 2),
        "edge_2",
        [flags, weights],
        arrays,
        [full],
        scratch + [full, pltpu.SemaphoreType.DMA((2 * groups,))],
        out_hbm=True,
    )
    return out


def on_device(density, velocity, bfield, pressure, shear_shift, remap_weight):
    rows, high, width = density.shape
    count_x, count_y = lax.axis_size("gx"), lax.axis_size("gy")
    total_x = rows * count_x
    omega = 1.0 / (SHEAR_Q * total_x)
    row = lax.axis_index("gx")
    is_first, is_last = row == 0, row == count_x - 1
    radial0 = (row * rows).astype(jnp.float32) + 0.5 - 0.5 * total_x
    radial0 = jnp.stack([radial0, jnp.float32(SHEAR_Q * omega)])
    weight = remap_weight.astype(jnp.float32) * WEIGHT_SCALE
    block, rest = shear_shift // width, shear_shift % width
    start = jnp.where(is_first, width - 1 - rest, rest)
    even = 1 - lax.axis_index("gy") % 2
    flags = jnp.stack([x.astype(jnp.int32) for x in (is_first, is_last, start, even)])
    other = 1.0 - weight
    weights = jnp.stack(
        [
            jnp.where(is_first, 1.0 - weight, 1.0 - other),
            jnp.where(is_first, weight, other),
            jnp.where(is_first, 1.0, -1.0),
        ]
    )
    full = (FIELDS, rows, high, width)
    slab = (FIELDS, 2, high, width)
    groups = rows * high // width
    turned = (FIELDS, groups + 1, width + 2 * PAD, width)
    ends = (FIELDS, 2 * groups, width)
    sends = [(FIELDS, 6 * groups, width), ends, ends, (FIELDS, 6, high, width)]
    sends += [slab] * (2 if count_x == 2 else 3)
    start_state = call(
        prepare_kernel,
        "prepare",
        [flags, radial0],
        [density, velocity, bfield, pressure],
        [full, turned] + sends,
        [pltpu.SemaphoreType.DMA((4, groups))],
        in_hbm=True,
    )
    return sections(block, flags, weights, radial0, *start_state)


def solution(mesh):
    placed = (
        P("gx", None, "gy"),
        P(None, "gx", None, "gy"),
        P(None, "gx", None, "gy"),
        P("gx", None, "gy"),
        P(),
        P(),
    )
    return jax.shard_map(
        on_device, mesh=mesh, in_specs=placed, out_specs=P(None, "gx", None, "gy"), check_vma=False
    )
```

```python
import functools

import jax
import jax.numpy as jnp
from jax import lax
from jax.experimental import pallas as pl
from jax.experimental.pallas import tpu as pltpu
from jax.sharding import PartitionSpec as P

GAMMA = 5.0 / 3.0
SHEAR_Q = 1.5
TIME_STEP = 0.03
WEIGHT_SCALE = 1.0 / 65536.0
TINY = 1e-30
FIELDS = 8
PAD = 8


def root(x):
    return x * lax.rsqrt(jnp.maximum(x, TINY))


def signal(state, normal):
    rho, pressure, vn = state[0], state[7], state[1 + normal]
    one, two = [4 + c for c in range(3) if c != normal]
    bn2 = state[4 + normal] * state[4 + normal]
    bt2 = state[one] * state[one] + state[two] * state[two]
    half_b2 = 0.5 * (bt2 + bn2)
    half_gp = (0.5 * GAMMA) * pressure
    spread = half_gp - half_b2
    disc = spread * spread + (GAMMA * pressure) * bt2
    fast = (half_gp + half_b2) + root(disc)
    return jnp.abs(vn) + fast * lax.rsqrt(jnp.maximum(rho * fast, TINY)), bn2 - half_b2


def carried(state, normal, speed, excess):
    rho, pressure = state[0], state[7]
    vel, mag = state[1:4], state[4:7]
    one, two = [c for c in range(3) if c != normal]
    vn, bn = vel[normal], mag[normal]
    pace = vn + speed
    mass = rho * pace
    inner = (0.5 * rho) * (vn * vn + vel[one] * vel[one] + vel[two] * vel[two]) + 1.5 * pressure
    out = [None] * FIELDS
    out[0] = mass
    out[1 + normal] = mass * vn + (pressure - excess)
    out[1 + one] = mass * vel[one] - bn * mag[one]
    out[1 + two] = mass * vel[two] - bn * mag[two]
    out[4 + one] = pace * mag[one] - bn * vel[one]
    out[4 + two] = pace * mag[two] - bn * vel[two]
    work = (pace * inner + vn * pressure) + speed * excess
    out[7] = work + (mag[one] * out[4 + one] + mag[two] * out[4 + two])
    return out


def face(left, right, normal):
    speed_left, excess_left = signal(left, normal)
    speed_right, excess_right = signal(right, normal)
    speed = jnp.maximum(speed_left, speed_right)
    one = carried(left, normal, speed, excess_left)
    two = carried(right, normal, -speed, excess_right)
    field = 4 + normal
    return [speed * (left[f] - right[f]) if f == field else one[f] + two[f] for f in range(FIELDS)]


def limited(up, down):
    return jnp.maximum(jnp.minimum(up, down), jnp.minimum(jnp.maximum(up, down), 0.0))


def to_conserved(w):
    rho = w[0]
    mom = [rho * v for v in w[1:4]]
    kinetic = 0.5 * (mom[0] * w[1] + mom[1] * w[2] + mom[2] * w[3])
    magnetic = 0.5 * (w[4] * w[4] + w[5] * w[5] + w[6] * w[6])
    return [rho] + mom + list(w[4:7]) + [1.5 * w[7] + kinetic + magnetic]


def to_primitive(u):
    inverse = 1.0 / u[0]
    vel = [m * inverse for m in u[1:4]]
    kinetic = 0.5 * (u[1] * vel[0] + u[2] * vel[1] + u[3] * vel[2])
    magnetic = 0.5 * (u[4] * u[4] + u[5] * u[5] + u[6] * u[6])
    return [u[0]] + vel + list(u[4:7]) + [(GAMMA - 1.0) * (u[7] - kinetic - magnetic)]


def whereabouts(rows):
    count_x = lax.axis_size("gx")
    row = lax.axis_index("gx")
    total = rows * count_x
    radial = (row * rows).astype(jnp.float32) + (0.5 - 0.5 * total)
    return radial, 1.0 / (SHEAR_Q * total), row == 0, row == count_x - 1


def at_even_block():
    return lax.rem(lax.axis_index("gy"), 2) == 0


def lanes_of(shape):
    return lax.broadcasted_iota(jnp.int32, shape, 1)


def load_row(ref, i):
    return [ref[f, i] for f in range(FIELDS)]


def turn(w_ref, f, g, wt_ref):
    high, width = w_ref.shape[2:]
    size = width // high
    tile = w_ref[f, pl.ds(g * size, size)].reshape(width, width)
    wt_ref[f, g, PAD : PAD + width] = tile.T


def pad_ends(wt_ref, f, g):
    rows = wt_ref.shape[2]
    wt_ref[f, g, 0:PAD] = wt_ref[f, g, PAD : 2 * PAD]
    wt_ref[f, g, rows - PAD : rows] = wt_ref[f, g, rows - 2 * PAD : rows - PAD]


def send_columns(groups, wt_ref, cols_ref, even_ref, odd_ref):
    rows = wt_ref.shape[2]
    even = at_even_block()
    cells = [PAD, PAD + 1, PAD + 2, rows - PAD - 3, rows - PAD - 2, rows - PAD - 1]

    def body(f, carry):
        for g in range(groups):
            for k, cell in enumerate(cells):
                cols_ref[f, k * groups + g : k * groups + g + 1] = wt_ref[f, g, cell : cell + 1]
            pad_ends(wt_ref, f, g)
        first, last = cols_ref[f, 0 : 2 * groups], cols_ref[f, 4 * groups : 6 * groups]
        even_ref[f] = jnp.where(even, last, first)
        odd_ref[f] = jnp.where(even, first, last)
        return carry

    lax.fori_loop(0, FIELDS, body, 0)


def send_rows(rows, rows_ref, shear_ref, *swap_refs):
    _, _, first, _ = whereabouts(rows)

    def body(k, carry):
        low, high = load_row(rows_ref, k), load_row(rows_ref, 4 + k)
        if len(swap_refs) == 1:
            for f in range(FIELDS):
                swap_refs[0][f, k] = jnp.where(first, high[f], low[f])
        else:
            for f in range(FIELDS):
                swap_refs[0][f, k] = low[f]
                swap_refs[1][f, k] = high[f]
        outer = to_conserved([jnp.where(first, low[f], high[f]) for f in range(FIELDS)])
        for f in range(FIELDS):
            shear_ref[f, k] = outer[f]
        return carry

    lax.fori_loop(0, 2, body, 0)


def prepare_kernel(rho_hbm, vel_hbm, mag_hbm, pres_hbm, w_ref, wt_ref, cols_ref, even_ref, odd_ref, rows_ref, *rest):
    *sends, sems = rest
    rows = w_ref.shape[1]
    radial, omega, _, _ = whereabouts(rows)
    parts = sems.shape[1]
    size = rows // parts
    copies = []
    for part in range(parts):
        at = pl.ds(part * size, size)
        copies.append(
            [
                pltpu.make_async_copy(rho_hbm.at[at], w_ref.at[0, at], sems.at[0, part]),
                pltpu.make_async_copy(vel_hbm.at[:, at], w_ref.at[pl.ds(1, 3), at], sems.at[1, part]),
                pltpu.make_async_copy(mag_hbm.at[:, at], w_ref.at[pl.ds(4, 3), at], sems.at[2, part]),
                pltpu.make_async_copy(pres_hbm.at[at], w_ref.at[7, at], sems.at[3, part]),
            ]
        )
        for copy in copies[-1]:
            copy.start()
    for part in range(parts):
        for copy in copies[part]:
            copy.wait()
        for i in range(part * size, (part + 1) * size):
            w_ref[2, i] = w_ref[2, i] - (SHEAR_Q * omega) * (radial + float(i))

        def turn_fields(n, carry, part=part):
            for f in range(4):
                turn(w_ref, 4 * n + f, part, wt_ref)
            return carry

        lax.fori_loop(0, FIELDS // 4, turn_fields, 0)
    send_columns(parts, wt_ref, cols_ref, even_ref, odd_ref)

    def copy(f, carry):
        rows_ref[f, 0:3] = w_ref[f, 0:3]
        rows_ref[f, 3:6] = w_ref[f, rows - 3 : rows]
        return carry

    lax.fori_loop(0, FIELDS, copy, 0)
    send_rows(rows, rows_ref, *sends)


def three_states(cells):
    left, right = [], []
    for f in range(FIELDS):
        before, here, after = (c[f] for c in cells)
        slope = limited(0.5 * (after - here), 0.5 * (here - before))
        left.append(here + slope)
        right.append(here - slope)
    return left, right


def wrapped(ref, f, value, before, after):
    high = value.shape[0]
    ref[f, 8 : 8 + high] = value
    if before:
        ref[f, 0:8] = value[high - 8 : high]
    if after:
        ref[f, 8 + high : 16 + high] = value[0:8]


def behind(ref, f, at, value):
    ref[f, pl.ds(at, value.shape[0])] = value
    return ref[f, pl.ds(at - 1, value.shape[0])]


def interior_kernel(second, *refs):
    if second:
        wt_ref, w0_ref, v_ref, dy_ref, w_ref, *refs = refs
    else:
        w_ref, wt_ref, vt_ref, v_ref, *refs = refs
        dy_ref = vt_ref
    hz_ref, rz_ref, fz_ref, wl_ref, dx_ref, fx_ref, uy_ref, ly_ref, fy_ref = refs
    rows, high, width = w_ref.shape[1:]
    per_group = width // high
    groups = rows // per_group
    step = 0.5 * TIME_STEP if second else TIME_STEP
    coef = 0.5 * step
    radial, omega, _, _ = whereabouts(rows)
    next_row, last_row = slice(9, 9 + high), slice(7, 7 + high)
    early = per_group + 1

    def turn_result(m):
        g, f = lax.div(m, FIELDS), lax.rem(m, FIELDS)
        tile = v_ref[f, pl.ds(jnp.minimum(g, groups - 1) * per_group, per_group)].reshape(width, width)
        vt_ref[f, jnp.minimum(g, groups), PAD : PAD + width] = tile.T

    def turn_state(m):
        g, f = lax.div(m, FIELDS), lax.rem(m, FIELDS)
        tile = wt_ref[f, g, PAD : PAD + width].T
        w_ref[f, pl.ds(g * per_group, per_group)] = tile.reshape(per_group, high, width)

    def body(i, carry):
        if not second:
            turn_result(jnp.maximum(i - early, 0))
        w = load_row(w_ref, i)
        half = [0.5 * x for x in w]

        left = []
        for f in range(FIELDS):
            wrapped(hz_ref, f, half[f], True, True)
            slope = limited(hz_ref[f, next_row] - half[f], half[f] - hz_ref[f, last_row])
            left.append(w[f] + slope)
            wrapped(rz_ref, f, w[f] - slope, False, True)
        fz = face(left, [rz_ref[f, next_row] for f in range(FIELDS)], 2)
        total = []
        for f in range(FIELDS):
            wrapped(fz_ref, f, fz[f], True, False)
            total.append(fz[f] - fz_ref[f, last_row])

        after, before = jnp.minimum(i + 1, rows - 1), jnp.maximum(i - 1, 0)
        right, wl = [], [wl_ref[f] for f in range(FIELDS)]
        for f in range(FIELDS):
            up = 0.5 * w_ref[f, after] - half[f]
            slope = limited(up, dx_ref[f])
            dx_ref[f] = up
            wl_ref[f] = w[f] + slope
            right.append(w[f] - slope)
        fx = face(wl, right, 0)
        scale = jnp.where(jnp.logical_and(i >= 2, i <= rows - 2), coef, 0.0)
        for f in range(FIELDS):
            here = scale * fx[f]
            v_ref[f, before] = v_ref[f, before] - (here - fx_ref[f])
            fx_ref[f] = here

        x = radial + i.astype(jnp.float32)
        cons = to_conserved(w)
        if second:
            base = [0.5 * (a + b) for a, b in zip(to_conserved(load_row(w0_ref, i)), cons)]
        else:
            base = cons
        tidal = (2.0 * SHEAR_Q * omega * omega) * x
        value = [base[f] - coef * total[f] for f in range(FIELDS)]
        value[1] = value[1] + ((step * 2.0) * omega * cons[2] + (step * tidal) * cons[0])
        value[2] = value[2] - ((step * 2.0) * omega) * cons[1]
        value[7] = value[7] + (step * tidal) * cons[1]
        for f in range(FIELDS):
            v_ref[f, i] = value[f]
        return carry

    size = 2 * groups * width // rows
    strips = width // size
    row = lax.broadcasted_iota(jnp.int32, (size, width), 0)

    def body_y(n, carry):
        for m in (2 * n, 2 * n + 1):
            if second:
                turn_state(m)
            else:
                turn_result(rows - early + m)
        g, start = lax.div(n, strips), size * lax.rem(n, strips)
        at = pl.multiple_of(start + PAD, 8)
        left, right = [], []
        for f in range(FIELDS):
            w = wt_ref[f, g, pl.ds(at, size)]
            up = 0.5 * (wt_ref[f, g, pl.ds(at + 1, size)] - w)
            slope = limited(up, behind(uy_ref, f, at, up))
            left.append(behind(ly_ref, f, at, w + slope))
            right.append(w - slope)
        fy = face(left, right, 1)
        cell = row + start
        scale = jnp.where(jnp.logical_and(cell >= 2, cell <= width - 2), coef, 0.0)
        for f in range(FIELDS):
            here = scale * fy[f]
            change = here - behind(fy_ref, f, at, here)
            if second:
                dy_ref[f, g, pl.ds(at - 1, size)] = change
            else:
                vt_ref[f, g, pl.ds(at - 1, size)] = vt_ref[f, g, pl.ds(at - 1, size)] - change
        return carry

    def azimuthal():
        for f in range(FIELDS):
            uy_ref[f, 0:PAD] = jnp.zeros((PAD, width), jnp.float32)
            ly_ref[f, 0:PAD] = wt_ref[f, 0, PAD : 2 * PAD]
            fy_ref[f, 0:PAD] = jnp.zeros((PAD, width), jnp.float32)
        lax.fori_loop(0, rows // 2, body_y, 0)

    def others():
        for f in range(FIELDS):
            blank = jnp.zeros((high, width), jnp.float32)
            dx_ref[f], fx_ref[f], wl_ref[f] = blank, blank, w_ref[f, 0]
        lax.fori_loop(0, rows, body, 0)

    if second:
        azimuthal()
        others()
        for f in range(FIELDS):
            for g in range(groups):
                dy_ref[f, g, PAD + width - 1 : PAD + width] = jnp.zeros((1, width), jnp.float32)
    else:
        others()
        azimuthal()


def sheared_rows(first, shear_ref, near_ref, next_ref, ghost_ref):
    high, width = near_ref.shape[2:]
    rest = lax.rem(shear_ref[0], width)
    start = jnp.where(first, width - 1 - rest, rest)
    back = lax.rem(width - start, width)
    weight = shear_ref[1].astype(jnp.float32) * WEIGHT_SCALE
    other = 1.0 - weight
    ahead = jnp.where(first, 1.0 - weight, 1.0 - other)
    here = jnp.where(first, weight, other)
    delta = jnp.where(first, 1.0, -1.0)
    lane = lanes_of((high, width))

    def body(k, carry):
        ghost = []
        for f in range(FIELDS):
            near, following = near_ref[f, k], next_ref[f, k]
            one = jnp.where(first, following, near)
            two = jnp.where(first, near, following)
            one_up, two_up = pltpu.roll(one, width - 1, 1), pltpu.roll(two, width - 1, 1)
            one = ahead * jnp.where(lane < width - 1, one_up, two_up) + here * one
            two = ahead * two_up + here * two
            ghost.append(jnp.where(lane < width - start, pltpu.roll(one, back, 1), pltpu.roll(two, back, 1)))
        boosted = list(ghost)
        boosted[2] = ghost[2] + ghost[0] * delta
        boosted[7] = ghost[7] + ghost[2] * delta + 0.5 * ghost[0] * delta * delta
        prim = to_primitive(boosted)
        for f in range(FIELDS):
            ghost_ref[f, k] = prim[f]
        return carry

    lax.fori_loop(0, 2, body, 0)


def edge_kernel(second, beside, shear_any, *refs):
    *refs, shear_smem, shear_sem = refs
    shear_copy = pltpu.make_async_copy(shear_any, shear_smem, shear_sem)
    shear_copy.start()
    if second:
        v_ref, dy_ref, rows_ref, cols_ref, ends_ref, slabs_ref, out_hbm, *refs = refs
        e_ref, a_ref, c_ref, x_ref, ghost_ref, out_ref, sems = refs
        even_ref, odd_ref = ends_ref.at[0], ends_ref.at[1]
        near_ref, next_ref, xl_ref, xr_ref = (slabs_ref.at[k] for k in (0, 1, 2, 1 + beside))
    else:
        vt_ref, rows_ref, cols_ref, even_ref, odd_ref, near_ref, next_ref, *refs = refs
        xl_ref, xr_ref = refs[0], refs[beside - 1]
        w1_ref, cols1_ref, even1_ref, odd1_ref, rows1_ref, *sends, e_ref, a_ref, c_ref, x_ref, ghost_ref = refs[beside:]
    high, width = rows_ref.shape[2:]
    groups = cols_ref.shape[1] // 6
    size = width // high
    rows = groups * size
    step = 0.5 * TIME_STEP if second else TIME_STEP
    coef = 0.5 * step
    _, _, first, last = whereabouts(rows)
    even = at_even_block()

    def gather(f, carry):
        for k in range(2):
            at = slice(k * groups, (k + 1) * groups)
            e_ref[f, k, 0:groups] = jnp.where(even, odd_ref[f, at], even_ref[f, at])
            e_ref[f, 3 + k, groups : 2 * groups] = jnp.where(even, even_ref[f, at], odd_ref[f, at])
        for k in range(3):
            e_ref[f, 2 + k, 0:groups] = cols_ref[f, k * groups : (k + 1) * groups]
            e_ref[f, k, groups : 2 * groups] = cols_ref[f, (3 + k) * groups : (4 + k) * groups]
        return carry

    lax.fori_loop(0, FIELDS, gather, 0)
    cells = [[e_ref[f, k] for f in range(FIELDS)] for k in range(5)]
    sides = [three_states(cells[k : k + 3]) for k in range(3)]
    one = face(sides[0][0], sides[1][1], 1)
    two = face(sides[1][0], sides[2][1], 1)
    low_end = lax.broadcasted_iota(jnp.int32, one[0].shape, 0) < groups
    for f in range(FIELDS):
        a_ref[f, 0] = coef * (two[f] - one[f])
        a_ref[f, 1] = coef * jnp.where(low_end, -two[f], one[f])

    if second:

        def scatter(f, carry):
            for g in range(groups):
                c_ref[f, g] = jnp.zeros((2 * PAD, width), jnp.float32)
                c_ref[f, g, 0:1] = a_ref[f, 0, g : g + 1]
                c_ref[f, g, 1:2] = a_ref[f, 1, g : g + 1]
                c_ref[f, g, 2 * PAD - 2 : 2 * PAD - 1] = a_ref[f, 1, groups + g : groups + g + 1]
                c_ref[f, g, 2 * PAD - 1 : 2 * PAD] = a_ref[f, 0, groups + g : groups + g + 1]
            return carry

        lax.fori_loop(0, FIELDS, scatter, 0)

    shear_copy.wait()
    sheared_rows(first, shear_smem, near_ref, next_ref, ghost_ref)
    def place(f, carry):
        x_ref[0, f, 0:2] = jnp.where(first, ghost_ref[f], xl_ref[f])
        x_ref[1, f, 3:5] = jnp.where(last, ghost_ref[f], xr_ref[f])
        x_ref[0, f, 2:5] = rows_ref[f, 0:3]
        x_ref[1, f, 0:3] = rows_ref[f, 3:6]
        return carry

    lax.fori_loop(0, FIELDS, place, 0)

    def radial(n, carry):
        end = lax.div(n, 2)
        at = pl.ds(pl.multiple_of(lax.rem(n, 2) * (high // 2), 8), high // 2)
        cells = [[x_ref[end, f, k, at] for f in range(FIELDS)] for k in range(5)]
        sides = [three_states(cells[k : k + 3]) for k in range(3)]
        one = face(sides[0][0], sides[1][1], 0)
        two = face(sides[1][0], sides[2][1], 0)
        for f in range(FIELDS):
            x_ref[end, f, 0, at] = coef * (two[f] - one[f])
            x_ref[end, f, 1, at] = coef * jnp.where(end == 0, -two[f], one[f])
        return carry

    lax.fori_loop(0, 4, radial, 0)
    batch = FIELDS // 2

    if not second:
        lane = lanes_of((width, width))

        def correct(n, carry):
            for k in range(batch):
                f = n * batch + k
                strip = [x_ref[0, f, 0], x_ref[0, f, 1], jnp.zeros((width - 4 * high, width), jnp.float32)]
                strip = jnp.concatenate(strip + [x_ref[1, f, 1], x_ref[1, f, 0]], axis=0).T
                at = slice(PAD, PAD + width)
                w1_ref[f, 0, at] = vt_ref[f, 0, at] - jnp.where(lane < width // 2, strip, 0.0)
                w1_ref[f, groups - 1, at] = vt_ref[f, groups - 1, at] - jnp.where(lane < width // 2, 0.0, strip)
            return carry

        lax.fori_loop(0, FIELDS // batch, correct, 0)

        def correct_rows(f, carry):
            for g in range(groups):
                places = [(0, 0, g), (1, 1, g), (width - 2, 1, groups + g), (width - 1, 0, groups + g)]
                for to, kind, at in places:
                    to = slice(PAD + to, PAD + to + 1)
                    w1_ref[f, g, to] = w1_ref[f, g, to] - a_ref[f, kind, at : at + 1]
            return carry

        lax.fori_loop(0, FIELDS, correct_rows, 0)
        strips = width // 16

        def primitives(n, carry):
            g, at = lax.div(n, strips), pl.ds(pl.multiple_of(PAD + 16 * lax.rem(n, strips), 8), 16)
            prim = to_primitive([w1_ref[f, g, at] for f in range(FIELDS)])
            for f in range(FIELDS):
                w1_ref[f, g, at] = prim[f]
            return carry

        lax.fori_loop(0, groups * strips, primitives, 0, unroll=4)

        def turn_rows(n, carry):
            for k in range(batch):
                f = n * batch + k
                at = slice(PAD, PAD + width)
                strip = jnp.where(lane < width // 2, w1_ref[f, 0, at], w1_ref[f, groups - 1, at]).T
                rows1_ref[f, 0:3] = strip[0 : 3 * high].reshape(3, high, width)
                rows1_ref[f, 3:6] = strip[width - 3 * high : width].reshape(3, high, width)
            return carry

        lax.fori_loop(0, FIELDS // batch, turn_rows, 0)
        send_columns(groups, w1_ref, cols1_ref, even1_ref, odd1_ref)
        send_rows(rows, rows1_ref, *sends)
        return

    def finish(n, carry):
        g = lax.div(n, 2)
        at = pl.ds(g * size, size)
        fields = [lax.rem(n, 2) * batch + f for f in range(batch)]
        for f in fields:
            head = dy_ref[f, g, PAD : 2 * PAD] + c_ref[f, g, 0:PAD]
            tail = dy_ref[f, g, width : PAD + width] + c_ref[f, g, PAD : 2 * PAD]
            strip = jnp.concatenate([head, dy_ref[f, g, 2 * PAD : width], tail], axis=0)
            out_ref[f, at] = v_ref[f, at] - strip.T.reshape(size, high, width)

        @pl.when(g == 0)
        def _():
            for f in fields:
                out_ref[f, 0] = out_ref[f, 0] - x_ref[0, f, 0]
                out_ref[f, 1] = out_ref[f, 1] - x_ref[0, f, 1]

        @pl.when(g == groups - 1)
        def _():
            for f in fields:
                out_ref[f, rows - 1] = out_ref[f, rows - 1] - x_ref[1, f, 0]
                out_ref[f, rows - 2] = out_ref[f, rows - 2] - x_ref[1, f, 1]

        part = pl.ds(fields[0], batch)
        pltpu.make_async_copy(out_ref.at[part, at], out_hbm.at[part, at], sems.at[n]).start()
        return carry

    lax.fori_loop(0, 2 * groups, finish, 0)
    for n in range(2 * groups):
        at, part = pl.ds(n // 2 * size, size), pl.ds(n % 2 * batch, batch)
        pltpu.make_async_copy(out_ref.at[part, at], out_hbm.at[part, at], sems.at[n]).wait()


def gather_kernel(even_ref, odd_ref, *refs):
    *slabs, ends_ref, slabs_ref = refs

    def body(f, carry):
        ends_ref[0, f], ends_ref[1, f] = even_ref[f], odd_ref[f]
        for k, ref in enumerate(slabs):
            slabs_ref[k, f] = ref[f]
        return carry

    lax.fori_loop(0, FIELDS, body, 0)


def call(kernel, name, arrays, shapes, scratch=(), in_hbm=False, out_hbm=False, aliases=None, shear=()):
    vmem = pl.BlockSpec(memory_space=pltpu.VMEM)
    hbm = pl.BlockSpec(memory_space=pltpu.HBM)
    if in_hbm:
        arrays = [pltpu.with_memory_space_constraint(x, pltpu.HBM) for x in arrays]
    return pl.pallas_call(
        kernel,
        name=name,
        out_shape=[jax.ShapeDtypeStruct(s, jnp.float32) for s in shapes],
        in_specs=[pl.BlockSpec(memory_space=pl.ANY)] * len(shear) + [hbm if in_hbm else vmem] * len(arrays),
        out_specs=[hbm if out_hbm else vmem] * len(shapes),
        scratch_shapes=[pltpu.VMEM(s, jnp.float32) if isinstance(s, tuple) else s for s in scratch],
        input_output_aliases=aliases or {},
        compiler_params=pltpu.CompilerParams(vmem_limit_bytes=20 * 1024 * 1024),
    )(*shear, *arrays)


def exchange(even, odd, swap):
    count_x, count_y = lax.axis_size("gx"), lax.axis_size("gy")

    def pairs(start):
        ends = [(i, (i + 1) % count_y) for i in range(start, count_y, 2)]
        return ends + [(j, i) for i, j in ends]

    even, odd = lax.ppermute(even, "gy", pairs(0)), lax.ppermute(odd, "gy", pairs(1))
    if len(swap) == 1:
        return even, odd, lax.ppermute(swap[0], "gx", [(0, 1), (1, 0)])
    x_low = lax.ppermute(swap[1], "gx", [(i, i + 1) for i in range(count_x - 1)])
    x_high = lax.ppermute(swap[0], "gx", [(i + 1, i) for i in range(count_x - 1)])
    return even, odd, x_low, x_high


def crossing(by, shear):
    count_x, count_y = lax.axis_size("gx"), lax.axis_size("gy")
    last = (count_x - 1) * count_y
    pairs = []
    for gy in range(count_y):
        pairs.append((last + gy, (gy + by) % count_y))
        pairs.append((gy, last + (gy - by) % count_y))
    return lax.ppermute(shear, ("gx", "gy"), pairs)


def inner_scratch(full):
    high, width = full[2:]
    tile = (FIELDS, high, width)
    padded = (FIELDS, high + 2 * PAD, width)
    column = (FIELDS, PAD + width, width)
    return [padded] * 3 + [tile] * 3 + [column] * 3


def edge_scratch(full, groups):
    high, width = full[2:]
    return [
        (FIELDS, 5, 2 * groups, width),
        (FIELDS, 2, 2 * groups, width),
        (FIELDS, groups, 2 * PAD, width),
        (2, FIELDS, 5, high, width),
        (FIELDS, 2, high, width),
        pltpu.SMEM((2,), jnp.int32),
        pltpu.SemaphoreType.DMA,
    ]


def sections(block, drift, w0, wt0, cols, even, odd, rows, shear, *swap):
    full, turned = w0.shape, wt0.shape
    groups = cols.shape[1] // 6
    sends = [x.shape for x in (cols, even, odd, rows, shear, *swap)]
    scratch = edge_scratch(full, groups)
    received = [(2,) + even.shape, (2 + (1 if len(swap) == 1 else 2),) + shear.shape]

    def branch(by):
        def run(drift, w0, wt0, cols, even, odd, rows, shear, *swap):
            even, odd, *beside = exchange(even, odd, swap)
            sheared = crossing(by, shear), crossing(by + 1, shear)
            kernel = functools.partial(interior_kernel, False)
            (vt,) = call(kernel, "inner_1", [w0, wt0], [turned], [full] + inner_scratch(full))
            wt1, cols, even, odd, rows, shear, *swap = call(
                functools.partial(edge_kernel, False, len(beside)),
                "edge_1",
                [vt, rows, cols, even, odd, *sheared, *beside],
                [turned] + sends,
                scratch,
                aliases={1: 0},
                shear=[drift],
            )
            even, odd, *beside = exchange(even, odd, swap)
            sheared = crossing(by, shear), crossing(by + 1, shear)
            kernel = functools.partial(interior_kernel, True)
            v, dy = call(kernel, "inner_2", [wt1, w0], [full, turned], [full] + inner_scratch(full))
            ends, slabs = call(gather_kernel, "gather", [even, odd, *sheared, *beside], received)
            return v, dy, rows, cols, ends, slabs

        return run

    branches = [branch(by) for by in range(lax.axis_size("gy"))]
    arrays = lax.switch(block, branches, drift, w0, wt0, cols, even, odd, rows, shear, *swap)
    (out,) = call(
        functools.partial(edge_kernel, True, received[1][0] - 2),
        "edge_2",
        arrays,
        [full],
        scratch[:-2] + [full, pltpu.SemaphoreType.DMA((2 * groups,))] + scratch[-2:],
        out_hbm=True,
        shear=[drift],
    )
    return out


def on_device(density, velocity, bfield, pressure, shear_shift, remap_weight):
    rows, high, width = density.shape
    count_x = lax.axis_size("gx")
    drift = jnp.stack([shear_shift, remap_weight])
    full = (FIELDS, rows, high, width)
    slab = (FIELDS, 2, high, width)
    groups = rows * high // width
    turned = (FIELDS, groups + 1, width + 2 * PAD, width)
    ends = (FIELDS, 2 * groups, width)
    sends = [(FIELDS, 6 * groups, width), ends, ends, (FIELDS, 6, high, width)]
    sends += [slab] * (2 if count_x == 2 else 3)
    start_state = call(
        prepare_kernel,
        "prepare",
        [density, velocity, bfield, pressure],
        [full, turned] + sends,
        [pltpu.SemaphoreType.DMA((4, groups))],
        in_hbm=True,
    )
    return sections(shear_shift // width, drift, *start_state)


def solution(mesh):
    placed = (
        P("gx", None, "gy"),
        P(None, "gx", None, "gy"),
        P(None, "gx", None, "gy"),
        P("gx", None, "gy"),
        P(),
        P(),
    )
    return jax.shard_map(
        on_device, mesh=mesh, in_specs=placed, out_specs=P(None, "gx", None, "gy"), check_vma=False
    )
```

```python
import functools

import jax
import jax.numpy as jnp
from jax import lax
from jax.experimental import pallas as pl
from jax.experimental.pallas import tpu as pltpu
from jax.sharding import PartitionSpec as P

GAMMA = 5.0 / 3.0
SHEAR_Q = 1.5
TIME_STEP = 0.03
WEIGHT_SCALE = 1.0 / 65536.0
TINY = 1e-30
FIELDS = 8
PAD = 8


def root(x):
    return x * lax.rsqrt(jnp.maximum(x, TINY))


def signal(state, normal):
    rho, pressure, vn = state[0], state[7], state[1 + normal]
    one, two = [4 + c for c in range(3) if c != normal]
    bn2 = state[4 + normal] * state[4 + normal]
    bt2 = state[one] * state[one] + state[two] * state[two]
    half_b2 = 0.5 * (bt2 + bn2)
    half_gp = (0.5 * GAMMA) * pressure
    spread = half_gp - half_b2
    disc = spread * spread + (GAMMA * pressure) * bt2
    fast = (half_gp + half_b2) + root(disc)
    return jnp.abs(vn) + fast * lax.rsqrt(jnp.maximum(rho * fast, TINY)), bn2 - half_b2


def carried(state, normal, speed, excess):
    rho, pressure = state[0], state[7]
    vel, mag = state[1:4], state[4:7]
    one, two = [c for c in range(3) if c != normal]
    vn, bn = vel[normal], mag[normal]
    pace = vn + speed
    mass = rho * pace
    inner = (0.5 * rho) * (vn * vn + vel[one] * vel[one] + vel[two] * vel[two]) + 1.5 * pressure
    out = [None] * FIELDS
    out[0] = mass
    out[1 + normal] = mass * vn + (pressure - excess)
    out[1 + one] = mass * vel[one] - bn * mag[one]
    out[1 + two] = mass * vel[two] - bn * mag[two]
    out[4 + one] = pace * mag[one] - bn * vel[one]
    out[4 + two] = pace * mag[two] - bn * vel[two]
    work = (pace * inner + vn * pressure) + speed * excess
    out[7] = work + (mag[one] * out[4 + one] + mag[two] * out[4 + two])
    return out


def face(left, right, normal):
    speed_left, excess_left = signal(left, normal)
    speed_right, excess_right = signal(right, normal)
    speed = jnp.maximum(speed_left, speed_right)
    one = carried(left, normal, speed, excess_left)
    two = carried(right, normal, -speed, excess_right)
    field = 4 + normal
    return [speed * (left[f] - right[f]) if f == field else one[f] + two[f] for f in range(FIELDS)]


def limited(up, down):
    return jnp.maximum(jnp.minimum(up, down), jnp.minimum(jnp.maximum(up, down), 0.0))


def to_conserved(w):
    rho = w[0]
    mom = [rho * v for v in w[1:4]]
    kinetic = 0.5 * (mom[0] * w[1] + mom[1] * w[2] + mom[2] * w[3])
    magnetic = 0.5 * (w[4] * w[4] + w[5] * w[5] + w[6] * w[6])
    return [rho] + mom + list(w[4:7]) + [1.5 * w[7] + kinetic + magnetic]


def to_primitive(u):
    inverse = 1.0 / u[0]
    vel = [m * inverse for m in u[1:4]]
    kinetic = 0.5 * (u[1] * vel[0] + u[2] * vel[1] + u[3] * vel[2])
    magnetic = 0.5 * (u[4] * u[4] + u[5] * u[5] + u[6] * u[6])
    return [u[0]] + vel + list(u[4:7]) + [(GAMMA - 1.0) * (u[7] - kinetic - magnetic)]


def whereabouts(rows):
    count_x = lax.axis_size("gx")
    row = lax.axis_index("gx")
    total = rows * count_x
    radial = (row * rows).astype(jnp.float32) + (0.5 - 0.5 * total)
    return radial, 1.0 / (SHEAR_Q * total), row == 0, row == count_x - 1


def at_even_block():
    return lax.rem(lax.axis_index("gy"), 2) == 0


def lanes_of(shape):
    return lax.broadcasted_iota(jnp.int32, shape, 1)


def load_row(ref, i):
    return [ref[f, i] for f in range(FIELDS)]


def turn(w_ref, f, g, wt_ref):
    high, width = w_ref.shape[2:]
    size = width // high
    tile = w_ref[f, pl.ds(g * size, size)].reshape(width, width)
    wt_ref[f, g, PAD : PAD + width] = tile.T


def pad_ends(wt_ref, f, g):
    rows = wt_ref.shape[2]
    wt_ref[f, g, 0:PAD] = wt_ref[f, g, PAD : 2 * PAD]
    wt_ref[f, g, rows - PAD : rows] = wt_ref[f, g, rows - 2 * PAD : rows - PAD]


def send_columns(groups, wt_ref, cols_ref, even_ref, odd_ref):
    rows = wt_ref.shape[2]
    even = at_even_block()
    cells = [PAD, PAD + 1, PAD + 2, rows - PAD - 3, rows - PAD - 2, rows - PAD - 1]

    def body(f, carry):
        for g in range(groups):
            for k, cell in enumerate(cells):
                cols_ref[f, k * groups + g : k * groups + g + 1] = wt_ref[f, g, cell : cell + 1]
            pad_ends(wt_ref, f, g)
        first, last = cols_ref[f, 0 : 2 * groups], cols_ref[f, 4 * groups : 6 * groups]
        even_ref[f] = jnp.where(even, last, first)
        odd_ref[f] = jnp.where(even, first, last)
        return carry

    lax.fori_loop(0, FIELDS, body, 0)


def send_rows(rows, rows_ref, shear_ref, *swap_refs):
    _, _, first, _ = whereabouts(rows)

    def body(k, carry):
        low, high = load_row(rows_ref, k), load_row(rows_ref, 4 + k)
        if len(swap_refs) == 1:
            for f in range(FIELDS):
                swap_refs[0][f, k] = jnp.where(first, high[f], low[f])
        else:
            for f in range(FIELDS):
                swap_refs[0][f, k] = low[f]
                swap_refs[1][f, k] = high[f]
        outer = to_conserved([jnp.where(first, low[f], high[f]) for f in range(FIELDS)])
        for f in range(FIELDS):
            shear_ref[f, k] = outer[f]
        return carry

    lax.fori_loop(0, 2, body, 0)


def prepare_kernel(rho_hbm, vel_hbm, mag_hbm, pres_hbm, w_ref, wt_ref, cols_ref, even_ref, odd_ref, rows_ref, *rest):
    *sends, sems = rest
    rows = w_ref.shape[1]
    radial, omega, _, _ = whereabouts(rows)
    parts = sems.shape[1]
    size = rows // parts
    copies = []
    for part in range(parts):
        at = pl.ds(part * size, size)
        copies.append(
            [
                pltpu.make_async_copy(rho_hbm.at[at], w_ref.at[0, at], sems.at[0, part]),
                pltpu.make_async_copy(vel_hbm.at[:, at], w_ref.at[pl.ds(1, 3), at], sems.at[1, part]),
                pltpu.make_async_copy(mag_hbm.at[:, at], w_ref.at[pl.ds(4, 3), at], sems.at[2, part]),
                pltpu.make_async_copy(pres_hbm.at[at], w_ref.at[7, at], sems.at[3, part]),
            ]
        )
        for copy in copies[-1]:
            copy.start()
    for part in range(parts):
        for copy in copies[part]:
            copy.wait()
        for i in range(part * size, (part + 1) * size):
            w_ref[2, i] = w_ref[2, i] - (SHEAR_Q * omega) * (radial + float(i))
        for f in range(FIELDS):
            turn(w_ref, f, part, wt_ref)
    send_columns(parts, wt_ref, cols_ref, even_ref, odd_ref)

    def copy(f, carry):
        rows_ref[f, 0:3] = w_ref[f, 0:3]
        rows_ref[f, 3:6] = w_ref[f, rows - 3 : rows]
        return carry

    lax.fori_loop(0, FIELDS, copy, 0)
    send_rows(rows, rows_ref, *sends)


def three_states(cells):
    left, right = [], []
    for f in range(FIELDS):
        before, here, after = (c[f] for c in cells)
        slope = limited(0.5 * (after - here), 0.5 * (here - before))
        left.append(here + slope)
        right.append(here - slope)
    return left, right


def wrapped(ref, f, value, before, after):
    high = value.shape[0]
    ref[f, 8 : 8 + high] = value
    if before:
        ref[f, 0:8] = value[high - 8 : high]
    if after:
        ref[f, 8 + high : 16 + high] = value[0:8]


def behind(ref, f, at, value):
    ref[f, pl.ds(at, value.shape[0])] = value
    return ref[f, pl.ds(at - 1, value.shape[0])]


def interior_kernel(second, *refs):
    if second:
        wt_ref, w0_ref, v_ref, dy_ref, w_ref, *refs = refs
    else:
        w_ref, wt_ref, vt_ref, v_ref, *refs = refs
        dy_ref = vt_ref
    hz_ref, rz_ref, fz_ref, wl_ref, dx_ref, fx_ref, half_ref, uy_ref, ly_ref, fy_ref = refs
    rows, high, width = w_ref.shape[1:]
    per_group = width // high
    groups = rows // per_group
    step = 0.5 * TIME_STEP if second else TIME_STEP
    coef = 0.5 * step
    radial, omega, _, _ = whereabouts(rows)
    next_row, last_row = slice(9, 9 + high), slice(7, 7 + high)
    early = per_group + 1

    def turn_result(m):
        g, f = lax.div(m, FIELDS), lax.rem(m, FIELDS)
        tile = v_ref[f, pl.ds(jnp.minimum(g, groups - 1) * per_group, per_group)].reshape(width, width)
        vt_ref[f, jnp.minimum(g, groups), PAD : PAD + width] = tile.T

    def turn_state(m):
        g, f = lax.div(m, FIELDS), lax.rem(m, FIELDS)
        tile = wt_ref[f, g, PAD : PAD + width].T
        w_ref[f, pl.ds(g * per_group, per_group)] = tile.reshape(per_group, high, width)

    def body(i, carry):
        if not second:
            turn_result(jnp.maximum(i - early, 0))
        w = load_row(w_ref, i)
        half = [half_ref[f] for f in range(FIELDS)]

        after, before = jnp.minimum(i + 1, rows - 1), jnp.maximum(i - 1, 0)
        right, wl = [], [wl_ref[f] for f in range(FIELDS)]
        for f in range(FIELDS):
            half_after = 0.5 * w_ref[f, after]
            half_ref[f] = half_after
            up = half_after - half[f]
            slope = limited(up, dx_ref[f])
            dx_ref[f] = up
            wl_ref[f] = w[f] + slope
            right.append(w[f] - slope)
        fx = face(wl, right, 0)
        scale = jnp.where(jnp.logical_and(i >= 2, i <= rows - 2), coef, 0.0)
        for f in range(FIELDS):
            here = scale * fx[f]
            v_ref[f, before] = v_ref[f, before] - (here - fx_ref[f])
            fx_ref[f] = here

        left = []
        for f in range(FIELDS):
            wrapped(hz_ref, f, half[f], True, True)
            slope = limited(hz_ref[f, next_row] - half[f], half[f] - hz_ref[f, last_row])
            left.append(w[f] + slope)
            wrapped(rz_ref, f, w[f] - slope, False, True)
        fz = face(left, [rz_ref[f, next_row] for f in range(FIELDS)], 2)
        total = []
        for f in range(FIELDS):
            wrapped(fz_ref, f, fz[f], True, False)
            total.append(fz[f] - fz_ref[f, last_row])

        x = radial + i.astype(jnp.float32)
        cons = to_conserved(w)
        if second:
            base = [0.5 * (a + b) for a, b in zip(to_conserved(load_row(w0_ref, i)), cons)]
        else:
            base = cons
        tidal = (2.0 * SHEAR_Q * omega * omega) * x
        value = [base[f] - coef * total[f] for f in range(FIELDS)]
        value[1] = value[1] + ((step * 2.0) * omega * cons[2] + (step * tidal) * cons[0])
        value[2] = value[2] - ((step * 2.0) * omega) * cons[1]
        value[7] = value[7] + (step * tidal) * cons[1]
        for f in range(FIELDS):
            v_ref[f, i] = value[f]
        return carry

    size = 2 * groups * width // rows
    strips = width // size
    row = lax.broadcasted_iota(jnp.int32, (size, width), 0)

    def body_y(n, carry):
        for m in (2 * n, 2 * n + 1):
            if second:
                turn_state(m)
            else:
                turn_result(rows - early + m)
        g, start = lax.div(n, strips), size * lax.rem(n, strips)
        at = pl.multiple_of(start + PAD, 8)
        left, right = [], []
        for f in range(FIELDS):
            w = wt_ref[f, g, pl.ds(at, size)]
            up = 0.5 * (wt_ref[f, g, pl.ds(at + 1, size)] - w)
            slope = limited(up, behind(uy_ref, f, at, up))
            left.append(behind(ly_ref, f, at, w + slope))
            right.append(w - slope)
        fy = face(left, right, 1)
        cell = row + start
        scale = jnp.where(jnp.logical_and(cell >= 2, cell <= width - 2), coef, 0.0)
        for f in range(FIELDS):
            here = scale * fy[f]
            change = here - behind(fy_ref, f, at, here)
            if second:
                dy_ref[f, g, pl.ds(at - 1, size)] = change
            else:
                vt_ref[f, g, pl.ds(at - 1, size)] = vt_ref[f, g, pl.ds(at - 1, size)] - change
        return carry

    def azimuthal():
        for f in range(FIELDS):
            uy_ref[f, 0:PAD] = jnp.zeros((PAD, width), jnp.float32)
            ly_ref[f, 0:PAD] = wt_ref[f, 0, PAD : 2 * PAD]
            fy_ref[f, 0:PAD] = jnp.zeros((PAD, width), jnp.float32)
        lax.fori_loop(0, rows // 2, body_y, 0)

    def others():
        for f in range(FIELDS):
            blank = jnp.zeros((high, width), jnp.float32)
            dx_ref[f], fx_ref[f], wl_ref[f] = blank, blank, w_ref[f, 0]
            half_ref[f] = 0.5 * w_ref[f, 0]
        lax.fori_loop(0, rows, body, 0)

    if second:
        azimuthal()
        others()
        for f in range(FIELDS):
            for g in range(groups):
                dy_ref[f, g, PAD + width - 1 : PAD + width] = jnp.zeros((1, width), jnp.float32)
    else:
        others()
        azimuthal()


def sheared_rows(loop, first, shear_ref, near_ref, next_ref, ghost_ref):
    high, width = near_ref.shape[2:]
    rest = lax.rem(shear_ref[0], width)
    start = jnp.where(first, width - 1 - rest, rest)
    back = lax.rem(width - start, width)
    weight = shear_ref[1].astype(jnp.float32) * WEIGHT_SCALE
    other = 1.0 - weight
    ahead = jnp.where(first, 1.0 - weight, 1.0 - other)
    here = jnp.where(first, weight, other)
    delta = jnp.where(first, 1.0, -1.0)
    lane = lanes_of((high, width))

    def body(k, carry):
        ghost = []
        for f in range(FIELDS):
            near, following = near_ref[f, k], next_ref[f, k]
            one = jnp.where(first, following, near)
            two = jnp.where(first, near, following)
            two = pltpu.roll(two, back, 1)
            one = jnp.where(lane < width - start, pltpu.roll(one, back, 1), two)
            two = pltpu.roll(jnp.where(lane == 0, two, one), width - 1, 1)
            ghost.append(ahead * two + here * one)
        boosted = list(ghost)
        boosted[2] = ghost[2] + ghost[0] * delta
        boosted[7] = ghost[7] + ghost[2] * delta + 0.5 * ghost[0] * delta * delta
        prim = to_primitive(boosted)
        for f in range(FIELDS):
            ghost_ref[f, k] = prim[f]
        return carry

    loop(2, body)


def in_loop(count, body):
    lax.fori_loop(0, count, body, 0)


def unrolled(count, body):
    for n in range(count):
        body(n, 0)


def edge_kernel(second, beside, shear_any, *refs):
    *refs, shear_smem, shear_sem = refs
    shear_copy = pltpu.make_async_copy(shear_any, shear_smem, shear_sem)
    shear_copy.start()
    if second:
        v_ref, dy_ref, rows_ref, cols_ref, ends_ref, slabs_ref, out_hbm, *refs = refs
        e_ref, a_ref, c_ref, x_ref, ghost_ref, out_ref, sems = refs
        even_ref, odd_ref = ends_ref.at[0], ends_ref.at[1]
        near_ref, next_ref, xl_ref, xr_ref = (slabs_ref.at[k] for k in (0, 1, 2, 1 + beside))
    else:
        vt_ref, rows_ref, cols_ref, even_ref, odd_ref, near_ref, next_ref, *refs = refs
        xl_ref, xr_ref = refs[0], refs[beside - 1]
        w1_ref, cols1_ref, even1_ref, odd1_ref, rows1_ref, *sends, e_ref, a_ref, c_ref, x_ref, ghost_ref = refs[beside:]
    high, width = rows_ref.shape[2:]
    groups = cols_ref.shape[1] // 6
    size = width // high
    rows = groups * size
    step = 0.5 * TIME_STEP if second else TIME_STEP
    coef = 0.5 * step
    _, _, first, last = whereabouts(rows)
    even = at_even_block()
    loop = unrolled if second else in_loop

    def gather(f, carry):
        for k in range(2):
            at = slice(k * groups, (k + 1) * groups)
            e_ref[f, k, 0:groups] = jnp.where(even, odd_ref[f, at], even_ref[f, at])
            e_ref[f, 3 + k, groups : 2 * groups] = jnp.where(even, even_ref[f, at], odd_ref[f, at])
        for k in range(3):
            e_ref[f, 2 + k, 0:groups] = cols_ref[f, k * groups : (k + 1) * groups]
            e_ref[f, k, groups : 2 * groups] = cols_ref[f, (3 + k) * groups : (4 + k) * groups]
        return carry

    lax.fori_loop(0, FIELDS, gather, 0)
    if second:
        shear_copy.wait()
        sheared_rows(loop, first, shear_smem, near_ref, next_ref, ghost_ref)
    cells = [[e_ref[f, k] for f in range(FIELDS)] for k in range(5)]
    sides = [three_states(cells[k : k + 3]) for k in range(3)]
    one = face(sides[0][0], sides[1][1], 1)
    two = face(sides[1][0], sides[2][1], 1)
    low_end = lax.broadcasted_iota(jnp.int32, one[0].shape, 0) < groups
    for f in range(FIELDS):
        a_ref[f, 0] = coef * (two[f] - one[f])
        a_ref[f, 1] = coef * jnp.where(low_end, -two[f], one[f])

    if second:

        def scatter(f, carry):
            for g in range(groups):
                c_ref[f, g] = jnp.zeros((2 * PAD, width), jnp.float32)
                c_ref[f, g, 0:1] = a_ref[f, 0, g : g + 1]
                c_ref[f, g, 1:2] = a_ref[f, 1, g : g + 1]
                c_ref[f, g, 2 * PAD - 2 : 2 * PAD - 1] = a_ref[f, 1, groups + g : groups + g + 1]
                c_ref[f, g, 2 * PAD - 1 : 2 * PAD] = a_ref[f, 0, groups + g : groups + g + 1]
            return carry

        lax.fori_loop(0, FIELDS, scatter, 0)

    if not second:
        shear_copy.wait()
        sheared_rows(loop, first, shear_smem, near_ref, next_ref, ghost_ref)
    def place(f, carry):
        x_ref[0, f, 0:2] = jnp.where(first, ghost_ref[f], xl_ref[f])
        x_ref[1, f, 3:5] = jnp.where(last, ghost_ref[f], xr_ref[f])
        x_ref[0, f, 2:5] = rows_ref[f, 0:3]
        x_ref[1, f, 0:3] = rows_ref[f, 3:6]
        return carry

    lax.fori_loop(0, FIELDS, place, 0)

    def radial(n, carry):
        if second:
            end, at = n // 2, pl.ds(n % 2 * (high // 2), high // 2)
        else:
            end, at = lax.div(n, 2), pl.ds(pl.multiple_of(lax.rem(n, 2) * (high // 2), 8), high // 2)
        cells = [[x_ref[end, f, k, at] for f in range(FIELDS)] for k in range(5)]
        sides = [three_states(cells[k : k + 3]) for k in range(3)]
        one = face(sides[0][0], sides[1][1], 0)
        two = face(sides[1][0], sides[2][1], 0)
        for f in range(FIELDS):
            x_ref[end, f, 0, at] = coef * (two[f] - one[f])
            x_ref[end, f, 1, at] = coef * jnp.where(end == 0, -two[f], one[f])
        return carry

    loop(4, radial)
    batch = FIELDS // 4

    if not second:
        lane = lanes_of((width, width))

        def correct(n, carry):
            for k in range(batch):
                f = n * batch + k
                strip = [x_ref[0, f, 0], x_ref[0, f, 1], jnp.zeros((width - 4 * high, width), jnp.float32)]
                strip = jnp.concatenate(strip + [x_ref[1, f, 1], x_ref[1, f, 0]], axis=0).T
                at = slice(PAD, PAD + width)
                w1_ref[f, 0, at] = vt_ref[f, 0, at] - jnp.where(lane < width // 2, strip, 0.0)
                w1_ref[f, groups - 1, at] = vt_ref[f, groups - 1, at] - jnp.where(lane < width // 2, 0.0, strip)
            return carry

        lax.fori_loop(0, FIELDS // batch, correct, 0)

        def correct_rows(f, carry):
            for g in range(groups):
                places = [(0, 0, g), (1, 1, g), (width - 2, 1, groups + g), (width - 1, 0, groups + g)]
                for to, kind, at in places:
                    to = slice(PAD + to, PAD + to + 1)
                    w1_ref[f, g, to] = w1_ref[f, g, to] - a_ref[f, kind, at : at + 1]
            return carry

        lax.fori_loop(0, FIELDS, correct_rows, 0)
        block = width // 2

        def primitives(n, carry):
            g, at = lax.div(n, 2), pl.ds(pl.multiple_of(PAD + block * lax.rem(n, 2), 8), block)
            prim = to_primitive([w1_ref[f, g, at] for f in range(FIELDS)])
            for f in range(FIELDS):
                w1_ref[f, g, at] = prim[f]
            return carry

        lax.fori_loop(0, 2 * groups, primitives, 0)

        def turn_rows(n, carry):
            for k in range(batch):
                f = n * batch + k
                at = slice(PAD, PAD + width)
                strip = jnp.where(lane < width // 2, w1_ref[f, 0, at], w1_ref[f, groups - 1, at]).T
                rows1_ref[f, 0:3] = strip[0 : 3 * high].reshape(3, high, width)
                rows1_ref[f, 3:6] = strip[width - 3 * high : width].reshape(3, high, width)
            return carry

        lax.fori_loop(0, FIELDS // batch, turn_rows, 0)
        send_columns(groups, w1_ref, cols1_ref, even1_ref, odd1_ref)
        send_rows(rows, rows1_ref, *sends)
        return

    batch = FIELDS // 2
    copies = []
    for g in [*range(1, groups - 1), 0, groups - 1]:
        at = pl.ds(g * size, size)
        for half in range(2):
            for f in range(half * batch, (half + 1) * batch):
                head = dy_ref[f, g, PAD : 2 * PAD] + c_ref[f, g, 0:PAD]
                tail = dy_ref[f, g, width : PAD + width] + c_ref[f, g, PAD : 2 * PAD]
                strip = jnp.concatenate([head, dy_ref[f, g, 2 * PAD : width], tail], axis=0)
                strip = strip.T.reshape(size, high, width)
                value = [v_ref[f, g * size + i] - strip[i] for i in range(size)]
                if g == 0:
                    value[0], value[1] = value[0] - x_ref[0, f, 0], value[1] - x_ref[0, f, 1]
                if g == groups - 1:
                    value[-1], value[-2] = value[-1] - x_ref[1, f, 0], value[-2] - x_ref[1, f, 1]
                for i in range(size):
                    out_ref[f, g * size + i] = value[i]
            part = pl.ds(half * batch, batch)
            copy = pltpu.make_async_copy(out_ref.at[part, at], out_hbm.at[part, at], sems.at[len(copies)])
            copy.start()
            copies.append(copy)
    for copy in copies:
        copy.wait()


def gather_kernel(even_ref, odd_ref, *refs):
    *slabs, ends_ref, slabs_ref = refs

    def body(f, carry):
        ends_ref[0, f], ends_ref[1, f] = even_ref[f], odd_ref[f]
        for k, ref in enumerate(slabs):
            slabs_ref[k, f] = ref[f]
        return carry

    lax.fori_loop(0, FIELDS, body, 0)


def call(kernel, name, arrays, shapes, scratch=(), in_hbm=False, out_hbm=False, aliases=None, shear=()):
    vmem = pl.BlockSpec(memory_space=pltpu.VMEM)
    hbm = pl.BlockSpec(memory_space=pltpu.HBM)
    if in_hbm:
        arrays = [pltpu.with_memory_space_constraint(x, pltpu.HBM) for x in arrays]
    return pl.pallas_call(
        kernel,
        name=name,
        out_shape=[jax.ShapeDtypeStruct(s, jnp.float32) for s in shapes],
        in_specs=[pl.BlockSpec(memory_space=pl.ANY)] * len(shear) + [hbm if in_hbm else vmem] * len(arrays),
        out_specs=[hbm if out_hbm else vmem] * len(shapes),
        scratch_shapes=[pltpu.VMEM(s, jnp.float32) if isinstance(s, tuple) else s for s in scratch],
        input_output_aliases=aliases or {},
        compiler_params=pltpu.CompilerParams(vmem_limit_bytes=20 * 1024 * 1024),
    )(*shear, *arrays)


def exchange(even, odd, swap):
    count_x, count_y = lax.axis_size("gx"), lax.axis_size("gy")

    def pairs(start):
        ends = [(i, (i + 1) % count_y) for i in range(start, count_y, 2)]
        return ends + [(j, i) for i, j in ends]

    even, odd = lax.ppermute(even, "gy", pairs(0)), lax.ppermute(odd, "gy", pairs(1))
    if len(swap) == 1:
        return even, odd, lax.ppermute(swap[0], "gx", [(0, 1), (1, 0)])
    x_low = lax.ppermute(swap[1], "gx", [(i, i + 1) for i in range(count_x - 1)])
    x_high = lax.ppermute(swap[0], "gx", [(i + 1, i) for i in range(count_x - 1)])
    return even, odd, x_low, x_high


def crossing(by, shear):
    count_x, count_y = lax.axis_size("gx"), lax.axis_size("gy")
    last = (count_x - 1) * count_y
    pairs = []
    for gy in range(count_y):
        pairs.append((last + gy, (gy + by) % count_y))
        pairs.append((gy, last + (gy - by) % count_y))
    return lax.ppermute(shear, ("gx", "gy"), pairs)


def inner_scratch(full):
    high, width = full[2:]
    tile = (FIELDS, high, width)
    padded = (FIELDS, high + 2 * PAD, width)
    column = (FIELDS, PAD + width, width)
    return [padded] * 3 + [tile] * 4 + [column] * 3


def edge_scratch(full, groups):
    high, width = full[2:]
    return [
        (FIELDS, 5, 2 * groups, width),
        (FIELDS, 2, 2 * groups, width),
        (FIELDS, groups, 2 * PAD, width),
        (2, FIELDS, 5, high, width),
        (FIELDS, 2, high, width),
        pltpu.SMEM((2,), jnp.int32),
        pltpu.SemaphoreType.DMA,
    ]


def sections(block, drift, w0, wt0, cols, even, odd, rows, shear, *swap):
    full, turned = w0.shape, wt0.shape
    groups = cols.shape[1] // 6
    sends = [x.shape for x in (cols, even, odd, rows, shear, *swap)]
    scratch = edge_scratch(full, groups)
    received = [(2,) + even.shape, (2 + (1 if len(swap) == 1 else 2),) + shear.shape]

    def branch(by):
        def run(drift, w0, wt0, cols, even, odd, rows, shear, *swap):
            even, odd, *beside = exchange(even, odd, swap)
            sheared = crossing(by, shear), crossing(by + 1, shear)
            kernel = functools.partial(interior_kernel, False)
            (vt,) = call(kernel, "inner_1", [w0, wt0], [turned], [full] + inner_scratch(full))
            wt1, cols, even, odd, rows, shear, *swap = call(
                functools.partial(edge_kernel, False, len(beside)),
                "edge_1",
                [vt, rows, cols, even, odd, *sheared, *beside],
                [turned] + sends,
                scratch,
                aliases={1: 0},
                shear=[drift],
            )
            even, odd, *beside = exchange(even, odd, swap)
            sheared = crossing(by, shear), crossing(by + 1, shear)
            kernel = functools.partial(interior_kernel, True)
            v, dy = call(kernel, "inner_2", [wt1, w0], [full, turned], [full] + inner_scratch(full))
            ends, slabs = call(gather_kernel, "gather", [even, odd, *sheared, *beside], received)
            return v, dy, rows, cols, ends, slabs

        return run

    branches = [branch(by) for by in range(lax.axis_size("gy"))]
    arrays = lax.switch(block, branches, drift, w0, wt0, cols, even, odd, rows, shear, *swap)
    (out,) = call(
        functools.partial(edge_kernel, True, received[1][0] - 2),
        "edge_2",
        arrays,
        [full],
        scratch[:-2] + [full, pltpu.SemaphoreType.DMA((2 * groups,))] + scratch[-2:],
        out_hbm=True,
        shear=[drift],
    )
    return out


def on_device(density, velocity, bfield, pressure, shear_shift, remap_weight):
    rows, high, width = density.shape
    count_x = lax.axis_size("gx")
    drift = jnp.stack([shear_shift, remap_weight])
    full = (FIELDS, rows, high, width)
    slab = (FIELDS, 2, high, width)
    groups = rows * high // width
    turned = (FIELDS, groups + 1, width + 2 * PAD, width)
    ends = (FIELDS, 2 * groups, width)
    sends = [(FIELDS, 6 * groups, width), ends, ends, (FIELDS, 6, high, width)]
    sends += [slab] * (2 if count_x == 2 else 3)
    start_state = call(
        prepare_kernel,
        "prepare",
        [density, velocity, bfield, pressure],
        [full, turned] + sends,
        [pltpu.SemaphoreType.DMA((4, groups))],
        in_hbm=True,
    )
    return sections(shear_shift // width, drift, *start_state)


def solution(mesh):
    placed = (
        P("gx", None, "gy"),
        P(None, "gx", None, "gy"),
        P(None, "gx", None, "gy"),
        P("gx", None, "gy"),
        P(),
        P(),
    )
    return jax.shard_map(
        on_device, mesh=mesh, in_specs=placed, out_specs=P(None, "gx", None, "gy"), check_vma=False
    )
```

```python
import functools

import jax
import jax.numpy as jnp
from jax import lax
from jax.experimental import pallas as pl
from jax.experimental.pallas import tpu as pltpu
from jax.sharding import PartitionSpec as P

GAMMA = 5.0 / 3.0
SHEAR_Q = 1.5
TIME_STEP = 0.03
WEIGHT_SCALE = 1.0 / 65536.0
TINY = 1e-30
FIELDS = 8
PAD = 8


def root(x):
    return x * lax.rsqrt(jnp.maximum(x, TINY))


def signal(state, normal):
    rho, pressure, vn = state[0], state[7], state[1 + normal]
    one, two = [4 + c for c in range(3) if c != normal]
    bn2 = state[4 + normal] * state[4 + normal]
    bt2 = state[one] * state[one] + state[two] * state[two]
    half_b2 = 0.5 * (bt2 + bn2)
    half_gp = (0.5 * GAMMA) * pressure
    spread = half_gp - half_b2
    disc = spread * spread + (GAMMA * pressure) * bt2
    fast = (half_gp + half_b2) + root(disc)
    return jnp.abs(vn) + fast * lax.rsqrt(jnp.maximum(rho * fast, TINY)), bn2 - half_b2


def carried(state, normal, speed, excess):
    rho, pressure = state[0], state[7]
    vel, mag = state[1:4], state[4:7]
    one, two = [c for c in range(3) if c != normal]
    vn, bn = vel[normal], mag[normal]
    pace = vn + speed
    mass = rho * pace
    inner = (0.5 * rho) * (vn * vn + vel[one] * vel[one] + vel[two] * vel[two]) + 1.5 * pressure
    out = [None] * FIELDS
    out[0] = mass
    out[1 + normal] = mass * vn + (pressure - excess)
    out[1 + one] = mass * vel[one] - bn * mag[one]
    out[1 + two] = mass * vel[two] - bn * mag[two]
    out[4 + one] = pace * mag[one] - bn * vel[one]
    out[4 + two] = pace * mag[two] - bn * vel[two]
    work = (pace * inner + vn * pressure) + speed * excess
    out[7] = work + (mag[one] * out[4 + one] + mag[two] * out[4 + two])
    return out


def face(left, right, normal):
    speed_left, excess_left = signal(left, normal)
    speed_right, excess_right = signal(right, normal)
    speed = jnp.maximum(speed_left, speed_right)
    one = carried(left, normal, speed, excess_left)
    two = carried(right, normal, -speed, excess_right)
    field = 4 + normal
    return [speed * (left[f] - right[f]) if f == field else one[f] + two[f] for f in range(FIELDS)]


def limited(up, down):
    return jnp.maximum(jnp.minimum(up, down), jnp.minimum(jnp.maximum(up, down), 0.0))


def to_conserved(w):
    rho = w[0]
    mom = [rho * v for v in w[1:4]]
    kinetic = 0.5 * (mom[0] * w[1] + mom[1] * w[2] + mom[2] * w[3])
    magnetic = 0.5 * (w[4] * w[4] + w[5] * w[5] + w[6] * w[6])
    return [rho] + mom + list(w[4:7]) + [1.5 * w[7] + kinetic + magnetic]


def to_primitive(u):
    inverse = 1.0 / u[0]
    vel = [m * inverse for m in u[1:4]]
    kinetic = 0.5 * (u[1] * vel[0] + u[2] * vel[1] + u[3] * vel[2])
    magnetic = 0.5 * (u[4] * u[4] + u[5] * u[5] + u[6] * u[6])
    return [u[0]] + vel + list(u[4:7]) + [(GAMMA - 1.0) * (u[7] - kinetic - magnetic)]


def whereabouts(rows):
    count_x = lax.axis_size("gx")
    row = lax.axis_index("gx")
    total = rows * count_x
    radial = (row * rows).astype(jnp.float32) + (0.5 - 0.5 * total)
    return radial, 1.0 / (SHEAR_Q * total), row == 0, row == count_x - 1


def at_even_block():
    return lax.rem(lax.axis_index("gy"), 2) == 0


def lanes_of(shape):
    return lax.broadcasted_iota(jnp.int32, shape, 1)


def load_row(ref, i):
    return [ref[f, i] for f in range(FIELDS)]


def turn(w_ref, f, g, wt_ref):
    high, width = w_ref.shape[2:]
    size = width // high
    tile = w_ref[f, pl.ds(g * size, size)].reshape(width, width)
    wt_ref[f, g, PAD : PAD + width] = tile.T


def pad_ends(wt_ref, f, g):
    rows = wt_ref.shape[2]
    wt_ref[f, g, 0:PAD] = wt_ref[f, g, PAD : 2 * PAD]
    wt_ref[f, g, rows - PAD : rows] = wt_ref[f, g, rows - 2 * PAD : rows - PAD]


def send_columns(groups, wt_ref, cols_ref, even_ref, odd_ref):
    rows = wt_ref.shape[2]
    even = at_even_block()
    cells = [PAD, PAD + 1, PAD + 2, rows - PAD - 3, rows - PAD - 2, rows - PAD - 1]

    def body(f, carry):
        for g in range(groups):
            for k, cell in enumerate(cells):
                cols_ref[f, k * groups + g : k * groups + g + 1] = wt_ref[f, g, cell : cell + 1]
            pad_ends(wt_ref, f, g)
        first, last = cols_ref[f, 0 : 2 * groups], cols_ref[f, 4 * groups : 6 * groups]
        even_ref[f] = jnp.where(even, last, first)
        odd_ref[f] = jnp.where(even, first, last)
        return carry

    lax.fori_loop(0, FIELDS, body, 0)


def send_rows(rows, rows_ref, shear_ref, *swap_refs):
    _, _, first, _ = whereabouts(rows)

    def body(k, carry):
        low, high = load_row(rows_ref, k), load_row(rows_ref, 4 + k)
        if len(swap_refs) == 1:
            for f in range(FIELDS):
                swap_refs[0][f, k] = jnp.where(first, high[f], low[f])
        else:
            for f in range(FIELDS):
                swap_refs[0][f, k] = low[f]
                swap_refs[1][f, k] = high[f]
        outer = to_conserved([jnp.where(first, low[f], high[f]) for f in range(FIELDS)])
        for f in range(FIELDS):
            shear_ref[f, k] = outer[f]
        return carry

    lax.fori_loop(0, 2, body, 0)


def prepare_kernel(rho_hbm, vel_hbm, mag_hbm, pres_hbm, w_ref, wt_ref, cols_ref, even_ref, odd_ref, rows_ref, *rest):
    *sends, sems = rest
    rows = w_ref.shape[1]
    radial, omega, _, _ = whereabouts(rows)
    parts = sems.shape[1]
    size = rows // parts
    copies = []
    for part in range(parts):
        at = pl.ds(part * size, size)
        copies.append(
            [
                pltpu.make_async_copy(rho_hbm.at[at], w_ref.at[0, at], sems.at[0, part]),
                pltpu.make_async_copy(vel_hbm.at[:, at], w_ref.at[pl.ds(1, 3), at], sems.at[1, part]),
                pltpu.make_async_copy(mag_hbm.at[:, at], w_ref.at[pl.ds(4, 3), at], sems.at[2, part]),
                pltpu.make_async_copy(pres_hbm.at[at], w_ref.at[7, at], sems.at[3, part]),
            ]
        )
        for copy in copies[-1]:
            copy.start()
    for part in range(parts):
        for copy in copies[part]:
            copy.wait()
        for i in range(part * size, (part + 1) * size):
            w_ref[2, i] = w_ref[2, i] - (SHEAR_Q * omega) * (radial + float(i))
        for f in range(FIELDS):
            turn(w_ref, f, part, wt_ref)
    send_columns(parts, wt_ref, cols_ref, even_ref, odd_ref)

    def copy(f, carry):
        rows_ref[f, 0:3] = w_ref[f, 0:3]
        rows_ref[f, 3:6] = w_ref[f, rows - 3 : rows]
        return carry

    lax.fori_loop(0, FIELDS, copy, 0)
    send_rows(rows, rows_ref, *sends)


def three_states(cells):
    left, right = [], []
    for f in range(FIELDS):
        before, here, after = (c[f] for c in cells)
        slope = limited(0.5 * (after - here), 0.5 * (here - before))
        left.append(here + slope)
        right.append(here - slope)
    return left, right


def wrapped(ref, f, value, before, after):
    high = value.shape[0]
    ref[f, 8 : 8 + high] = value
    if before:
        ref[f, 0:8] = value[high - 8 : high]
    if after:
        ref[f, 8 + high : 16 + high] = value[0:8]


def behind(ref, f, at, value):
    ref[f, pl.ds(at, value.shape[0])] = value
    return ref[f, pl.ds(at - 1, value.shape[0])]


def interior_kernel(second, *refs):
    if second:
        wt_ref, w0_ref, v_ref, dy_ref, w_ref, *refs = refs
    else:
        w_ref, wt_ref, vt_ref, v_ref, *refs = refs
        dy_ref = vt_ref
    hz_ref, rz_ref, fz_ref, wl_ref, dx_ref, fx_ref, half_ref, uy_ref, ly_ref, fy_ref, ry_ref = refs
    rows, high, width = w_ref.shape[1:]
    per_group = width // high
    groups = rows // per_group
    step = 0.5 * TIME_STEP if second else TIME_STEP
    coef = 0.5 * step
    radial, omega, _, _ = whereabouts(rows)
    next_row, last_row = slice(9, 9 + high), slice(7, 7 + high)
    early = per_group + 1

    def turn_result(m):
        g, f = lax.div(m, FIELDS), lax.rem(m, FIELDS)
        tile = v_ref[f, pl.ds(jnp.minimum(g, groups - 1) * per_group, per_group)].reshape(width, width)
        vt_ref[f, jnp.minimum(g, groups), PAD : PAD + width] = tile.T

    def turn_state(m):
        g, f = lax.div(m, FIELDS), lax.rem(m, FIELDS)
        tile = wt_ref[f, g, PAD : PAD + width].T
        w_ref[f, pl.ds(g * per_group, per_group)] = tile.reshape(per_group, high, width)

    def body(i, carry):
        if not second:
            turn_result(jnp.maximum(i - early, 0))
        w = load_row(w_ref, i)
        half = [half_ref[f] for f in range(FIELDS)]

        after, before = jnp.minimum(i + 1, rows - 1), jnp.maximum(i - 1, 0)
        right, wl = [], [wl_ref[f] for f in range(FIELDS)]
        for f in range(FIELDS):
            half_after = 0.5 * w_ref[f, after]
            half_ref[f] = half_after
            up = half_after - half[f]
            slope = limited(up, dx_ref[f])
            dx_ref[f] = up
            wl_ref[f] = w[f] + slope
            right.append(w[f] - slope)
        fx = face(wl, right, 0)
        scale = jnp.where(jnp.logical_and(i >= 2, i <= rows - 2), coef, 0.0)
        for f in range(FIELDS):
            here = scale * fx[f]
            v_ref[f, before] = v_ref[f, before] - (here - fx_ref[f])
            fx_ref[f] = here

        left = []
        w = load_row(w_ref, i)
        for f in range(FIELDS):
            wrapped(hz_ref, f, half[f], True, True)
            slope = limited(hz_ref[f, next_row] - half[f], half[f] - hz_ref[f, last_row])
            left.append(w[f] + slope)
            wrapped(rz_ref, f, w[f] - slope, False, True)
        fz = face(left, [rz_ref[f, next_row] for f in range(FIELDS)], 2)
        total = []
        for f in range(FIELDS):
            wrapped(fz_ref, f, fz[f], True, False)
            total.append(fz[f] - fz_ref[f, last_row])

        x = radial + i.astype(jnp.float32)
        cons = to_conserved(w)
        if second:
            base = [0.5 * (a + b) for a, b in zip(to_conserved(load_row(w0_ref, i)), cons)]
        else:
            base = cons
        tidal = (2.0 * SHEAR_Q * omega * omega) * x
        value = [base[f] - coef * total[f] for f in range(FIELDS)]
        value[1] = value[1] + ((step * 2.0) * omega * cons[2] + (step * tidal) * cons[0])
        value[2] = value[2] - ((step * 2.0) * omega) * cons[1]
        value[7] = value[7] + (step * tidal) * cons[1]
        for f in range(FIELDS):
            v_ref[f, i] = value[f]
        return carry

    size = 2 * groups * width // rows
    strips = width // size
    row = lax.broadcasted_iota(jnp.int32, (size // 2, width), 0)

    def body_y(n, carry):
        for m in (2 * n, 2 * n + 1):
            if second:
                turn_state(m)
            else:
                turn_result(rows - early + m)
        g, start = lax.div(n, strips), size * lax.rem(n, strips)
        at = pl.multiple_of(start + PAD, 8)
        for f in range(FIELDS):
            w = wt_ref[f, g, pl.ds(at, size)]
            up = 0.5 * (wt_ref[f, g, pl.ds(at + 1, size)] - w)
            slope = limited(up, behind(uy_ref, f, at, up))
            ly_ref[f, pl.ds(at, size)] = w + slope
            ry_ref[f] = w - slope
        for part in range(2):
            half = size // 2
            to = at + part * half
            left = [ly_ref[f, pl.ds(to - 1, half)] for f in range(FIELDS)]
            right = [ry_ref[f, part * half : (part + 1) * half] for f in range(FIELDS)]
            fy = face(left, right, 1)
            cell = row + (start + part * half)
            scale = jnp.where(jnp.logical_and(cell >= 2, cell <= width - 2), coef, 0.0)
            for f in range(FIELDS):
                here = scale * fy[f]
                change = here - behind(fy_ref, f, to, here)
                if second:
                    dy_ref[f, g, pl.ds(to - 1, half)] = change
                else:
                    vt_ref[f, g, pl.ds(to - 1, half)] = vt_ref[f, g, pl.ds(to - 1, half)] - change
        return carry

    def azimuthal():
        for f in range(FIELDS):
            uy_ref[f, 0:PAD] = jnp.zeros((PAD, width), jnp.float32)
            ly_ref[f, 0:PAD] = wt_ref[f, 0, PAD : 2 * PAD]
            fy_ref[f, 0:PAD] = jnp.zeros((PAD, width), jnp.float32)
        lax.fori_loop(0, rows // 2, body_y, 0)

    def others():
        for f in range(FIELDS):
            blank = jnp.zeros((high, width), jnp.float32)
            dx_ref[f], fx_ref[f], wl_ref[f] = blank, blank, w_ref[f, 0]
            half_ref[f] = 0.5 * w_ref[f, 0]
        lax.fori_loop(0, rows, body, 0)

    if second:
        azimuthal()
        others()
        for f in range(FIELDS):
            for g in range(groups):
                dy_ref[f, g, PAD + width - 1 : PAD + width] = jnp.zeros((1, width), jnp.float32)
    else:
        others()
        azimuthal()


def sheared_rows(first, shear_ref, near_ref, next_ref, ghost_ref):
    high, width = near_ref.shape[2:]
    rest = lax.rem(shear_ref[0], width)
    start = jnp.where(first, width - 1 - rest, rest)
    back = lax.rem(width - start, width)
    weight = shear_ref[1].astype(jnp.float32) * WEIGHT_SCALE
    other = 1.0 - weight
    ahead = jnp.where(first, 1.0 - weight, 1.0 - other)
    here = jnp.where(first, weight, other)
    delta = jnp.where(first, 1.0, -1.0)
    lane = lanes_of((high, width))

    for k in range(2):
        ghost = []
        for f in range(FIELDS):
            near, following = near_ref[f, k], next_ref[f, k]
            one = jnp.where(first, following, near)
            two = jnp.where(first, near, following)
            two = pltpu.roll(two, back, 1)
            one = jnp.where(lane < width - start, pltpu.roll(one, back, 1), two)
            two = pltpu.roll(jnp.where(lane == 0, two, one), width - 1, 1)
            ghost.append(ahead * two + here * one)
        boosted = list(ghost)
        boosted[2] = ghost[2] + ghost[0] * delta
        boosted[7] = ghost[7] + ghost[2] * delta + 0.5 * ghost[0] * delta * delta
        prim = to_primitive(boosted)
        for f in range(FIELDS):
            ghost_ref[f, k] = prim[f]


def in_loop(count, body):
    lax.fori_loop(0, count, body, 0)


def unrolled(count, body):
    for n in range(count):
        body(n, 0)


def edge_kernel(second, beside, shear_any, *refs):
    *refs, shear_smem, shear_sem = refs
    shear_copy = pltpu.make_async_copy(shear_any, shear_smem, shear_sem)
    shear_copy.start()
    if second:
        v_ref, dy_ref, rows_ref, cols_ref, ends_ref, slabs_ref, out_hbm, *refs = refs
        e_ref, a_ref, c_ref, x_ref, ghost_ref, out_ref, sems = refs
        even_ref, odd_ref = ends_ref.at[0], ends_ref.at[1]
        near_ref, next_ref, xl_ref, xr_ref = (slabs_ref.at[k] for k in (0, 1, 2, 1 + beside))
    else:
        vt_ref, rows_ref, cols_ref, even_ref, odd_ref, near_ref, next_ref, *refs = refs
        xl_ref, xr_ref = refs[0], refs[beside - 1]
        w1_ref, cols1_ref, even1_ref, odd1_ref, rows1_ref, *sends, e_ref, a_ref, c_ref, x_ref, ghost_ref = refs[beside:]
    high, width = rows_ref.shape[2:]
    groups = cols_ref.shape[1] // 6
    size = width // high
    rows = groups * size
    step = 0.5 * TIME_STEP if second else TIME_STEP
    coef = 0.5 * step
    _, _, first, last = whereabouts(rows)
    even = at_even_block()
    loop = unrolled if second else in_loop

    def gather(f, carry):
        for k in range(2):
            at = slice(k * groups, (k + 1) * groups)
            e_ref[f, k, 0:groups] = jnp.where(even, odd_ref[f, at], even_ref[f, at])
            e_ref[f, 3 + k, groups : 2 * groups] = jnp.where(even, even_ref[f, at], odd_ref[f, at])
        for k in range(3):
            e_ref[f, 2 + k, 0:groups] = cols_ref[f, k * groups : (k + 1) * groups]
            e_ref[f, k, groups : 2 * groups] = cols_ref[f, (3 + k) * groups : (4 + k) * groups]
        return carry

    lax.fori_loop(0, FIELDS, gather, 0)
    shear_copy.wait()
    sheared_rows(first, shear_smem, near_ref, next_ref, ghost_ref)
    cells = [[e_ref[f, k] for f in range(FIELDS)] for k in range(5)]
    sides = [three_states(cells[k : k + 3]) for k in range(3)]
    one = face(sides[0][0], sides[1][1], 1)
    two = face(sides[1][0], sides[2][1], 1)
    low_end = lax.broadcasted_iota(jnp.int32, one[0].shape, 0) < groups
    for f in range(FIELDS):
        a_ref[f, 0] = coef * (two[f] - one[f])
        a_ref[f, 1] = coef * jnp.where(low_end, -two[f], one[f])

    if second:

        def scatter(f, carry):
            for g in range(groups):
                c_ref[f, g] = jnp.zeros((2 * PAD, width), jnp.float32)
                c_ref[f, g, 0:1] = a_ref[f, 0, g : g + 1]
                c_ref[f, g, 1:2] = a_ref[f, 1, g : g + 1]
                c_ref[f, g, 2 * PAD - 2 : 2 * PAD - 1] = a_ref[f, 1, groups + g : groups + g + 1]
                c_ref[f, g, 2 * PAD - 1 : 2 * PAD] = a_ref[f, 0, groups + g : groups + g + 1]
            return carry

        lax.fori_loop(0, FIELDS, scatter, 0)

    def place(f, carry):
        x_ref[0, f, 0:2] = jnp.where(first, ghost_ref[f], xl_ref[f])
        x_ref[1, f, 3:5] = jnp.where(last, ghost_ref[f], xr_ref[f])
        x_ref[0, f, 2:5] = rows_ref[f, 0:3]
        x_ref[1, f, 0:3] = rows_ref[f, 3:6]
        return carry

    lax.fori_loop(0, FIELDS, place, 0)

    def radial(n, carry):
        if second:
            end, at = n // 2, pl.ds(n % 2 * (high // 2), high // 2)
        else:
            end, at = lax.div(n, 2), pl.ds(pl.multiple_of(lax.rem(n, 2) * (high // 2), 8), high // 2)
        cells = [[x_ref[end, f, k, at] for f in range(FIELDS)] for k in range(5)]
        sides = [three_states(cells[k : k + 3]) for k in range(3)]
        one = face(sides[0][0], sides[1][1], 0)
        two = face(sides[1][0], sides[2][1], 0)
        for f in range(FIELDS):
            x_ref[end, f, 0, at] = coef * (two[f] - one[f])
            x_ref[end, f, 1, at] = coef * jnp.where(end == 0, -two[f], one[f])
        return carry

    loop(4, radial)
    batch = FIELDS // 4

    if not second:
        lane = lanes_of((width, width))

        def correct(n, carry):
            for k in range(batch):
                f = n * batch + k
                strip = [x_ref[0, f, 0], x_ref[0, f, 1], jnp.zeros((width - 4 * high, width), jnp.float32)]
                strip = jnp.concatenate(strip + [x_ref[1, f, 1], x_ref[1, f, 0]], axis=0).T
                at = slice(PAD, PAD + width)
                w1_ref[f, 0, at] = vt_ref[f, 0, at] - jnp.where(lane < width // 2, strip, 0.0)
                w1_ref[f, groups - 1, at] = vt_ref[f, groups - 1, at] - jnp.where(lane < width // 2, 0.0, strip)
            return carry

        lax.fori_loop(0, FIELDS // batch, correct, 0)

        def correct_rows(f, carry):
            for g in range(groups):
                places = [(0, 0, g), (1, 1, g), (width - 2, 1, groups + g), (width - 1, 0, groups + g)]
                for to, kind, at in places:
                    to = slice(PAD + to, PAD + to + 1)
                    w1_ref[f, g, to] = w1_ref[f, g, to] - a_ref[f, kind, at : at + 1]
            return carry

        lax.fori_loop(0, FIELDS, correct_rows, 0)
        block = width // 2

        def primitives(n, carry):
            g, at = lax.div(n, 2), pl.ds(pl.multiple_of(PAD + block * lax.rem(n, 2), 8), block)
            prim = to_primitive([w1_ref[f, g, at] for f in range(FIELDS)])
            for f in range(FIELDS):
                w1_ref[f, g, at] = prim[f]
            return carry

        lax.fori_loop(0, 2 * groups, primitives, 0)

        def turn_rows(n, carry):
            for k in range(batch):
                f = n * batch + k
                at = slice(PAD, PAD + width)
                strip = jnp.where(lane < width // 2, w1_ref[f, 0, at], w1_ref[f, groups - 1, at]).T
                rows1_ref[f, 0:3] = strip[0 : 3 * high].reshape(3, high, width)
                rows1_ref[f, 3:6] = strip[width - 3 * high : width].reshape(3, high, width)
            return carry

        lax.fori_loop(0, FIELDS // batch, turn_rows, 0)
        send_columns(groups, w1_ref, cols1_ref, even1_ref, odd1_ref)
        send_rows(rows, rows1_ref, *sends)
        return

    batch = FIELDS // 2
    copies = []
    for g in [*range(1, groups - 1), 0, groups - 1]:
        at = pl.ds(g * size, size)
        for half in range(2):
            for f in range(half * batch, (half + 1) * batch):
                head = dy_ref[f, g, PAD : 2 * PAD] + c_ref[f, g, 0:PAD]
                tail = dy_ref[f, g, width : PAD + width] + c_ref[f, g, PAD : 2 * PAD]
                strip = jnp.concatenate([head, dy_ref[f, g, 2 * PAD : width], tail], axis=0)
                strip = strip.T.reshape(size, high, width)
                value = [v_ref[f, g * size + i] - strip[i] for i in range(size)]
                if g == 0:
                    value[0], value[1] = value[0] - x_ref[0, f, 0], value[1] - x_ref[0, f, 1]
                if g == groups - 1:
                    value[-1], value[-2] = value[-1] - x_ref[1, f, 0], value[-2] - x_ref[1, f, 1]
                for i in range(size):
                    out_ref[f, g * size + i] = value[i]
            part = pl.ds(half * batch, batch)
            copy = pltpu.make_async_copy(out_ref.at[part, at], out_hbm.at[part, at], sems.at[len(copies)])
            copy.start()
            copies.append(copy)
    for copy in copies:
        copy.wait()


def gather_kernel(even_ref, odd_ref, *refs):
    *slabs, ends_ref, slabs_ref = refs

    def body(f, carry):
        ends_ref[0, f], ends_ref[1, f] = even_ref[f], odd_ref[f]
        for k, ref in enumerate(slabs):
            slabs_ref[k, f] = ref[f]
        return carry

    lax.fori_loop(0, FIELDS, body, 0)


def call(kernel, name, arrays, shapes, scratch=(), in_hbm=False, out_hbm=False, aliases=None, shear=()):
    vmem = pl.BlockSpec(memory_space=pltpu.VMEM)
    hbm = pl.BlockSpec(memory_space=pltpu.HBM)
    if in_hbm:
        arrays = [pltpu.with_memory_space_constraint(x, pltpu.HBM) for x in arrays]
    return pl.pallas_call(
        kernel,
        name=name,
        out_shape=[jax.ShapeDtypeStruct(s, jnp.float32) for s in shapes],
        in_specs=[pl.BlockSpec(memory_space=pl.ANY)] * len(shear) + [hbm if in_hbm else vmem] * len(arrays),
        out_specs=[hbm if out_hbm else vmem] * len(shapes),
        scratch_shapes=[pltpu.VMEM(s, jnp.float32) if isinstance(s, tuple) else s for s in scratch],
        input_output_aliases=aliases or {},
        compiler_params=pltpu.CompilerParams(vmem_limit_bytes=20 * 1024 * 1024),
    )(*shear, *arrays)


def exchange(even, odd, swap):
    count_x, count_y = lax.axis_size("gx"), lax.axis_size("gy")

    def pairs(start):
        ends = [(i, (i + 1) % count_y) for i in range(start, count_y, 2)]
        return ends + [(j, i) for i, j in ends]

    even, odd = lax.ppermute(even, "gy", pairs(0)), lax.ppermute(odd, "gy", pairs(1))
    if len(swap) == 1:
        return even, odd, lax.ppermute(swap[0], "gx", [(0, 1), (1, 0)])
    x_low = lax.ppermute(swap[1], "gx", [(i, i + 1) for i in range(count_x - 1)])
    x_high = lax.ppermute(swap[0], "gx", [(i + 1, i) for i in range(count_x - 1)])
    return even, odd, x_low, x_high


def crossing(by, shear):
    count_x, count_y = lax.axis_size("gx"), lax.axis_size("gy")
    last = (count_x - 1) * count_y
    pairs = []
    for gy in range(count_y):
        pairs.append((last + gy, (gy + by) % count_y))
        pairs.append((gy, last + (gy - by) % count_y))
    return lax.ppermute(shear, ("gx", "gy"), pairs)


def inner_scratch(full):
    high, width = full[2:]
    tile = (FIELDS, high, width)
    padded = (FIELDS, high + 2 * PAD, width)
    column = (FIELDS, PAD + width, width)
    return [padded] * 3 + [tile] * 4 + [column] * 3 + [(FIELDS, 2 * high, width)]


def edge_scratch(full, groups):
    high, width = full[2:]
    return [
        (FIELDS, 5, 2 * groups, width),
        (FIELDS, 2, 2 * groups, width),
        (FIELDS, groups, 2 * PAD, width),
        (2, FIELDS, 5, high, width),
        (FIELDS, 2, high, width),
        pltpu.SMEM((2,), jnp.int32),
        pltpu.SemaphoreType.DMA,
    ]


def sections(block, drift, w0, wt0, cols, even, odd, rows, shear, *swap):
    full, turned = w0.shape, wt0.shape
    groups = cols.shape[1] // 6
    sends = [x.shape for x in (cols, even, odd, rows, shear, *swap)]
    scratch = edge_scratch(full, groups)
    received = [(2,) + even.shape, (2 + (1 if len(swap) == 1 else 2),) + shear.shape]

    def branch(by):
        def run(drift, w0, wt0, cols, even, odd, rows, shear, *swap):
            even, odd, *beside = exchange(even, odd, swap)
            sheared = crossing(by, shear), crossing(by + 1, shear)
            kernel = functools.partial(interior_kernel, False)
            (vt,) = call(kernel, "inner_1", [w0, wt0], [turned], [full] + inner_scratch(full))
            wt1, cols, even, odd, rows, shear, *swap = call(
                functools.partial(edge_kernel, False, len(beside)),
                "edge_1",
                [vt, rows, cols, even, odd, *sheared, *beside],
                [turned] + sends,
                scratch,
                aliases={1: 0},
                shear=[drift],
            )
            even, odd, *beside = exchange(even, odd, swap)
            sheared = crossing(by, shear), crossing(by + 1, shear)
            kernel = functools.partial(interior_kernel, True)
            v, dy = call(kernel, "inner_2", [wt1, w0], [full, turned], [full] + inner_scratch(full))
            ends, slabs = call(gather_kernel, "gather", [even, odd, *sheared, *beside], received)
            return v, dy, rows, cols, ends, slabs

        return run

    branches = [branch(by) for by in range(lax.axis_size("gy"))]
    arrays = lax.switch(block, branches, drift, w0, wt0, cols, even, odd, rows, shear, *swap)
    (out,) = call(
        functools.partial(edge_kernel, True, received[1][0] - 2),
        "edge_2",
        arrays,
        [full],
        scratch[:-2] + [full, pltpu.SemaphoreType.DMA((2 * groups,))] + scratch[-2:],
        out_hbm=True,
        shear=[drift],
    )
    return out


def on_device(density, velocity, bfield, pressure, shear_shift, remap_weight):
    rows, high, width = density.shape
    count_x = lax.axis_size("gx")
    drift = jnp.stack([shear_shift, remap_weight])
    full = (FIELDS, rows, high, width)
    slab = (FIELDS, 2, high, width)
    groups = rows * high // width
    turned = (FIELDS, groups + 1, width + 2 * PAD, width)
    ends = (FIELDS, 2 * groups, width)
    sends = [(FIELDS, 6 * groups, width), ends, ends, (FIELDS, 6, high, width)]
    sends += [slab] * (2 if count_x == 2 else 3)
    start_state = call(
        prepare_kernel,
        "prepare",
        [density, velocity, bfield, pressure],
        [full, turned] + sends,
        [pltpu.SemaphoreType.DMA((4, groups))],
        in_hbm=True,
    )
    return sections(shear_shift // width, drift, *start_state)


def solution(mesh):
    placed = (
        P("gx", None, "gy"),
        P(None, "gx", None, "gy"),
        P(None, "gx", None, "gy"),
        P("gx", None, "gy"),
        P(),
        P(),
    )
    return jax.shard_map(
        on_device, mesh=mesh, in_specs=placed, out_specs=P(None, "gx", None, "gy"), check_vma=False
    )
```

```python
import functools

import jax
import jax.numpy as jnp
from jax import lax
from jax.experimental import pallas as pl
from jax.experimental.pallas import tpu as pltpu
from jax.sharding import PartitionSpec as P

GAMMA = 5.0 / 3.0
SHEAR_Q = 1.5
TIME_STEP = 0.03
WEIGHT_SCALE = 1.0 / 65536.0
TINY = 1e-30
FIELDS = 8
PAD = 8


def root(x):
    return x * lax.rsqrt(jnp.maximum(x, TINY))


def signal(state, normal):
    rho, pressure, vn = state[0], state[7], state[1 + normal]
    one, two = [4 + c for c in range(3) if c != normal]
    bn2 = state[4 + normal] * state[4 + normal]
    bt2 = state[one] * state[one] + state[two] * state[two]
    half_b2 = 0.5 * (bt2 + bn2)
    half_gp = (0.5 * GAMMA) * pressure
    spread = half_gp - half_b2
    disc = spread * spread + (GAMMA * pressure) * bt2
    fast = (half_gp + half_b2) + root(disc)
    return jnp.abs(vn) + fast * lax.rsqrt(jnp.maximum(rho * fast, TINY)), bn2 - half_b2


def carried(state, normal, speed, excess):
    rho, pressure = state[0], state[7]
    vel, mag = state[1:4], state[4:7]
    one, two = [c for c in range(3) if c != normal]
    vn, bn = vel[normal], mag[normal]
    pace = vn + speed
    mass = rho * pace
    inner = (0.5 * rho) * (vn * vn + vel[one] * vel[one] + vel[two] * vel[two]) + 1.5 * pressure
    out = [None] * FIELDS
    out[0] = mass
    out[1 + normal] = mass * vn + (pressure - excess)
    out[1 + one] = mass * vel[one] - bn * mag[one]
    out[1 + two] = mass * vel[two] - bn * mag[two]
    out[4 + one] = pace * mag[one] - bn * vel[one]
    out[4 + two] = pace * mag[two] - bn * vel[two]
    work = (pace * inner + vn * pressure) + speed * excess
    out[7] = work + (mag[one] * out[4 + one] + mag[two] * out[4 + two])
    return out


def face(left, right, normal):
    speed_left, excess_left = signal(left, normal)
    speed_right, excess_right = signal(right, normal)
    speed = jnp.maximum(speed_left, speed_right)
    one = carried(left, normal, speed, excess_left)
    two = carried(right, normal, -speed, excess_right)
    field = 4 + normal
    return [speed * (left[f] - right[f]) if f == field else one[f] + two[f] for f in range(FIELDS)]


def limited(up, down):
    return jnp.maximum(jnp.minimum(up, down), jnp.minimum(jnp.maximum(up, down), 0.0))


def to_conserved(w):
    rho = w[0]
    mom = [rho * v for v in w[1:4]]
    kinetic = 0.5 * (mom[0] * w[1] + mom[1] * w[2] + mom[2] * w[3])
    magnetic = 0.5 * (w[4] * w[4] + w[5] * w[5] + w[6] * w[6])
    return [rho] + mom + list(w[4:7]) + [1.5 * w[7] + kinetic + magnetic]


def to_primitive(u):
    inverse = 1.0 / u[0]
    vel = [m * inverse for m in u[1:4]]
    kinetic = 0.5 * (u[1] * vel[0] + u[2] * vel[1] + u[3] * vel[2])
    magnetic = 0.5 * (u[4] * u[4] + u[5] * u[5] + u[6] * u[6])
    return [u[0]] + vel + list(u[4:7]) + [(GAMMA - 1.0) * (u[7] - kinetic - magnetic)]


def whereabouts(rows):
    count_x = lax.axis_size("gx")
    row = lax.axis_index("gx")
    total = rows * count_x
    radial = (row * rows).astype(jnp.float32) + (0.5 - 0.5 * total)
    return radial, 1.0 / (SHEAR_Q * total), row == 0, row == count_x - 1


def at_even_block():
    return lax.rem(lax.axis_index("gy"), 2) == 0


def lanes_of(shape):
    return lax.broadcasted_iota(jnp.int32, shape, 1)


def load_row(ref, i):
    return [ref[f, i] for f in range(FIELDS)]


def turn(w_ref, f, g, wt_ref):
    high, width = w_ref.shape[2:]
    size = width // high
    tile = w_ref[f, pl.ds(g * size, size)].reshape(width, width)
    wt_ref[f, g, PAD : PAD + width] = tile.T


def pad_ends(wt_ref, f, g):
    rows = wt_ref.shape[2]
    wt_ref[f, g, 0:PAD] = wt_ref[f, g, PAD : 2 * PAD]
    wt_ref[f, g, rows - PAD : rows] = wt_ref[f, g, rows - 2 * PAD : rows - PAD]


def send_columns(groups, wt_ref, cols_ref, even_ref, odd_ref):
    rows = wt_ref.shape[2]
    even = at_even_block()
    cells = [PAD, PAD + 1, PAD + 2, rows - PAD - 3, rows - PAD - 2, rows - PAD - 1]

    def body(f, carry):
        for g in range(groups):
            for k, cell in enumerate(cells):
                cols_ref[f, k * groups + g : k * groups + g + 1] = wt_ref[f, g, cell : cell + 1]
            pad_ends(wt_ref, f, g)
        first, last = cols_ref[f, 0 : 2 * groups], cols_ref[f, 4 * groups : 6 * groups]
        even_ref[f] = jnp.where(even, last, first)
        odd_ref[f] = jnp.where(even, first, last)
        return carry

    lax.fori_loop(0, FIELDS, body, 0)


def send_rows(rows, rows_ref, shear_ref, *swap_refs):
    _, _, first, _ = whereabouts(rows)

    def body(k, carry):
        low, high = load_row(rows_ref, k), load_row(rows_ref, 4 + k)
        if len(swap_refs) == 1:
            for f in range(FIELDS):
                swap_refs[0][f, k] = jnp.where(first, high[f], low[f])
        else:
            for f in range(FIELDS):
                swap_refs[0][f, k] = low[f]
                swap_refs[1][f, k] = high[f]
        outer = to_conserved([jnp.where(first, low[f], high[f]) for f in range(FIELDS)])
        for f in range(FIELDS):
            shear_ref[f, k] = outer[f]
        return carry

    lax.fori_loop(0, 2, body, 0)


def prepare_kernel(rho_hbm, vel_hbm, mag_hbm, pres_hbm, w_ref, wt_ref, cols_ref, even_ref, odd_ref, rows_ref, *rest):
    *sends, sems = rest
    rows = w_ref.shape[1]
    radial, omega, _, _ = whereabouts(rows)
    parts = sems.shape[1]
    size = rows // parts
    copies = []
    for part in range(parts):
        at = pl.ds(part * size, size)
        copies.append(
            [
                pltpu.make_async_copy(rho_hbm.at[at], w_ref.at[0, at], sems.at[0, part]),
                pltpu.make_async_copy(vel_hbm.at[:, at], w_ref.at[pl.ds(1, 3), at], sems.at[1, part]),
                pltpu.make_async_copy(mag_hbm.at[:, at], w_ref.at[pl.ds(4, 3), at], sems.at[2, part]),
                pltpu.make_async_copy(pres_hbm.at[at], w_ref.at[7, at], sems.at[3, part]),
            ]
        )
        for copy in copies[-1]:
            copy.start()
    for part in range(parts):
        for copy in copies[part]:
            copy.wait()
        for i in range(part * size, (part + 1) * size):
            w_ref[2, i] = w_ref[2, i] - (SHEAR_Q * omega) * (radial + float(i))
        for f in range(FIELDS):
            turn(w_ref, f, part, wt_ref)
    send_columns(parts, wt_ref, cols_ref, even_ref, odd_ref)

    def copy(f, carry):
        rows_ref[f, 0:3] = w_ref[f, 0:3]
        rows_ref[f, 3:6] = w_ref[f, rows - 3 : rows]
        return carry

    lax.fori_loop(0, FIELDS, copy, 0)
    send_rows(rows, rows_ref, *sends)


def three_states(cells):
    left, right = [], []
    for f in range(FIELDS):
        before, here, after = (c[f] for c in cells)
        slope = limited(0.5 * (after - here), 0.5 * (here - before))
        left.append(here + slope)
        right.append(here - slope)
    return left, right


def wrapped(ref, f, value, before, after):
    high = value.shape[0]
    ref[f, 8 : 8 + high] = value
    if before:
        ref[f, 0:8] = value[high - 8 : high]
    if after:
        ref[f, 8 + high : 16 + high] = value[0:8]


def behind(ref, f, at, value):
    ref[f, pl.ds(at, value.shape[0])] = value
    return ref[f, pl.ds(at - 1, value.shape[0])]


def interior_kernel(second, *refs):
    if second:
        wt_ref, w0_ref, v_ref, dy_ref, w_ref, *refs = refs
    else:
        w_ref, wt_ref, vt_ref, v_ref, *refs = refs
        dy_ref = vt_ref
    hz_ref, rz_ref, fz_ref, wl_ref, dx_ref, fx_ref, half_ref, uy_ref, ly_ref, fy_ref, ry_ref = refs
    rows, high, width = w_ref.shape[1:]
    per_group = width // high
    groups = rows // per_group
    step = 0.5 * TIME_STEP if second else TIME_STEP
    coef = 0.5 * step
    radial, omega, _, _ = whereabouts(rows)
    next_row, last_row = slice(9, 9 + high), slice(7, 7 + high)
    early = per_group + 1

    def turn_result(m):
        g, f = lax.div(m, FIELDS), lax.rem(m, FIELDS)
        tile = v_ref[f, pl.ds(jnp.minimum(g, groups - 1) * per_group, per_group)].reshape(width, width)
        vt_ref[f, jnp.minimum(g, groups), PAD : PAD + width] = tile.T

    def turn_state(m):
        g, f = lax.div(m, FIELDS), lax.rem(m, FIELDS)
        tile = wt_ref[f, g, PAD : PAD + width].T
        w_ref[f, pl.ds(g * per_group, per_group)] = tile.reshape(per_group, high, width)

    def body(i, carry):
        if not second:
            turn_result(jnp.maximum(i - early, 0))
        w = load_row(w_ref, i)
        half = [half_ref[f] for f in range(FIELDS)]

        after, before = jnp.minimum(i + 1, rows - 1), jnp.maximum(i - 1, 0)
        right, wl = [], [wl_ref[f] for f in range(FIELDS)]
        for f in range(FIELDS):
            half_after = 0.5 * w_ref[f, after]
            half_ref[f] = half_after
            up = half_after - half[f]
            slope = limited(up, dx_ref[f])
            dx_ref[f] = up
            wl_ref[f] = w[f] + slope
            right.append(w[f] - slope)
        fx = face(wl, right, 0)
        scale = jnp.where(jnp.logical_and(i >= 2, i <= rows - 2), coef, 0.0)
        for f in range(FIELDS):
            here = scale * fx[f]
            v_ref[f, before] = v_ref[f, before] - (here - fx_ref[f])
            fx_ref[f] = here

        left = []
        w = load_row(w_ref, i)
        for f in range(FIELDS):
            wrapped(hz_ref, f, half[f], True, True)
            slope = limited(hz_ref[f, next_row] - half[f], half[f] - hz_ref[f, last_row])
            left.append(w[f] + slope)
            wrapped(rz_ref, f, w[f] - slope, False, True)
        fz = face(left, [rz_ref[f, next_row] for f in range(FIELDS)], 2)
        total = []
        for f in range(FIELDS):
            wrapped(fz_ref, f, fz[f], True, False)
            total.append(fz[f] - fz_ref[f, last_row])

        x = radial + i.astype(jnp.float32)
        cons = to_conserved(w)
        if second:
            base = [0.5 * (a + b) for a, b in zip(to_conserved(load_row(w0_ref, i)), cons)]
        else:
            base = cons
        tidal = (2.0 * SHEAR_Q * omega * omega) * x
        value = [base[f] - coef * total[f] for f in range(FIELDS)]
        value[1] = value[1] + ((step * 2.0) * omega * cons[2] + (step * tidal) * cons[0])
        value[2] = value[2] - ((step * 2.0) * omega) * cons[1]
        value[7] = value[7] + (step * tidal) * cons[1]
        for f in range(FIELDS):
            v_ref[f, i] = value[f]
        return carry

    size = 2 * groups * width // rows
    strips = width // size
    row = lax.broadcasted_iota(jnp.int32, (size // 2, width), 0)

    def body_y(n, carry):
        for m in (2 * n, 2 * n + 1):
            if second:
                turn_state(m)
            else:
                turn_result(rows - early + m)
        g, start = lax.div(n, strips), size * lax.rem(n, strips)
        at = pl.multiple_of(start + PAD, 8)
        for f in range(FIELDS):
            w = wt_ref[f, g, pl.ds(at, size)]
            up = 0.5 * (wt_ref[f, g, pl.ds(at + 1, size)] - w)
            slope = limited(up, behind(uy_ref, f, at, up))
            ly_ref[f, pl.ds(at, size)] = w + slope
            ry_ref[f] = w - slope
        for part in range(2):
            half = size // 2
            to = at + part * half
            left = [ly_ref[f, pl.ds(to - 1, half)] for f in range(FIELDS)]
            right = [ry_ref[f, part * half : (part + 1) * half] for f in range(FIELDS)]
            fy = face(left, right, 1)
            cell = row + (start + part * half)
            scale = jnp.where(jnp.logical_and(cell >= 2, cell <= width - 2), coef, 0.0)
            for f in range(FIELDS):
                here = scale * fy[f]
                change = here - behind(fy_ref, f, to, here)
                if second:
                    dy_ref[f, g, pl.ds(to - 1, half)] = change
                else:
                    vt_ref[f, g, pl.ds(to - 1, half)] = vt_ref[f, g, pl.ds(to - 1, half)] - change
        return carry

    def azimuthal():
        for f in range(FIELDS):
            uy_ref[f, 0:PAD] = jnp.zeros((PAD, width), jnp.float32)
            ly_ref[f, 0:PAD] = wt_ref[f, 0, PAD : 2 * PAD]
            fy_ref[f, 0:PAD] = jnp.zeros((PAD, width), jnp.float32)
        lax.fori_loop(0, rows // 2, body_y, 0)

    def others():
        for f in range(FIELDS):
            blank = jnp.zeros((high, width), jnp.float32)
            dx_ref[f], fx_ref[f], wl_ref[f] = blank, blank, w_ref[f, 0]
            half_ref[f] = 0.5 * w_ref[f, 0]
        lax.fori_loop(0, rows, body, 0)

    if second:
        azimuthal()
        others()
        for f in range(FIELDS):
            for g in range(groups):
                dy_ref[f, g, PAD + width - 1 : PAD + width] = jnp.zeros((1, width), jnp.float32)
    else:
        others()
        azimuthal()


def sheared_rows(first, shear_ref, near_ref, next_ref, ghost_ref):
    high, width = near_ref.shape[2:]
    rest = lax.rem(shear_ref[0], width)
    start = jnp.where(first, width - 1 - rest, rest)
    back = lax.rem(width - start, width)
    weight = shear_ref[1].astype(jnp.float32) * WEIGHT_SCALE
    other = 1.0 - weight
    ahead = jnp.where(first, 1.0 - weight, 1.0 - other)
    here = jnp.where(first, weight, other)
    delta = jnp.where(first, 1.0, -1.0)
    lane = lanes_of((high, width))

    for k in range(2):
        ghost = []
        for f in range(FIELDS):
            near, following = near_ref[f, k], next_ref[f, k]
            one = jnp.where(first, following, near)
            two = jnp.where(first, near, following)
            two = pltpu.roll(two, back, 1)
            one = jnp.where(lane < width - start, pltpu.roll(one, back, 1), two)
            two = pltpu.roll(jnp.where(lane == 0, two, one), width - 1, 1)
            ghost.append(ahead * two + here * one)
        boosted = list(ghost)
        boosted[2] = ghost[2] + ghost[0] * delta
        boosted[7] = ghost[7] + ghost[2] * delta + 0.5 * ghost[0] * delta * delta
        prim = to_primitive(boosted)
        for f in range(FIELDS):
            ghost_ref[f, k] = prim[f]


def in_loop(count, body):
    lax.fori_loop(0, count, body, 0)


def unrolled(count, body):
    for n in range(count):
        body(n, 0)


def edge_kernel(second, beside, shear_any, *refs):
    *refs, shear_smem, shear_sem = refs
    shear_copy = pltpu.make_async_copy(shear_any, shear_smem, shear_sem)
    shear_copy.start()
    if second:
        v_ref, dy_ref, rows_ref, cols_ref, ends_ref, slabs_ref, out_hbm, *refs = refs
        e_ref, a_ref, c_ref, x_ref, ghost_ref, out_ref, sems = refs
        even_ref, odd_ref = ends_ref.at[0], ends_ref.at[1]
        near_ref, next_ref, xl_ref, xr_ref = (slabs_ref.at[k] for k in (0, 1, 2, 1 + beside))
    else:
        vt_ref, rows_ref, cols_ref, even_ref, odd_ref, near_ref, next_ref, *refs = refs
        xl_ref, xr_ref = refs[0], refs[beside - 1]
        w1_ref, cols1_ref, even1_ref, odd1_ref, rows1_ref, *sends, e_ref, a_ref, c_ref, x_ref, ghost_ref = refs[beside:]
    high, width = rows_ref.shape[2:]
    groups = cols_ref.shape[1] // 6
    size = width // high
    rows = groups * size
    step = 0.5 * TIME_STEP if second else TIME_STEP
    coef = 0.5 * step
    _, _, first, last = whereabouts(rows)
    even = at_even_block()
    loop = unrolled if second else in_loop

    def gather(f, carry):
        for k in range(2):
            at = slice(k * groups, (k + 1) * groups)
            e_ref[f, k, 0:groups] = jnp.where(even, odd_ref[f, at], even_ref[f, at])
            e_ref[f, 3 + k, groups : 2 * groups] = jnp.where(even, even_ref[f, at], odd_ref[f, at])
        for k in range(3):
            e_ref[f, 2 + k, 0:groups] = cols_ref[f, k * groups : (k + 1) * groups]
            e_ref[f, k, groups : 2 * groups] = cols_ref[f, (3 + k) * groups : (4 + k) * groups]
        return carry

    lax.fori_loop(0, FIELDS, gather, 0)
    shear_copy.wait()
    sheared_rows(first, shear_smem, near_ref, next_ref, ghost_ref)
    cells = [[e_ref[f, k] for f in range(FIELDS)] for k in range(5)]
    sides = [three_states(cells[k : k + 3]) for k in range(3)]
    one = face(sides[0][0], sides[1][1], 1)
    two = face(sides[1][0], sides[2][1], 1)
    low_end = lax.broadcasted_iota(jnp.int32, one[0].shape, 0) < groups
    for f in range(FIELDS):
        a_ref[f, 0] = coef * (two[f] - one[f])
        a_ref[f, 1] = coef * jnp.where(low_end, -two[f], one[f])

    if second:

        def scatter(f, carry):
            for g in range(groups):
                c_ref[f, g] = jnp.zeros((2 * PAD, width), jnp.float32)
                c_ref[f, g, 0:1] = a_ref[f, 0, g : g + 1]
                c_ref[f, g, 1:2] = a_ref[f, 1, g : g + 1]
                c_ref[f, g, 2 * PAD - 2 : 2 * PAD - 1] = a_ref[f, 1, groups + g : groups + g + 1]
                c_ref[f, g, 2 * PAD - 1 : 2 * PAD] = a_ref[f, 0, groups + g : groups + g + 1]
            return carry

        lax.fori_loop(0, FIELDS, scatter, 0)

    def place(f, carry):
        x_ref[0, f, 0:2] = jnp.where(first, ghost_ref[f], xl_ref[f])
        x_ref[1, f, 3:5] = jnp.where(last, ghost_ref[f], xr_ref[f])
        x_ref[0, f, 2:5] = rows_ref[f, 0:3]
        x_ref[1, f, 0:3] = rows_ref[f, 3:6]
        return carry

    lax.fori_loop(0, FIELDS, place, 0)

    def radial(n, carry):
        if second:
            end, at = n // 2, pl.ds(n % 2 * (high // 2), high // 2)
        else:
            end, at = lax.div(n, 2), pl.ds(pl.multiple_of(lax.rem(n, 2) * (high // 2), 8), high // 2)
        cells = [[x_ref[end, f, k, at] for f in range(FIELDS)] for k in range(5)]
        sides = [three_states(cells[k : k + 3]) for k in range(3)]
        one = face(sides[0][0], sides[1][1], 0)
        two = face(sides[1][0], sides[2][1], 0)
        for f in range(FIELDS):
            x_ref[end, f, 0, at] = coef * (two[f] - one[f])
            x_ref[end, f, 1, at] = coef * jnp.where(end == 0, -two[f], one[f])
        return carry

    loop(4, radial)
    batch = FIELDS // 4

    if not second:
        lane = lanes_of((width, width))

        def correct(n, carry):
            for k in range(2 * batch):
                f = 2 * n * batch + k
                strip = [x_ref[0, f, 0], x_ref[0, f, 1], jnp.zeros((width - 4 * high, width), jnp.float32)]
                strip = jnp.concatenate(strip + [x_ref[1, f, 1], x_ref[1, f, 0]], axis=0).T
                at = slice(PAD, PAD + width)
                w1_ref[f, 0, at] = vt_ref[f, 0, at] - jnp.where(lane < width // 2, strip, 0.0)
                w1_ref[f, groups - 1, at] = vt_ref[f, groups - 1, at] - jnp.where(lane < width // 2, 0.0, strip)
            return carry

        lax.fori_loop(0, FIELDS // (2 * batch), correct, 0)

        def correct_rows(f, carry):
            for g in range(groups):
                places = [(0, 0, g), (1, 1, g), (width - 2, 1, groups + g), (width - 1, 0, groups + g)]
                for to, kind, at in places:
                    to = slice(PAD + to, PAD + to + 1)
                    w1_ref[f, g, to] = w1_ref[f, g, to] - a_ref[f, kind, at : at + 1]
            return carry

        lax.fori_loop(0, FIELDS, correct_rows, 0)
        block = width // 2

        def primitives(n, carry):
            g, at = lax.div(n, 2), pl.ds(pl.multiple_of(PAD + block * lax.rem(n, 2), 8), block)
            prim = to_primitive([w1_ref[f, g, at] for f in range(FIELDS)])
            for f in range(FIELDS):
                w1_ref[f, g, at] = prim[f]
            return carry

        lax.fori_loop(0, 2 * groups, primitives, 0)

        def turn_rows(n, carry):
            for k in range(batch):
                f = n * batch + k
                at = slice(PAD, PAD + width)
                strip = jnp.where(lane < width // 2, w1_ref[f, 0, at], w1_ref[f, groups - 1, at]).T
                rows1_ref[f, 0:3] = strip[0 : 3 * high].reshape(3, high, width)
                rows1_ref[f, 3:6] = strip[width - 3 * high : width].reshape(3, high, width)
            return carry

        lax.fori_loop(0, FIELDS // batch, turn_rows, 0)
        send_columns(groups, w1_ref, cols1_ref, even1_ref, odd1_ref)
        send_rows(rows, rows1_ref, *sends)
        return

    batch = FIELDS // 2
    copies = []
    for g in [*range(1, groups - 1), 0, groups - 1]:
        at = pl.ds(g * size, size)
        for half in range(2):
            for f in range(half * batch, (half + 1) * batch):
                head = dy_ref[f, g, PAD : 2 * PAD] + c_ref[f, g, 0:PAD]
                tail = dy_ref[f, g, width : PAD + width] + c_ref[f, g, PAD : 2 * PAD]
                strip = jnp.concatenate([head, dy_ref[f, g, 2 * PAD : width], tail], axis=0)
                strip = strip.T.reshape(size, high, width)
                value = [v_ref[f, g * size + i] - strip[i] for i in range(size)]
                if g == 0:
                    value[0], value[1] = value[0] - x_ref[0, f, 0], value[1] - x_ref[0, f, 1]
                if g == groups - 1:
                    value[-1], value[-2] = value[-1] - x_ref[1, f, 0], value[-2] - x_ref[1, f, 1]
                for i in range(size):
                    out_ref[f, g * size + i] = value[i]
            part = pl.ds(half * batch, batch)
            copy = pltpu.make_async_copy(out_ref.at[part, at], out_hbm.at[part, at], sems.at[len(copies)])
            copy.start()
            copies.append(copy)
    for copy in copies:
        copy.wait()


def gather_kernel(even_ref, odd_ref, *refs):
    *slabs, ends_ref, slabs_ref = refs

    def body(f, carry):
        ends_ref[0, f], ends_ref[1, f] = even_ref[f], odd_ref[f]
        for k, ref in enumerate(slabs):
            slabs_ref[k, f] = ref[f]
        return carry

    lax.fori_loop(0, FIELDS, body, 0)


def call(kernel, name, arrays, shapes, scratch=(), in_hbm=False, out_hbm=False, aliases=None, shear=()):
    vmem = pl.BlockSpec(memory_space=pltpu.VMEM)
    hbm = pl.BlockSpec(memory_space=pltpu.HBM)
    if in_hbm:
        arrays = [pltpu.with_memory_space_constraint(x, pltpu.HBM) for x in arrays]
    return pl.pallas_call(
        kernel,
        name=name,
        out_shape=[jax.ShapeDtypeStruct(s, jnp.float32) for s in shapes],
        in_specs=[pl.BlockSpec(memory_space=pl.ANY)] * len(shear) + [hbm if in_hbm else vmem] * len(arrays),
        out_specs=[hbm if out_hbm else vmem] * len(shapes),
        scratch_shapes=[pltpu.VMEM(s, jnp.float32) if isinstance(s, tuple) else s for s in scratch],
        input_output_aliases=aliases or {},
        compiler_params=pltpu.CompilerParams(vmem_limit_bytes=20 * 1024 * 1024),
    )(*shear, *arrays)


def exchange(even, odd, swap):
    count_x, count_y = lax.axis_size("gx"), lax.axis_size("gy")

    def pairs(start):
        ends = [(i, (i + 1) % count_y) for i in range(start, count_y, 2)]
        return ends + [(j, i) for i, j in ends]

    even, odd = lax.ppermute(even, "gy", pairs(0)), lax.ppermute(odd, "gy", pairs(1))
    if len(swap) == 1:
        return even, odd, lax.ppermute(swap[0], "gx", [(0, 1), (1, 0)])
    x_low = lax.ppermute(swap[1], "gx", [(i, i + 1) for i in range(count_x - 1)])
    x_high = lax.ppermute(swap[0], "gx", [(i + 1, i) for i in range(count_x - 1)])
    return even, odd, x_low, x_high


def crossing(by, shear):
    count_x, count_y = lax.axis_size("gx"), lax.axis_size("gy")
    last = (count_x - 1) * count_y
    pairs = []
    for gy in range(count_y):
        pairs.append((last + gy, (gy + by) % count_y))
        pairs.append((gy, last + (gy - by) % count_y))
    return lax.ppermute(shear, ("gx", "gy"), pairs)


def inner_scratch(full):
    high, width = full[2:]
    tile = (FIELDS, high, width)
    padded = (FIELDS, high + 2 * PAD, width)
    column = (FIELDS, PAD + width, width)
    return [padded] * 3 + [tile] * 4 + [column] * 3 + [(FIELDS, 2 * high, width)]


def edge_scratch(full, groups):
    high, width = full[2:]
    return [
        (FIELDS, 5, 2 * groups, width),
        (FIELDS, 2, 2 * groups, width),
        (FIELDS, groups, 2 * PAD, width),
        (2, FIELDS, 5, high, width),
        (FIELDS, 2, high, width),
        pltpu.SMEM((2,), jnp.int32),
        pltpu.SemaphoreType.DMA,
    ]


def sections(block, drift, w0, wt0, cols, even, odd, rows, shear, *swap):
    full, turned = w0.shape, wt0.shape
    groups = cols.shape[1] // 6
    sends = [x.shape for x in (cols, even, odd, rows, shear, *swap)]
    scratch = edge_scratch(full, groups)
    received = [(2,) + even.shape, (2 + (1 if len(swap) == 1 else 2),) + shear.shape]

    def branch(by):
        def run(drift, w0, wt0, cols, even, odd, rows, shear, *swap):
            even, odd, *beside = exchange(even, odd, swap)
            sheared = crossing(by, shear), crossing(by + 1, shear)
            kernel = functools.partial(interior_kernel, False)
            (vt,) = call(kernel, "inner_1", [w0, wt0], [turned], [full] + inner_scratch(full))
            wt1, cols, even, odd, rows, shear, *swap = call(
                functools.partial(edge_kernel, False, len(beside)),
                "edge_1",
                [vt, rows, cols, even, odd, *sheared, *beside],
                [turned] + sends,
                scratch,
                aliases={1: 0},
                shear=[drift],
            )
            even, odd, *beside = exchange(even, odd, swap)
            sheared = crossing(by, shear), crossing(by + 1, shear)
            kernel = functools.partial(interior_kernel, True)
            v, dy = call(kernel, "inner_2", [wt1, w0], [full, turned], [full] + inner_scratch(full))
            ends, slabs = call(gather_kernel, "gather", [even, odd, *sheared, *beside], received)
            return v, dy, rows, cols, ends, slabs

        return run

    branches = [branch(by) for by in range(lax.axis_size("gy"))]
    arrays = lax.switch(block, branches, drift, w0, wt0, cols, even, odd, rows, shear, *swap)
    (out,) = call(
        functools.partial(edge_kernel, True, received[1][0] - 2),
        "edge_2",
        arrays,
        [full],
        scratch[:-2] + [full, pltpu.SemaphoreType.DMA((2 * groups,))] + scratch[-2:],
        out_hbm=True,
        shear=[drift],
    )
    return out


def on_device(density, velocity, bfield, pressure, shear_shift, remap_weight):
    rows, high, width = density.shape
    count_x = lax.axis_size("gx")
    drift = jnp.stack([shear_shift, remap_weight])
    full = (FIELDS, rows, high, width)
    slab = (FIELDS, 2, high, width)
    groups = rows * high // width
    turned = (FIELDS, groups + 1, width + 2 * PAD, width)
    ends = (FIELDS, 2 * groups, width)
    sends = [(FIELDS, 6 * groups, width), ends, ends, (FIELDS, 6, high, width)]
    sends += [slab] * (2 if count_x == 2 else 3)
    start_state = call(
        prepare_kernel,
        "prepare",
        [density, velocity, bfield, pressure],
        [full, turned] + sends,
        [pltpu.SemaphoreType.DMA((4, groups))],
        in_hbm=True,
    )
    return sections(shear_shift // width, drift, *start_state)


def solution(mesh):
    placed = (
        P("gx", None, "gy"),
        P(None, "gx", None, "gy"),
        P(None, "gx", None, "gy"),
        P("gx", None, "gy"),
        P(),
        P(),
    )
    return jax.shard_map(
        on_device, mesh=mesh, in_specs=placed, out_specs=P(None, "gx", None, "gy"), check_vma=False
    )
```
